32 devices in a mesh: groups: 2 (over y), gz: 8 (over z, x), tile: 2 (over core).
Axes of the slice: x: 2, y: 2, z: 4, core: 2. Of those that a mesh axis runs over, the one named last changes fastest.
Arguments:
- volume: bfloat16 [16, 32, 12288], P(('groups', 'gz'), 'tile'), parts along dimension 0, may hold values from -6 to 6
- norm_gains: float32 [4, 96], replicated, may hold values from 0.1 to 1.9
- qkv_weight: bfloat16 [2, 96, 288], replicated, may hold values from -0.625 to 0.625
- out_weight: bfloat16 [2, 96, 96], replicated, may hold values from -0.625 to 0.625
- up_weight: bfloat16 [2, 96, 384], replicated, may hold values from -0.625 to 0.625
- down_weight: bfloat16 [2, 384, 96], replicated, may hold values from -0.3125 to 0.3125
- window_bias: float32 [3, 64, 64], replicated, may hold values from -4 to 4
Outputs:
- result: bfloat16 [16, 32, 12288], P(('groups', 'gz'), 'tile'), parts along dimension 0
The draws below stay inside these ranges and needn't reach their ends.
There are 2 independent parts, one for each index of `groups`. The reference program is written for one: setup_inputs(seed, part) draws one part's arguments, and reference() takes and returns one part's arrays. A program takes and returns all parts, laid end to end along the dimension named above; an argument that names none is the same for every part. Nothing has to cross between parts.
All inputs are finite; a program needn't handle non-finite values.
Results may differ from the reference program's by a relative error of at most 0.02.
Values may be sent and summed in bfloat16 or wider, within the bound.
No kernel may reach another device: no remote copies, remote signals or barrier semaphores. Data moves between devices by JAX's collectives and lax.ppermute only.
A program may use at most 64 MiB of HBM per device.

```python
import jax
import jax.numpy as jnp
from jax import lax

C = 96
HEADS = 3
FF = 384
W = 128
H = 32
NZ = 8


def levels(key, shape, split, smallest, top_value):
    level, own = 1.0, jax.random.fold_in(key, 6)
    for axis_at, shards_of in split:
        steps = jnp.exp(jax.random.uniform(jax.random.fold_in(own, axis_at), (shards_of,), jnp.float32, smallest / len(split), top_value / len(split)))
        level = level * jnp.repeat(steps, shape[axis_at] // shards_of).reshape([-1 if axis == axis_at else 1 for axis in range(len(shape))])
    return level


def normal_values(own_key, shape, width, reach, split=(), kind=jnp.bfloat16):
    values = jax.random.normal(own_key, shape, jnp.float32) * width
    if len(split) > 0:
        values = levels(own_key, shape, split, -0.22, 0.18) * values
    return jnp.clip(values, min=-reach, max=reach).astype(kind)


def setup_inputs(seed: int = 0, part: int = 0) -> dict:
    arg_keys = jax.random.split(jax.random.key(seed), 8)
    part_keys = jax.random.split(jax.random.fold_in(arg_keys[7], part), 8)
    return {
        "volume": normal_values(part_keys[0], (NZ, H, W * C), 1.0, 6.0, ((0, 8), (1, 2))),
        "norm_gains": jnp.clip(1.0 + 0.18 * jax.random.normal(arg_keys[1], (4, C), jnp.float32), 0.1, 1.9),
        "qkv_weight": normal_values(arg_keys[2], (2, C, 3 * C), C ** -0.5, 0.625),
        "out_weight": normal_values(arg_keys[3], (2, C, C), C ** -0.5, 0.625),
        "up_weight": normal_values(arg_keys[4], (2, C, FF), C ** -0.5, 0.625),
        "down_weight": normal_values(arg_keys[5], (2, FF, C), FF ** -0.5, 0.3125),
        "window_bias": normal_values(arg_keys[6], (HEADS, 64, 64), 1.0, 4.0, (), jnp.float32),
    }


epsilon = 1e-05

def layer_norm(tokens, gain):
    values = tokens.astype(jnp.float32)
    average = lax.optimization_barrier(jnp.mean(values, -1, keepdims=True))
    centered = values - average
    variance = lax.optimization_barrier(jnp.mean(centered * centered, -1, keepdims=True))
    return (centered * lax.rsqrt(variance + epsilon) * gain).astype(jnp.bfloat16)

def feed_forward(tokens, gain, up_matrix, down_matrix):
    normed = layer_norm(tokens, gain)
    hidden = jax.nn.gelu(jnp.dot(normed, up_matrix, preferred_element_type=jnp.float32)).astype(jnp.bfloat16)
    total = tokens.astype(jnp.float32) + jnp.dot(hidden, down_matrix, preferred_element_type=jnp.float32)
    return total.astype(jnp.bfloat16)

def edge_label(index, extent):
    return jnp.where(index < 4, 2, jnp.where(index >= extent - 4, 1, 0)).astype(jnp.int32)

def lateral_block(plane, labels, norm_gains, qkv_weight, out_weight, up_weight, down_weight, window_bias):
    head_size = C // HEADS
    rolled = jnp.roll(plane, (-4, -4), (0, 1))
    rolled_labels = jnp.roll(labels, (-4, -4), (0, 1))
    normed = layer_norm(rolled.reshape(-1, C), norm_gains[0])
    packed = jnp.dot(normed, qkv_weight[0], preferred_element_type=jnp.float32).astype(jnp.bfloat16)
    packed = packed.reshape(H // 8, 8, W // 8, 8, 3, HEADS, head_size)
    packed = packed.transpose(0, 2, 1, 3, 4, 5, 6).reshape(-1, 64, 3, HEADS, head_size)
    window_labels = rolled_labels.reshape(H // 8, 8, W // 8, 8).transpose(0, 2, 1, 3).reshape(-1, 64)
    allowed = window_labels[:, :, None] == window_labels[:, None, :]
    queries = packed[:, :, 0].astype(jnp.float32)
    keys = packed[:, :, 1].astype(jnp.float32)
    values = packed[:, :, 2].astype(jnp.float32)
    scores = jnp.einsum('nqhd,nkhd->nhqk', queries, keys) * head_size ** (-0.5) + window_bias[None]
    scores = jnp.where(allowed[:, None], scores, -jnp.inf)
    weights = jax.nn.softmax(scores, axis=-1).astype(jnp.bfloat16)
    attended = jnp.einsum('nhqk,nkhd->nqhd', weights.astype(jnp.float32), values).astype(jnp.bfloat16)
    attended = attended.reshape(H // 8, W // 8, 8, 8, C).transpose(0, 2, 1, 3, 4).reshape(H, W, C)
    attended = jnp.roll(attended, (4, 4), (0, 1))
    lateral = jnp.dot(attended.reshape(-1, C), out_weight[0], preferred_element_type=jnp.float32).astype(jnp.bfloat16)
    middle = (plane.reshape(-1, C).astype(jnp.float32) + lateral.astype(jnp.float32)).astype(jnp.bfloat16)
    return feed_forward(middle, norm_gains[1], up_weight[0], down_weight[0]).reshape(H, W, C)

def axial_block(pencils, norm_gains, qkv_weight, out_weight, up_weight, down_weight):
    head_size = C // HEADS
    count = pencils.shape[0]
    flat = pencils.reshape(-1, C)
    normed = layer_norm(flat, norm_gains[2])
    packed = jnp.dot(normed, qkv_weight[1], preferred_element_type=jnp.float32).astype(jnp.bfloat16)
    packed = packed.reshape(count, NZ, 3, HEADS, head_size)
    queries = packed[:, :, 0].astype(jnp.float32)
    keys = packed[:, :, 1].astype(jnp.float32)
    values = packed[:, :, 2].astype(jnp.float32)
    scores = jnp.einsum('pzhd,pyhd->phzy', queries, keys) * head_size ** (-0.5)
    weights = jax.nn.softmax(scores, axis=-1).astype(jnp.bfloat16)
    attended = jnp.einsum('phzy,pyhd->pzhd', weights.astype(jnp.float32), values).astype(jnp.bfloat16)
    projected = jnp.dot(attended.reshape(-1, C), out_weight[1], preferred_element_type=jnp.float32).astype(jnp.bfloat16)
    after = (flat.astype(jnp.float32) + projected.astype(jnp.float32)).astype(jnp.bfloat16)
    return feed_forward(after, norm_gains[3], up_weight[1], down_weight[1]).reshape(count, NZ, C)

def reference(volume, norm_gains, qkv_weight, out_weight, up_weight, down_weight, window_bias):
    planes = volume.reshape(NZ, H, W, C)
    row_labels = edge_label(jnp.arange(H, dtype=jnp.int32), H)
    column_labels = edge_label(jnp.arange(W, dtype=jnp.int32), W)
    labels = row_labels[:, None] * 3 + column_labels[None, :]

    def one_plane(plane):
        return lateral_block(plane, labels, norm_gains, qkv_weight, out_weight, up_weight, down_weight, window_bias)
    planar = lax.map(one_plane, planes)
    pencils = jnp.transpose(planar.reshape(NZ, H * W, C), (1, 0, 2)).reshape(H * W // 128, 128, NZ, C)

    def one_block(block):
        return axial_block(block, norm_gains, qkv_weight, out_weight, up_weight, down_weight)
    mixed = lax.map(one_block, pencils).reshape(H * W, NZ, C)
    return jnp.transpose(mixed, (1, 0, 2)).reshape(NZ, H, W * C)
```

```python
import jax
import jax.numpy as jnp
from jax import lax
from jax.experimental import pallas as pl
from jax.experimental.pallas import tpu as pltpu
from jax.sharding import PartitionSpec as P

epsilon = 1e-05


def shifted(array, axis, by):
    peers = lax.axis_size(axis)
    return lax.ppermute(array, axis, [(i, (i + by) % peers) for i in range(peers)])


def layer_norm(tokens, gain):
    values = tokens.astype(jnp.float32)
    average = jnp.mean(values, -1, keepdims=True)
    centered = values - average
    variance = jnp.mean(centered * centered, -1, keepdims=True)
    return (centered * lax.rsqrt(variance + epsilon) * gain).astype(jnp.bfloat16)


def feed_forward(tokens, gain, up_matrix, down_matrix):
    normed = layer_norm(tokens, gain)
    hidden = jax.nn.gelu(jnp.dot(normed, up_matrix, preferred_element_type=jnp.float32)).astype(
        jnp.bfloat16
    )
    total = tokens.astype(jnp.float32) + jnp.dot(
        hidden, down_matrix, preferred_element_type=jnp.float32
    )
    return total.astype(jnp.bfloat16)


def edge_label(index, extent):
    return jnp.where(index < 4, 2, jnp.where(index >= extent - 4, 1, 0)).astype(jnp.int32)


def head_masks(heads, channels):
    owner = jnp.arange(channels, dtype=jnp.int32) // (channels // heads)
    return (owner[None, :] == jnp.arange(heads, dtype=jnp.int32)[:, None]).astype(jnp.bfloat16)


def window_attention(
    row_block, first_row, height, channels, norm_gains, qkv_weight, out_weight, window_bias
):
    count = row_block.shape[0]
    columns = row_block.shape[1] // channels
    heads = window_bias.shape[0]
    head_size = channels // heads
    masks = head_masks(heads, channels)
    rolled = jnp.roll(row_block, -4 * channels, axis=1)
    windowed = rolled.reshape(count // 8, 8, columns // 8, 8 * channels).transpose(0, 2, 1, 3)
    normed = layer_norm(windowed.reshape(-1, channels), norm_gains[0])
    packed = jnp.dot(normed, qkv_weight[0], preferred_element_type=jnp.float32).astype(jnp.bfloat16)
    packed = packed.reshape(-1, 64, 3 * channels)
    queries = packed[:, :, :channels]
    keys = packed[:, :, channels : 2 * channels]
    values = packed[:, :, 2 * channels :]
    initial_rows = jnp.mod(first_row + jnp.arange(count, dtype=jnp.int32), height)
    initial_columns = jnp.mod(jnp.arange(columns, dtype=jnp.int32) + 4, columns)
    labels = (
        edge_label(initial_rows, height)[:, None] * 3
        + edge_label(initial_columns, columns)[None, :]
    )
    window_labels = (
        labels.reshape(count // 8, 8, columns // 8, 8).transpose(0, 2, 1, 3).reshape(-1, 64)
    )
    allowed = window_labels[:, :, None] == window_labels[:, None, :]
    head_queries = queries[:, None] * masks[None, :, None, :]
    scores = jnp.einsum("nhqc,nkc->nhqk", head_queries, keys, preferred_element_type=jnp.float32)
    scores = scores * head_size ** (-0.5) + window_bias[None]
    scores = jnp.where(allowed[:, None], scores, -jnp.inf)
    weights = jax.nn.softmax(scores, axis=-1).astype(jnp.bfloat16)
    head_values = values[:, None] * masks[None, :, None, :]
    attended = jnp.einsum(
        "nhqk,nhkc->nqc", weights, head_values, preferred_element_type=jnp.float32
    ).astype(jnp.bfloat16)
    lateral = jnp.dot(
        attended.reshape(-1, channels), out_weight[0], preferred_element_type=jnp.float32
    ).astype(jnp.bfloat16)
    lateral = lateral.reshape(count // 8, columns // 8, 8, 8 * channels).transpose(0, 2, 1, 3)
    return jnp.roll(lateral.reshape(count, columns * channels), 4 * channels, axis=1)


def axial_block(pencils, norm_gains, qkv_weight, out_weight, up_weight, down_weight, heads):
    planes, count, channels = pencils.shape
    head_size = channels // heads
    masks = head_masks(heads, channels)
    flat = jnp.transpose(pencils, (1, 0, 2)).reshape(-1, channels)
    normed = layer_norm(flat, norm_gains[2])
    packed = jnp.dot(normed, qkv_weight[1], preferred_element_type=jnp.float32).astype(jnp.bfloat16)
    packed = packed.reshape(count, planes, 3 * channels)
    queries = packed[:, :, :channels]
    keys = packed[:, :, channels : 2 * channels]
    values = packed[:, :, 2 * channels :]
    head_queries = queries[:, None] * masks[None, :, None, :]
    scores = jnp.einsum("phzc,pyc->phzy", head_queries, keys, preferred_element_type=jnp.float32)
    weights = jax.nn.softmax(scores * head_size ** (-0.5), axis=-1).astype(jnp.bfloat16)
    head_values = values[:, None] * masks[None, :, None, :]
    attended = jnp.einsum(
        "phzy,phyc->pzc", weights, head_values, preferred_element_type=jnp.float32
    ).astype(jnp.bfloat16)
    projected = jnp.dot(
        attended.reshape(-1, channels), out_weight[1], preferred_element_type=jnp.float32
    ).astype(jnp.bfloat16)
    after = (flat.astype(jnp.float32) + projected.astype(jnp.float32)).astype(jnp.bfloat16)
    mixed = feed_forward(after, norm_gains[3], up_weight[1], down_weight[1]).reshape(
        count, planes, channels
    )
    return jnp.transpose(mixed, (1, 0, 2))


def general_body(volume, norm_gains, qkv_weight, out_weight, up_weight, down_weight, window_bias):
    rows_here = volume.shape[1]
    row_width = volume.shape[2]
    channels = norm_gains.shape[1]
    heads = window_bias.shape[0]
    height = rows_here * lax.axis_size("tile")
    tile_start = lax.axis_index("tile") * rows_here
    plane = volume.reshape(rows_here, row_width)
    next_rows = shifted(plane[:4], "tile", -1)
    extended = jnp.concatenate([plane[4:], next_rows], 0)
    attended = window_attention(
        extended, tile_start + 4, height, channels, norm_gains, qkv_weight, out_weight, window_bias
    )
    tail_rows = shifted(attended[-4:], "tile", 1)
    lateral = jnp.concatenate([tail_rows, attended[:-4]], 0)
    middle = (
        (plane.astype(jnp.float32) + lateral.astype(jnp.float32))
        .astype(jnp.bfloat16)
        .reshape(-1, channels)
    )
    planes = lax.axis_size("gz")
    middle = feed_forward(middle, norm_gains[1], up_weight[0], down_weight[0])
    grouped = middle.reshape(planes, -1, channels)
    pencils = lax.all_to_all(grouped, "gz", split_axis=0, concat_axis=0, tiled=True)
    returned = lax.all_to_all(
        axial_block(pencils, norm_gains, qkv_weight, out_weight, up_weight, down_weight, heads),
        "gz",
        split_axis=0,
        concat_axis=0,
        tiled=True,
    )
    return returned.reshape(1, rows_here, row_width)


LOG2E = 1.4426950408889634


def normalised(tokens):
    average = jnp.mean(tokens, 0, keepdims=True)
    centered = tokens - average
    variance = jnp.mean(centered * centered, 0, keepdims=True)
    return (centered * lax.rsqrt(variance + epsilon)).astype(jnp.bfloat16)


def product(left, right):
    return jnp.dot(left, right, preferred_element_type=jnp.float32)


def gated(hidden):
    inner = hidden * (0.7978845608028654 + 0.035677408136300125 * (hidden * hidden))
    half = 0.5 * hidden
    return (half + half * jnp.tanh(inner)).astype(jnp.bfloat16)


def column_feed_forward(tokens, up, down):
    return tokens + product(down, gated(product(up, normalised(tokens))))


def pack_kernel(volume_ref, packed_ref):
    windows, channels, _ = packed_ref.shape
    width = 8 * channels
    half = width // 2
    for window in range(windows):
        start = window * width + half
        if window < windows - 1:
            chunk = volume_ref[:, start : start + width]
        else:
            chunk = jnp.concatenate([volume_ref[:, start:], volume_ref[:, :half]], axis=1)
        chunk = chunk.astype(jnp.float32)
        rolled = jnp.concatenate([chunk[4:], chunk[:4]], axis=0)
        pieces = [
            rolled[8 * part : 8 * part + 8, channels * column : channels * (column + 1)]
            for part in range(2)
            for column in range(8)
        ]
        tokens = jnp.concatenate(pieces, axis=0)
        packed_ref[window] = tokens.T.astype(jnp.bfloat16)


def unpack_kernel(packed_ref, volume_ref):
    windows, channels, _ = packed_ref.shape
    width = 8 * channels
    half = width // 2
    for window in range(windows):
        tokens = packed_ref[window].astype(jnp.float32).T
        parts = [
            jnp.concatenate(
                [tokens[64 * part + 8 * column : 64 * part + 8 * column + 8] for column in range(8)], axis=1
            )
            for part in range(2)
        ]
        rows = jnp.concatenate([parts[1][4:], parts[0], parts[1][:4]], axis=0).astype(jnp.bfloat16)
        start = window * width + half
        if window < windows - 1:
            volume_ref[:, start : start + width] = rows
        else:
            volume_ref[:, start:] = rows[:, :half]
            volume_ref[:, :half] = rows[:, half:]


def blocks_kernel(
    tokens_ref,
    bias_ref,
    qkv_ref,
    out_ref,
    up_ref,
    down_ref,
    gather_ref,
    result_ref,
    planar_ref,
    query_ref,
    key_ref,
    value_ref,
):
    planes, channels, _ = planar_ref.shape
    heads = bias_ref.shape[1] // 64
    head_size = channels // heads
    scale = LOG2E * head_size ** (-0.5)
    lane = lax.broadcasted_iota(jnp.int32, (1, 128), 1)
    own = (lane < 64) | (lane % 8 < 4)
    first = lane < 64

    def lateral(plane, carry):
        one = tokens_ref[2 * plane].astype(jnp.float32)
        two = tokens_ref[2 * plane + 1].astype(jnp.float32)
        tokens = jnp.concatenate([jnp.where(own, one, two), jnp.where(own, two, one)], axis=1)
        packed = product(qkv_ref[0], normalised(tokens))
        queries = packed[:channels] * scale
        keys = packed[channels : 2 * channels]
        values = packed[2 * channels :].astype(jnp.bfloat16)
        blank = jnp.zeros((128 - channels, 128), jnp.bfloat16)
        attended = []
        for pair in range(2):
            lanes = slice(128 * pair, 128 * pair + 128)
            query = queries[:, lanes]
            right = jnp.concatenate(
                [
                    jnp.where(first, query, 0.0).astype(jnp.bfloat16),
                    blank,
                    jnp.where(first, 0.0, query).astype(jnp.bfloat16),
                    blank,
                ],
                axis=0,
            )
            key = jnp.concatenate([keys[:, lanes], jnp.zeros((128 - channels, 128), jnp.float32)], axis=0).T
            left = []
            for head in range(heads):
                mine = lane // head_size == head
                masked = jnp.where(mine, key, 0.0).astype(jnp.bfloat16)
                left.append(jnp.concatenate([masked[:64], masked[64:]], axis=1))
            scores = product(jnp.concatenate(left, axis=0), right) + bias_ref[pair]
            for head in range(heads):
                own_scores = scores[64 * head : 64 * head + 64]
                weights = jnp.exp2(own_scores - jnp.max(own_scores, axis=0, keepdims=True))
                total = jnp.sum(weights, axis=0, keepdims=True)
                spread = jnp.concatenate(
                    [
                        jnp.where(first, weights, 0.0).astype(jnp.bfloat16),
                        jnp.where(first, 0.0, weights).astype(jnp.bfloat16),
                    ],
                    axis=0,
                )
                mixed = product(values[head_size * head : head_size * (head + 1), lanes], spread)
                attended.append((mixed * (1.0 / total)).astype(jnp.bfloat16))
        attended = jnp.concatenate(
            [jnp.concatenate(attended[:heads], axis=0), jnp.concatenate(attended[heads:], axis=0)], axis=1
        )
        middle = tokens + product(out_ref[0], attended)
        planar = column_feed_forward(middle, up_ref[0], down_ref[0])
        planar_ref[plane] = planar
        packed = product(qkv_ref[1], normalised(planar))
        query_ref[plane] = (packed[:channels] * scale).astype(jnp.bfloat16)
        key_ref[plane] = packed[channels : 2 * channels].astype(jnp.bfloat16)
        value_ref[plane] = packed[2 * channels :]
        return carry

    def axial(plane, carry):
        query = query_ref[plane]
        pairs = jnp.concatenate([query * key_ref[other] for other in range(planes)], axis=0)
        scores = product(gather_ref[...], pairs)
        attended = []
        for head in range(heads):
            own_scores = scores[planes * head : planes * (head + 1)]
            weights = jnp.exp2(own_scores - jnp.max(own_scores, axis=0, keepdims=True))
            weights = weights / jnp.sum(weights, axis=0, keepdims=True)
            mixed = jnp.zeros((head_size, 256), jnp.float32)
            for other in range(planes):
                value = value_ref[other, head_size * head : head_size * (head + 1), :]
                mixed += weights[other : other + 1] * value
            attended.append(mixed.astype(jnp.bfloat16))
        after = planar_ref[plane] + product(out_ref[1], jnp.concatenate(attended, axis=0))
        mixed = column_feed_forward(after, up_ref[1], down_ref[1])
        one, two = mixed[:, :128], mixed[:, 128:]
        result_ref[2 * plane] = jnp.where(own, one, two).astype(jnp.bfloat16)
        result_ref[2 * plane + 1] = jnp.where(own, two, one).astype(jnp.bfloat16)
        return carry

    lax.fori_loop(0, planes, lateral, 0)
    lax.fori_loop(0, planes, axial, 0)


def pack(rows, windows, channels):
    return pl.pallas_call(
        pack_kernel,
        out_shape=jax.ShapeDtypeStruct((windows, channels, 128), jnp.bfloat16),
        name="pack_windows",
    )(rows)


def unpack(packed, rows, width):
    return pl.pallas_call(
        unpack_kernel,
        out_shape=jax.ShapeDtypeStruct((rows, width), jnp.bfloat16),
        name="unpack_windows",
    )(packed)


def blocks(tokens, bias, qkv, out, up, down, gather):
    sources, channels, _ = tokens.shape
    planes = sources // 2
    return pl.pallas_call(
        blocks_kernel,
        out_shape=jax.ShapeDtypeStruct(tokens.shape, jnp.bfloat16),
        scratch_shapes=[
            pltpu.VMEM((planes, channels, 256), jnp.float32),
            pltpu.VMEM((planes, channels, 256), jnp.bfloat16),
            pltpu.VMEM((planes, channels, 256), jnp.bfloat16),
            pltpu.VMEM((planes, channels, 256), jnp.float32),
        ],
        compiler_params=pltpu.CompilerParams(vmem_limit_bytes=40 * 1024 * 1024),
        name="both_blocks",
    )(tokens, bias, qkv, out, up, down, gather)


def pair_bias(window_bias, last):
    heads = window_bias.shape[0]
    split = window_bias.reshape(heads, 8, 8, 8, 8).transpose(0, 4, 3, 2, 1).reshape(heads, 64, 64) * LOG2E
    index = jnp.arange(64, dtype=jnp.int32)
    column_side = (index // 8 < 4).astype(jnp.int32)
    row_side = (index % 8 < 4).astype(jnp.int32)
    column_cut = (column_side[:, None] != column_side[None, :]) & last
    row_cut = row_side[:, None] != row_side[None, :]
    plain = jnp.where(column_cut[None], -jnp.inf, split)
    cut = jnp.where(row_cut[None], -jnp.inf, plain)
    one = jnp.concatenate([plain, plain], axis=2).reshape(heads * 64, 128)
    two = jnp.concatenate([plain, cut], axis=2).reshape(heads * 64, 128)
    return jnp.stack([one, two])


def folded(gain, matrix):
    return (gain[:, None] * matrix.astype(jnp.float32)).T.astype(jnp.bfloat16)


def window_body(volume, norm_gains, qkv_weight, out_weight, up_weight, down_weight, window_bias):
    rows = volume.shape[1]
    width = volume.shape[2]
    channels = norm_gains.shape[1]
    heads = window_bias.shape[0]
    planes = lax.axis_size("gz")
    windows = width // channels // 8
    position = lax.axis_index("gz") * lax.axis_size("tile") + lax.axis_index("tile")
    packed = pack(volume.reshape(rows, width), windows, channels)
    tokens = lax.all_to_all(packed, ("gz", "tile"), split_axis=0, concat_axis=0, tiled=True)
    bias = pair_bias(window_bias, position == windows - 1)
    qkv = jnp.stack([folded(norm_gains[0], qkv_weight[0]), folded(norm_gains[2], qkv_weight[1])])
    up = jnp.stack([folded(norm_gains[1], up_weight[0]), folded(norm_gains[3], up_weight[1])])
    out = jnp.transpose(out_weight, (0, 2, 1))
    down = jnp.transpose(down_weight, (0, 2, 1))
    row = jnp.arange(heads * planes, dtype=jnp.int32)[:, None]
    column = jnp.arange(planes * channels, dtype=jnp.int32)[None, :]
    gather = (
        (row // planes == column % channels // (channels // heads)) & (row % planes == column // channels)
    ).astype(jnp.bfloat16)
    mixed = blocks(tokens, bias, qkv, out, up, down, gather)
    returned = lax.all_to_all(mixed, ("gz", "tile"), split_axis=0, concat_axis=0, tiled=True)
    return unpack(returned, rows, width).reshape(1, rows, width)


def fits_windows(mesh, volume, norm_gains, window_bias):
    planes, tiles = mesh.shape["gz"], mesh.shape["tile"]
    channels, heads = norm_gains.shape[1], window_bias.shape[0]
    return (
        tiles == 2
        and planes == 8
        and volume.shape[1] == 16 * tiles
        and volume.shape[2] == 8 * channels * planes * tiles
        and channels == 96
        and heads == 3
    )


def solution(mesh):
    placed = (P(("groups", "gz"), "tile", None), P(), P(), P(), P(), P(), P())

    def run(volume, norm_gains, *weights):
        chosen = window_body if fits_windows(mesh, volume, norm_gains, weights[-1]) else general_body
        return jax.shard_map(
            chosen,
            mesh=mesh,
            in_specs=placed,
            out_specs=P(("groups", "gz"), "tile", None),
            check_vma=False,
        )(volume, norm_gains, *weights)

    return run
```

```python
import jax
import jax.numpy as jnp
from jax import lax
from jax.experimental import pallas as pl
from jax.experimental.pallas import tpu as pltpu
from jax.sharding import PartitionSpec as P

epsilon = 1e-05


def shifted(array, axis, by):
    peers = lax.axis_size(axis)
    return lax.ppermute(array, axis, [(i, (i + by) % peers) for i in range(peers)])


def layer_norm(tokens, gain):
    values = tokens.astype(jnp.float32)
    average = jnp.mean(values, -1, keepdims=True)
    centered = values - average
    variance = jnp.mean(centered * centered, -1, keepdims=True)
    return (centered * lax.rsqrt(variance + epsilon) * gain).astype(jnp.bfloat16)


def feed_forward(tokens, gain, up_matrix, down_matrix):
    normed = layer_norm(tokens, gain)
    hidden = jax.nn.gelu(jnp.dot(normed, up_matrix, preferred_element_type=jnp.float32)).astype(
        jnp.bfloat16
    )
    total = tokens.astype(jnp.float32) + jnp.dot(
        hidden, down_matrix, preferred_element_type=jnp.float32
    )
    return total.astype(jnp.bfloat16)


def edge_label(index, extent):
    return jnp.where(index < 4, 2, jnp.where(index >= extent - 4, 1, 0)).astype(jnp.int32)


def head_masks(heads, channels):
    owner = jnp.arange(channels, dtype=jnp.int32) // (channels // heads)
    return (owner[None, :] == jnp.arange(heads, dtype=jnp.int32)[:, None]).astype(jnp.bfloat16)


def window_attention(
    row_block, first_row, height, channels, norm_gains, qkv_weight, out_weight, window_bias
):
    count = row_block.shape[0]
    columns = row_block.shape[1] // channels
    heads = window_bias.shape[0]
    head_size = channels // heads
    masks = head_masks(heads, channels)
    rolled = jnp.roll(row_block, -4 * channels, axis=1)
    windowed = rolled.reshape(count // 8, 8, columns // 8, 8 * channels).transpose(0, 2, 1, 3)
    normed = layer_norm(windowed.reshape(-1, channels), norm_gains[0])
    packed = jnp.dot(normed, qkv_weight[0], preferred_element_type=jnp.float32).astype(jnp.bfloat16)
    packed = packed.reshape(-1, 64, 3 * channels)
    queries = packed[:, :, :channels]
    keys = packed[:, :, channels : 2 * channels]
    values = packed[:, :, 2 * channels :]
    initial_rows = jnp.mod(first_row + jnp.arange(count, dtype=jnp.int32), height)
    initial_columns = jnp.mod(jnp.arange(columns, dtype=jnp.int32) + 4, columns)
    labels = (
        edge_label(initial_rows, height)[:, None] * 3
        + edge_label(initial_columns, columns)[None, :]
    )
    window_labels = (
        labels.reshape(count // 8, 8, columns // 8, 8).transpose(0, 2, 1, 3).reshape(-1, 64)
    )
    allowed = window_labels[:, :, None] == window_labels[:, None, :]
    head_queries = queries[:, None] * masks[None, :, None, :]
    scores = jnp.einsum("nhqc,nkc->nhqk", head_queries, keys, preferred_element_type=jnp.float32)
    scores = scores * head_size ** (-0.5) + window_bias[None]
    scores = jnp.where(allowed[:, None], scores, -jnp.inf)
    weights = jax.nn.softmax(scores, axis=-1).astype(jnp.bfloat16)
    head_values = values[:, None] * masks[None, :, None, :]
    attended = jnp.einsum(
        "nhqk,nhkc->nqc", weights, head_values, preferred_element_type=jnp.float32
    ).astype(jnp.bfloat16)
    lateral = jnp.dot(
        attended.reshape(-1, channels), out_weight[0], preferred_element_type=jnp.float32
    ).astype(jnp.bfloat16)
    lateral = lateral.reshape(count // 8, columns // 8, 8, 8 * channels).transpose(0, 2, 1, 3)
    return jnp.roll(lateral.reshape(count, columns * channels), 4 * channels, axis=1)


def axial_block(pencils, norm_gains, qkv_weight, out_weight, up_weight, down_weight, heads):
    planes, count, channels = pencils.shape
    head_size = channels // heads
    masks = head_masks(heads, channels)
    flat = jnp.transpose(pencils, (1, 0, 2)).reshape(-1, channels)
    normed = layer_norm(flat, norm_gains[2])
    packed = jnp.dot(normed, qkv_weight[1], preferred_element_type=jnp.float32).astype(jnp.bfloat16)
    packed = packed.reshape(count, planes, 3 * channels)
    queries = packed[:, :, :channels]
    keys = packed[:, :, channels : 2 * channels]
    values = packed[:, :, 2 * channels :]
    head_queries = queries[:, None] * masks[None, :, None, :]
    scores = jnp.einsum("phzc,pyc->phzy", head_queries, keys, preferred_element_type=jnp.float32)
    weights = jax.nn.softmax(scores * head_size ** (-0.5), axis=-1).astype(jnp.bfloat16)
    head_values = values[:, None] * masks[None, :, None, :]
    attended = jnp.einsum(
        "phzy,phyc->pzc", weights, head_values, preferred_element_type=jnp.float32
    ).astype(jnp.bfloat16)
    projected = jnp.dot(
        attended.reshape(-1, channels), out_weight[1], preferred_element_type=jnp.float32
    ).astype(jnp.bfloat16)
    after = (flat.astype(jnp.float32) + projected.astype(jnp.float32)).astype(jnp.bfloat16)
    mixed = feed_forward(after, norm_gains[3], up_weight[1], down_weight[1]).reshape(
        count, planes, channels
    )
    return jnp.transpose(mixed, (1, 0, 2))


def general_body(volume, norm_gains, qkv_weight, out_weight, up_weight, down_weight, window_bias):
    rows_here = volume.shape[1]
    row_width = volume.shape[2]
    channels = norm_gains.shape[1]
    heads = window_bias.shape[0]
    height = rows_here * lax.axis_size("tile")
    tile_start = lax.axis_index("tile") * rows_here
    plane = volume.reshape(rows_here, row_width)
    next_rows = shifted(plane[:4], "tile", -1)
    extended = jnp.concatenate([plane[4:], next_rows], 0)
    attended = window_attention(
        extended, tile_start + 4, height, channels, norm_gains, qkv_weight, out_weight, window_bias
    )
    tail_rows = shifted(attended[-4:], "tile", 1)
    lateral = jnp.concatenate([tail_rows, attended[:-4]], 0)
    middle = (
        (plane.astype(jnp.float32) + lateral.astype(jnp.float32))
        .astype(jnp.bfloat16)
        .reshape(-1, channels)
    )
    planes = lax.axis_size("gz")
    middle = feed_forward(middle, norm_gains[1], up_weight[0], down_weight[0])
    grouped = middle.reshape(planes, -1, channels)
    pencils = lax.all_to_all(grouped, "gz", split_axis=0, concat_axis=0, tiled=True)
    returned = lax.all_to_all(
        axial_block(pencils, norm_gains, qkv_weight, out_weight, up_weight, down_weight, heads),
        "gz",
        split_axis=0,
        concat_axis=0,
        tiled=True,
    )
    return returned.reshape(1, rows_here, row_width)


LOG2E = 1.4426950408889634


def normalised(tokens):
    average = jnp.mean(tokens, 0, keepdims=True)
    centered = tokens - average
    variance = jnp.mean(centered * centered, 0, keepdims=True)
    return (centered * lax.rsqrt(variance + epsilon)).astype(jnp.bfloat16)


def product(left, right):
    return jnp.dot(left, right, preferred_element_type=jnp.float32)


def gated(half):
    half = half.astype(jnp.bfloat16)
    inner = half * (1.5957691216057308 + 0.285419265090401 * (half * half))
    return half + half * jnp.tanh(inner)


def column_feed_forward(tokens, up, down):
    return tokens + product(down, gated(product(up, normalised(tokens))))


def pack_kernel(volume_ref, packed_ref):
    windows, channels, _ = packed_ref.shape
    width = 8 * channels
    half = width // 2
    for window in range(windows):
        start = window * width + half
        if window < windows - 1:
            chunk = volume_ref[:, start : start + width]
        else:
            chunk = jnp.concatenate([volume_ref[:, start:], volume_ref[:, :half]], axis=1)
        chunk = chunk.astype(jnp.float32)
        rolled = jnp.concatenate([chunk[4:], chunk[:4]], axis=0)
        pieces = [
            rolled[8 * part : 8 * part + 8, channels * column : channels * (column + 1)]
            for part in range(2)
            for column in range(8)
        ]
        tokens = jnp.concatenate(pieces, axis=0)
        packed_ref[window] = tokens.T.astype(jnp.bfloat16)


def unpack_kernel(packed_ref, volume_ref):
    windows, channels, _ = packed_ref.shape
    width = 8 * channels
    half = width // 2
    for window in range(windows):
        tokens = packed_ref[window].astype(jnp.float32).T
        parts = [
            jnp.concatenate(
                [tokens[64 * part + 8 * column : 64 * part + 8 * column + 8] for column in range(8)], axis=1
            )
            for part in range(2)
        ]
        rows = jnp.concatenate([parts[1][4:], parts[0], parts[1][:4]], axis=0).astype(jnp.bfloat16)
        start = window * width + half
        if window < windows - 1:
            volume_ref[:, start : start + width] = rows
        else:
            volume_ref[:, start:] = rows[:, :half]
            volume_ref[:, :half] = rows[:, half:]


GROUP = 8


def blocks_kernel(
    tokens_ref,
    bias_ref,
    qkv_ref,
    out_ref,
    mix_ref,
    up_ref,
    down_ref,
    gather_ref,
    result_ref,
    planar_ref,
    query_ref,
    key_ref,
    value_ref,
):
    channels = tokens_ref.shape[1]
    planes = tokens_ref.shape[0] // 2
    heads = bias_ref.shape[1] // 64
    head_size = channels // heads
    lane = lax.broadcasted_iota(jnp.int32, (1, 128), 1)
    own = (lane < 64) | (lane % 8 < 4)
    first = lane < 64

    def lateral(step, carry):
        tokens = []
        for plane in range(GROUP):
            one = tokens_ref[2 * (step * GROUP + plane)].astype(jnp.float32)
            two = tokens_ref[2 * (step * GROUP + plane) + 1].astype(jnp.float32)
            tokens += [jnp.where(own, one, two), jnp.where(own, two, one)]
        tokens = jnp.concatenate(tokens, axis=1)
        packed = product(qkv_ref[0], normalised(tokens))
        queries = packed[:channels]
        keys = packed[channels : 2 * channels]
        values = packed[2 * channels :].astype(jnp.bfloat16)
        blank = jnp.zeros((128 - channels, 128), jnp.bfloat16)
        scores = []
        for pair in range(2 * GROUP):
            lanes = slice(128 * pair, 128 * pair + 128)
            query = queries[:, lanes]
            right = jnp.concatenate(
                [
                    jnp.where(first, query, 0.0).astype(jnp.bfloat16),
                    blank,
                    jnp.where(first, 0.0, query).astype(jnp.bfloat16),
                    blank,
                ],
                axis=0,
            )
            key = jnp.concatenate([keys[:, lanes], jnp.zeros((128 - channels, 128), jnp.float32)], axis=0).T
            left = []
            for head in range(heads):
                mine = lane // head_size == head
                masked = jnp.where(mine, key, 0.0).astype(jnp.bfloat16)
                left.append(jnp.concatenate([masked[:64], masked[64:]], axis=1))
            scores.append(product(jnp.concatenate(left, axis=0), right) + bias_ref[pair % 2])
        attended = []
        for pair in range(2 * GROUP):
            lanes = slice(128 * pair, 128 * pair + 128)
            mixed = []
            for head in range(heads):
                own_scores = scores[pair][64 * head : 64 * head + 64]
                weights = jnp.exp2(own_scores - jnp.max(own_scores, axis=0, keepdims=True))
                total = jnp.sum(weights, axis=0, keepdims=True)
                spread = jnp.concatenate(
                    [
                        jnp.where(first, weights, 0.0).astype(jnp.bfloat16),
                        jnp.where(first, 0.0, weights).astype(jnp.bfloat16),
                    ],
                    axis=0,
                )
                head_mixed = product(values[head_size * head : head_size * (head + 1), lanes], spread)
                mixed.append((head_mixed * (1.0 / total)).astype(jnp.bfloat16))
            attended.append(jnp.concatenate(mixed, axis=0))
        attended = jnp.concatenate(attended, axis=1)
        middle = tokens + product(out_ref[...], attended)
        planar = column_feed_forward(middle, up_ref[0], down_ref[0])
        packed = product(qkv_ref[1], normalised(planar)).astype(jnp.bfloat16)
        for plane in range(GROUP):
            here = pl.ds(pl.multiple_of((step * GROUP + plane) * channels, channels), channels)
            lanes = slice(256 * plane, 256 * plane + 256)
            planar_ref[here, :] = planar[:, lanes]
            query_ref[here, :] = packed[:channels, lanes]
            key_ref[here, :] = packed[channels : 2 * channels, lanes]
            value_ref[here, :] = packed[2 * channels :, lanes]
        return carry

    def axial(step, carry):
        scores = []
        for plane in range(GROUP):
            here = pl.ds(pl.multiple_of((step * GROUP + plane) * channels, channels), channels)
            query = query_ref[here, :]
            pairs = jnp.concatenate(
                [query * key_ref[channels * other : channels * (other + 1), :] for other in range(planes)], axis=0
            )
            scores.append(product(gather_ref[...], pairs))
        after = []
        for plane in range(GROUP):
            here = pl.ds(pl.multiple_of((step * GROUP + plane) * channels, channels), channels)
            weights = []
            for head in range(heads):
                own_scores = scores[plane][planes * head : planes * (head + 1)]
                own_weights = jnp.exp2(own_scores - jnp.max(own_scores, axis=0, keepdims=True))
                weights.append(own_weights * (1.0 / jnp.sum(own_weights, axis=0, keepdims=True)))
            spread = []
            for other in range(planes):
                wide = jnp.concatenate(
                    [
                        jnp.broadcast_to(weights[head][other : other + 1], (head_size, 256)).astype(jnp.bfloat16)
                        for head in range(heads)
                    ],
                    axis=0,
                )
                spread.append(wide * value_ref[channels * other : channels * (other + 1), :])
            after.append(planar_ref[here, :] + product(mix_ref[...], jnp.concatenate(spread, axis=0)))
        after = jnp.concatenate(after, axis=1)
        mixed = column_feed_forward(after, up_ref[1], down_ref[1])
        for plane in range(GROUP):
            one = mixed[:, 256 * plane : 256 * plane + 128]
            two = mixed[:, 256 * plane + 128 : 256 * plane + 256]
            result_ref[2 * (step * GROUP + plane)] = jnp.where(own, one, two).astype(jnp.bfloat16)
            result_ref[2 * (step * GROUP + plane) + 1] = jnp.where(own, two, one).astype(jnp.bfloat16)
        return carry

    lax.fori_loop(0, planes // GROUP, lateral, 0)
    lax.fori_loop(0, planes // GROUP, axial, 0)


def pack(rows, windows, channels):
    return pl.pallas_call(
        pack_kernel,
        out_shape=jax.ShapeDtypeStruct((windows, channels, 128), jnp.bfloat16),
        name="pack_windows",
    )(rows)


def unpack(packed, rows, width):
    return pl.pallas_call(
        unpack_kernel,
        out_shape=jax.ShapeDtypeStruct((rows, width), jnp.bfloat16),
        name="unpack_windows",
    )(packed)


def blocks(tokens, *operands):
    sources, channels, _ = tokens.shape
    rows = sources // 2 * channels
    return pl.pallas_call(
        blocks_kernel,
        out_shape=jax.ShapeDtypeStruct(tokens.shape, jnp.bfloat16),
        scratch_shapes=[
            pltpu.VMEM((rows, 256), jnp.float32),
            pltpu.VMEM((rows, 256), jnp.bfloat16),
            pltpu.VMEM((rows, 256), jnp.bfloat16),
            pltpu.VMEM((rows, 256), jnp.bfloat16),
        ],
        compiler_params=pltpu.CompilerParams(vmem_limit_bytes=40 * 1024 * 1024),
        name="both_blocks",
    )(tokens, *operands)


def pair_bias(window_bias, last):
    heads = window_bias.shape[0]
    split = window_bias.reshape(heads, 8, 8, 8, 8).transpose(0, 4, 3, 2, 1).reshape(heads, 64, 64) * LOG2E
    index = jnp.arange(64, dtype=jnp.int32)
    column_side = (index // 8 < 4).astype(jnp.int32)
    row_side = (index % 8 < 4).astype(jnp.int32)
    column_cut = (column_side[:, None] != column_side[None, :]) & last
    row_cut = row_side[:, None] != row_side[None, :]
    plain = jnp.where(column_cut[None], -jnp.inf, split)
    cut = jnp.where(row_cut[None], -jnp.inf, plain)
    one = jnp.concatenate([plain, plain], axis=2).reshape(heads * 64, 128)
    two = jnp.concatenate([plain, cut], axis=2).reshape(heads * 64, 128)
    return jnp.stack([one, two])


def folded(gain, matrix, scale):
    return (gain[:, None] * matrix.astype(jnp.float32) * scale).T.astype(jnp.bfloat16)


def window_body(volume, norm_gains, qkv_weight, out_weight, up_weight, down_weight, window_bias):
    rows = volume.shape[1]
    width = volume.shape[2]
    channels = norm_gains.shape[1]
    heads = window_bias.shape[0]
    planes = lax.axis_size("gz")
    windows = width // channels // 8
    position = lax.axis_index("gz") * lax.axis_size("tile") + lax.axis_index("tile")
    packed = pack(volume.reshape(rows, width), windows, channels)
    tokens = lax.all_to_all(packed, ("gz", "tile"), split_axis=0, concat_axis=0, tiled=True)
    bias = pair_bias(window_bias, position == windows - 1)
    is_query = jnp.arange(3 * channels, dtype=jnp.int32) < channels
    scale = jnp.where(is_query, LOG2E * (channels // heads) ** (-0.5), 1.0)[None, :]
    qkv = jnp.stack([folded(norm_gains[0], qkv_weight[0], scale), folded(norm_gains[2], qkv_weight[1], scale)])
    up = jnp.stack([folded(norm_gains[1], up_weight[0], 0.5), folded(norm_gains[3], up_weight[1], 0.5)])
    out = out_weight[0].T
    mix = jnp.tile(out_weight[1].T, (1, planes))
    down = jnp.transpose(down_weight, (0, 2, 1))
    row = jnp.arange(heads * planes, dtype=jnp.int32)[:, None]
    column = jnp.arange(planes * channels, dtype=jnp.int32)[None, :]
    gather = (
        (row // planes == column % channels // (channels // heads)) & (row % planes == column // channels)
    ).astype(jnp.bfloat16)
    mixed = blocks(tokens, bias, qkv, out, mix, up, down, gather)
    returned = lax.all_to_all(mixed, ("gz", "tile"), split_axis=0, concat_axis=0, tiled=True)
    return unpack(returned, rows, width).reshape(1, rows, width)


def fits_windows(mesh, volume, norm_gains, window_bias):
    planes, tiles = mesh.shape["gz"], mesh.shape["tile"]
    channels, heads = norm_gains.shape[1], window_bias.shape[0]
    return (
        tiles == 2
        and planes == 8
        and volume.shape[1] == 16 * tiles
        and volume.shape[2] == 8 * channels * planes * tiles
        and channels == 96
        and heads == 3
    )


def solution(mesh):
    placed = (P(("groups", "gz"), "tile", None), P(), P(), P(), P(), P(), P())

    def run(volume, norm_gains, *weights):
        chosen = window_body if fits_windows(mesh, volume, norm_gains, weights[-1]) else general_body
        return jax.shard_map(
            chosen,
            mesh=mesh,
            in_specs=placed,
            out_specs=P(("groups", "gz"), "tile", None),
            check_vma=False,
        )(volume, norm_gains, *weights)

    return run
```

```python
import jax
import jax.numpy as jnp
from jax import lax
from jax.experimental import pallas as pl
from jax.experimental.pallas import tpu as pltpu
from jax.sharding import PartitionSpec as P

epsilon = 1e-05


def shifted(array, axis, by):
    peers = lax.axis_size(axis)
    return lax.ppermute(array, axis, [(i, (i + by) % peers) for i in range(peers)])


def layer_norm(tokens, gain):
    values = tokens.astype(jnp.float32)
    average = jnp.mean(values, -1, keepdims=True)
    centered = values - average
    variance = jnp.mean(centered * centered, -1, keepdims=True)
    return (centered * lax.rsqrt(variance + epsilon) * gain).astype(jnp.bfloat16)


def feed_forward(tokens, gain, up_matrix, down_matrix):
    normed = layer_norm(tokens, gain)
    hidden = jax.nn.gelu(jnp.dot(normed, up_matrix, preferred_element_type=jnp.float32)).astype(
        jnp.bfloat16
    )
    total = tokens.astype(jnp.float32) + jnp.dot(
        hidden, down_matrix, preferred_element_type=jnp.float32
    )
    return total.astype(jnp.bfloat16)


def edge_label(index, extent):
    return jnp.where(index < 4, 2, jnp.where(index >= extent - 4, 1, 0)).astype(jnp.int32)


def head_masks(heads, channels):
    owner = jnp.arange(channels, dtype=jnp.int32) // (channels // heads)
    return (owner[None, :] == jnp.arange(heads, dtype=jnp.int32)[:, None]).astype(jnp.bfloat16)


def window_attention(
    row_block, first_row, height, channels, norm_gains, qkv_weight, out_weight, window_bias
):
    count = row_block.shape[0]
    columns = row_block.shape[1] // channels
    heads = window_bias.shape[0]
    head_size = channels // heads
    masks = head_masks(heads, channels)
    rolled = jnp.roll(row_block, -4 * channels, axis=1)
    windowed = rolled.reshape(count // 8, 8, columns // 8, 8 * channels).transpose(0, 2, 1, 3)
    normed = layer_norm(windowed.reshape(-1, channels), norm_gains[0])
    packed = jnp.dot(normed, qkv_weight[0], preferred_element_type=jnp.float32).astype(jnp.bfloat16)
    packed = packed.reshape(-1, 64, 3 * channels)
    queries = packed[:, :, :channels]
    keys = packed[:, :, channels : 2 * channels]
    values = packed[:, :, 2 * channels :]
    initial_rows = jnp.mod(first_row + jnp.arange(count, dtype=jnp.int32), height)
    initial_columns = jnp.mod(jnp.arange(columns, dtype=jnp.int32) + 4, columns)
    labels = (
        edge_label(initial_rows, height)[:, None] * 3
        + edge_label(initial_columns, columns)[None, :]
    )
    window_labels = (
        labels.reshape(count // 8, 8, columns // 8, 8).transpose(0, 2, 1, 3).reshape(-1, 64)
    )
    allowed = window_labels[:, :, None] == window_labels[:, None, :]
    head_queries = queries[:, None] * masks[None, :, None, :]
    scores = jnp.einsum("nhqc,nkc->nhqk", head_queries, keys, preferred_element_type=jnp.float32)
    scores = scores * head_size ** (-0.5) + window_bias[None]
    scores = jnp.where(allowed[:, None], scores, -jnp.inf)
    weights = jax.nn.softmax(scores, axis=-1).astype(jnp.bfloat16)
    head_values = values[:, None] * masks[None, :, None, :]
    attended = jnp.einsum(
        "nhqk,nhkc->nqc", weights, head_values, preferred_element_type=jnp.float32
    ).astype(jnp.bfloat16)
    lateral = jnp.dot(
        attended.reshape(-1, channels), out_weight[0], preferred_element_type=jnp.float32
    ).astype(jnp.bfloat16)
    lateral = lateral.reshape(count // 8, columns // 8, 8, 8 * channels).transpose(0, 2, 1, 3)
    return jnp.roll(lateral.reshape(count, columns * channels), 4 * channels, axis=1)


def axial_block(pencils, norm_gains, qkv_weight, out_weight, up_weight, down_weight, heads):
    planes, count, channels = pencils.shape
    head_size = channels // heads
    masks = head_masks(heads, channels)
    flat = jnp.transpose(pencils, (1, 0, 2)).reshape(-1, channels)
    normed = layer_norm(flat, norm_gains[2])
    packed = jnp.dot(normed, qkv_weight[1], preferred_element_type=jnp.float32).astype(jnp.bfloat16)
    packed = packed.reshape(count, planes, 3 * channels)
    queries = packed[:, :, :channels]
    keys = packed[:, :, channels : 2 * channels]
    values = packed[:, :, 2 * channels :]
    head_queries = queries[:, None] * masks[None, :, None, :]
    scores = jnp.einsum("phzc,pyc->phzy", head_queries, keys, preferred_element_type=jnp.float32)
    weights = jax.nn.softmax(scores * head_size ** (-0.5), axis=-1).astype(jnp.bfloat16)
    head_values = values[:, None] * masks[None, :, None, :]
    attended = jnp.einsum(
        "phzy,phyc->pzc", weights, head_values, preferred_element_type=jnp.float32
    ).astype(jnp.bfloat16)
    projected = jnp.dot(
        attended.reshape(-1, channels), out_weight[1], preferred_element_type=jnp.float32
    ).astype(jnp.bfloat16)
    after = (flat.astype(jnp.float32) + projected.astype(jnp.float32)).astype(jnp.bfloat16)
    mixed = feed_forward(after, norm_gains[3], up_weight[1], down_weight[1]).reshape(
        count, planes, channels
    )
    return jnp.transpose(mixed, (1, 0, 2))


def general_body(volume, norm_gains, qkv_weight, out_weight, up_weight, down_weight, window_bias):
    rows_here = volume.shape[1]
    row_width = volume.shape[2]
    channels = norm_gains.shape[1]
    heads = window_bias.shape[0]
    height = rows_here * lax.axis_size("tile")
    tile_start = lax.axis_index("tile") * rows_here
    plane = volume.reshape(rows_here, row_width)
    next_rows = shifted(plane[:4], "tile", -1)
    extended = jnp.concatenate([plane[4:], next_rows], 0)
    attended = window_attention(
        extended, tile_start + 4, height, channels, norm_gains, qkv_weight, out_weight, window_bias
    )
    tail_rows = shifted(attended[-4:], "tile", 1)
    lateral = jnp.concatenate([tail_rows, attended[:-4]], 0)
    middle = (
        (plane.astype(jnp.float32) + lateral.astype(jnp.float32))
        .astype(jnp.bfloat16)
        .reshape(-1, channels)
    )
    planes = lax.axis_size("gz")
    middle = feed_forward(middle, norm_gains[1], up_weight[0], down_weight[0])
    grouped = middle.reshape(planes, -1, channels)
    pencils = lax.all_to_all(grouped, "gz", split_axis=0, concat_axis=0, tiled=True)
    returned = lax.all_to_all(
        axial_block(pencils, norm_gains, qkv_weight, out_weight, up_weight, down_weight, heads),
        "gz",
        split_axis=0,
        concat_axis=0,
        tiled=True,
    )
    return returned.reshape(1, rows_here, row_width)


LOG2E = 1.4426950408889634


def normalised(tokens):
    average = jnp.mean(tokens, 0, keepdims=True)
    centered = tokens - average
    variance = jnp.mean(centered * centered, 0, keepdims=True)
    return (centered * lax.rsqrt(variance + epsilon)).astype(jnp.bfloat16)


def product(left, right):
    return jnp.dot(left, right, preferred_element_type=jnp.float32)


GELU_IN = 0.035677408136300125 ** (1 / 3)
GELU_LINEAR = 0.7978845608028654 / GELU_IN
GELU_OUT = 0.5 / GELU_IN


def gated(scaled):
    scaled = scaled.astype(jnp.bfloat16)
    return scaled + scaled * jnp.tanh(scaled * (GELU_LINEAR + scaled * scaled))


def pack_kernel(volume_ref, packed_ref):
    windows, channels, _ = packed_ref.shape
    width = 8 * channels
    half = width // 2
    for window in range(windows):
        start = window * width + half
        if window < windows - 1:
            chunk = volume_ref[:, start : start + width]
        else:
            chunk = jnp.concatenate([volume_ref[:, start:], volume_ref[:, :half]], axis=1)
        chunk = chunk.astype(jnp.float32)
        rolled = jnp.concatenate([chunk[4:], chunk[:4]], axis=0)
        pieces = [
            rolled[8 * part : 8 * part + 8, channels * column : channels * (column + 1)]
            for part in range(2)
            for column in range(8)
        ]
        tokens = jnp.concatenate(pieces, axis=0)
        packed_ref[window] = tokens.T.astype(jnp.bfloat16)


def unpack_kernel(packed_ref, volume_ref):
    windows, channels, _ = packed_ref.shape
    width = 8 * channels
    half = width // 2
    for window in range(windows):
        tokens = packed_ref[window].astype(jnp.float32).T
        parts = [
            jnp.concatenate(
                [tokens[64 * part + 8 * column : 64 * part + 8 * column + 8] for column in range(8)], axis=1
            )
            for part in range(2)
        ]
        rows = jnp.concatenate([parts[1][4:], parts[0], parts[1][:4]], axis=0).astype(jnp.bfloat16)
        start = window * width + half
        if window < windows - 1:
            volume_ref[:, start : start + width] = rows
        else:
            volume_ref[:, start:] = rows[:, :half]
            volume_ref[:, :half] = rows[:, half:]


TOGETHER = 8
LAG = 1


def in_waves(stages, members, together, lag):
    groups = [members[start : start + together] for start in range(0, len(members), together)]
    for step in range(len(stages) + lag * (len(groups) - 1)):
        for index, group in enumerate(groups):
            if 0 <= step - lag * index < len(stages):
                for member in group:
                    stages[step - lag * index](member)


def blocks_kernel(
    tokens_ref,
    bias_ref,
    qkv_ref,
    out_ref,
    mix_ref,
    up_ref,
    down_ref,
    gather_ref,
    result_ref,
    planar_ref,
    query_ref,
    key_ref,
    value_ref,
):
    channels = tokens_ref.shape[1]
    planes = tokens_ref.shape[0] // 2
    heads = bias_ref.shape[1] // 64
    head_size = channels // heads
    lane = lax.broadcasted_iota(jnp.int32, (1, 128), 1)
    own = (lane < 64) | (lane % 8 < 4)
    first = lane < 64
    blank = jnp.zeros((128 - channels, 128), jnp.bfloat16)
    blank_rows = jnp.zeros((128 - channels, 128), jnp.float32)
    held = [{} for _ in range(planes)]

    def rows_of(plane):
        return slice(plane * channels, (plane + 1) * channels)

    def load(plane):
        one, two = tokens_ref[2 * plane], tokens_ref[2 * plane + 1]
        tokens = jnp.concatenate([jnp.where(own, one, two), jnp.where(own, two, one)], axis=1)
        held[plane]["x"] = tokens.astype(jnp.float32)

    def norm(plane):
        held[plane]["n"] = normalised(held[plane]["x"])

    def lateral_qkv(plane):
        packed = product(qkv_ref[0], held[plane].pop("n"))
        held[plane]["q"] = packed[:channels]
        held[plane]["k"] = packed[channels : 2 * channels]
        held[plane]["v"] = packed[2 * channels :].astype(jnp.bfloat16)

    def lateral_scores(plane):
        queries, keys = held[plane].pop("q"), held[plane].pop("k")
        scores = []
        for pair in range(2):
            lanes = slice(128 * pair, 128 * pair + 128)
            query = queries[:, lanes]
            right = jnp.concatenate(
                [
                    jnp.where(first, query, 0.0).astype(jnp.bfloat16),
                    blank,
                    jnp.where(first, 0.0, query).astype(jnp.bfloat16),
                    blank,
                ],
                axis=0,
            )
            key = jnp.concatenate([keys[:, lanes], blank_rows], axis=0).T
            left = []
            for head in range(heads):
                masked = jnp.where(lane // head_size == head, key, 0.0).astype(jnp.bfloat16)
                left.append(jnp.concatenate([masked[:64], masked[64:]], axis=1))
            scores.append(product(jnp.concatenate(left, axis=0), right) + bias_ref[pair])
        held[plane]["s"] = scores

    def lateral_weights(plane):
        scores = held[plane].pop("s")
        held[plane]["w"] = []
        for pair in range(2):
            for head in range(heads):
                own_scores = scores[pair][64 * head : 64 * head + 64]
                weights = jnp.exp2(own_scores - jnp.max(own_scores, axis=0, keepdims=True))
                total = jnp.sum(weights, axis=0, keepdims=True)
                spread = jnp.concatenate(
                    [
                        jnp.where(first, weights, 0.0).astype(jnp.bfloat16),
                        jnp.where(first, 0.0, weights).astype(jnp.bfloat16),
                    ],
                    axis=0,
                )
                held[plane]["w"].append((spread, 1.0 / total))

    def lateral_values(plane):
        weights, values = held[plane].pop("w"), held[plane].pop("v")
        attended = []
        for pair in range(2):
            lanes = slice(128 * pair, 128 * pair + 128)
            mixed = []
            for head in range(heads):
                spread, inverse = weights[heads * pair + head]
                own_mixed = product(values[head_size * head : head_size * (head + 1), lanes], spread)
                mixed.append((own_mixed * inverse).astype(jnp.bfloat16))
            attended.append(jnp.concatenate(mixed, axis=0))
        held[plane]["a"] = jnp.concatenate(attended, axis=1)

    def lateral_out(plane):
        held[plane]["x"] = held[plane]["x"] + product(out_ref[...], held[plane].pop("a"))

    def raised(layer):
        def stage(plane):
            held[plane]["h"] = product(up_ref[layer], held[plane].pop("n"))

        return stage

    def gelu(plane):
        held[plane]["g"] = gated(held[plane].pop("h"))

    def lowered(layer):
        def stage(plane):
            held[plane]["x"] = held[plane]["x"] + product(down_ref[layer], held[plane].pop("g"))

        return stage

    def axial_qkv(plane):
        packed = product(qkv_ref[1], held[plane].pop("n")).astype(jnp.bfloat16)
        planar_ref[rows_of(plane), :] = held[plane].pop("x")
        query_ref[rows_of(plane), :] = packed[:channels]
        key_ref[rows_of(plane), :] = packed[channels : 2 * channels]
        value_ref[rows_of(plane), :] = packed[2 * channels :]

    def axial_scores(plane):
        query = query_ref[rows_of(plane), :]
        pairs = jnp.concatenate([query * key_ref[rows_of(other), :] for other in range(planes)], axis=0)
        held[plane]["s"] = product(gather_ref[...], pairs)

    def axial_weights(plane):
        scores = held[plane].pop("s")
        weights = []
        for head in range(heads):
            own_scores = scores[planes * head : planes * (head + 1)]
            own_weights = jnp.exp2(own_scores - jnp.max(own_scores, axis=0, keepdims=True))
            weights.append(own_weights * (1.0 / jnp.sum(own_weights, axis=0, keepdims=True)))
        held[plane]["w"] = weights

    def axial_values(plane):
        weights = held[plane].pop("w")
        spread = []
        for other in range(planes):
            wide = jnp.concatenate(
                [
                    jnp.broadcast_to(weights[head][other : other + 1], (head_size, 256)).astype(jnp.bfloat16)
                    for head in range(heads)
                ],
                axis=0,
            )
            spread.append(wide * value_ref[rows_of(other), :])
        held[plane]["x"] = planar_ref[rows_of(plane), :] + product(mix_ref[...], jnp.concatenate(spread, axis=0))

    def store(plane):
        mixed = held[plane].pop("x").astype(jnp.bfloat16)
        one, two = mixed[:, :128], mixed[:, 128:]
        result_ref[2 * plane] = jnp.where(own, one, two)
        result_ref[2 * plane + 1] = jnp.where(own, two, one)

    members = list(range(planes))
    lateral = [load, norm, lateral_qkv, lateral_scores, lateral_weights, lateral_values, lateral_out]
    lateral += [norm, raised(0), gelu, lowered(0), norm, axial_qkv]
    axial = [axial_scores, axial_weights, axial_values, norm, raised(1), gelu, lowered(1), store]
    in_waves(lateral, members, TOGETHER, LAG)
    in_waves(axial, members, TOGETHER, LAG)


def pack(rows, windows, channels):
    return pl.pallas_call(
        pack_kernel,
        out_shape=jax.ShapeDtypeStruct((windows, channels, 128), jnp.bfloat16),
        compiler_params=pltpu.CompilerParams(vmem_limit_bytes=16 * 1024 * 1024),
        name="pack_windows",
    )(rows)


def unpack(packed, rows, width):
    return pl.pallas_call(
        unpack_kernel,
        out_shape=jax.ShapeDtypeStruct((rows, width), jnp.bfloat16),
        compiler_params=pltpu.CompilerParams(vmem_limit_bytes=16 * 1024 * 1024),
        name="unpack_windows",
    )(packed)


def blocks(tokens, *operands):
    sources, channels, _ = tokens.shape
    rows = sources // 2 * channels
    return pl.pallas_call(
        blocks_kernel,
        out_shape=jax.ShapeDtypeStruct(tokens.shape, jnp.bfloat16),
        scratch_shapes=[
            pltpu.VMEM((rows, 256), jnp.float32),
            pltpu.VMEM((rows, 256), jnp.bfloat16),
            pltpu.VMEM((rows, 256), jnp.bfloat16),
            pltpu.VMEM((rows, 256), jnp.bfloat16),
        ],
        compiler_params=pltpu.CompilerParams(vmem_limit_bytes=40 * 1024 * 1024),
        name="both_blocks",
    )(tokens, *operands)


def pair_bias(window_bias, last):
    heads = window_bias.shape[0]
    split = window_bias.reshape(heads, 8, 8, 8, 8).transpose(0, 4, 3, 2, 1).reshape(heads, 64, 64) * LOG2E
    index = jnp.arange(64, dtype=jnp.int32)
    column_side = (index // 8 < 4).astype(jnp.int32)
    row_side = (index % 8 < 4).astype(jnp.int32)
    column_cut = (column_side[:, None] != column_side[None, :]) & last
    row_cut = row_side[:, None] != row_side[None, :]
    plain = jnp.where(column_cut[None], -jnp.inf, split)
    cut = jnp.where(row_cut[None], -jnp.inf, plain)
    one = jnp.concatenate([plain, plain], axis=2).reshape(heads * 64, 128)
    two = jnp.concatenate([plain, cut], axis=2).reshape(heads * 64, 128)
    return jnp.stack([one, two])


def folded(gain, matrix, scale):
    return (gain[:, None] * matrix.astype(jnp.float32) * scale).T.astype(jnp.bfloat16)


def window_body(volume, norm_gains, qkv_weight, out_weight, up_weight, down_weight, window_bias):
    rows = volume.shape[1]
    width = volume.shape[2]
    channels = norm_gains.shape[1]
    heads = window_bias.shape[0]
    planes = lax.axis_size("gz")
    windows = width // channels // 8
    position = lax.axis_index("gz") * lax.axis_size("tile") + lax.axis_index("tile")
    packed = pack(volume.reshape(rows, width), windows, channels)
    tokens = lax.all_to_all(packed, ("gz", "tile"), split_axis=0, concat_axis=0, tiled=True)
    bias = pair_bias(window_bias, position == windows - 1)
    is_query = jnp.arange(3 * channels, dtype=jnp.int32) < channels
    scale = jnp.where(is_query, LOG2E * (channels // heads) ** (-0.5), 1.0)[None, :]
    qkv = jnp.stack([folded(norm_gains[0], qkv_weight[0], scale), folded(norm_gains[2], qkv_weight[1], scale)])
    up = jnp.stack([folded(norm_gains[1], up_weight[0], GELU_IN), folded(norm_gains[3], up_weight[1], GELU_IN)])
    out = out_weight[0].T
    mix = jnp.tile(out_weight[1].T, (1, planes))
    down = (jnp.transpose(down_weight, (0, 2, 1)).astype(jnp.float32) * GELU_OUT).astype(jnp.bfloat16)
    row = jnp.arange(heads * planes, dtype=jnp.int32)[:, None]
    column = jnp.arange(planes * channels, dtype=jnp.int32)[None, :]
    gather = (
        (row // planes == column % channels // (channels // heads)) & (row % planes == column // channels)
    ).astype(jnp.bfloat16)
    mixed = blocks(tokens, bias, qkv, out, mix, up, down, gather)
    returned = lax.all_to_all(mixed, ("gz", "tile"), split_axis=0, concat_axis=0, tiled=True)
    return unpack(returned, rows, width).reshape(1, rows, width)


def fits_windows(mesh, volume, norm_gains, window_bias):
    planes, tiles = mesh.shape["gz"], mesh.shape["tile"]
    channels, heads = norm_gains.shape[1], window_bias.shape[0]
    return (
        tiles == 2
        and planes == 8
        and volume.shape[1] == 16 * tiles
        and volume.shape[2] == 8 * channels * planes * tiles
        and channels == 96
        and heads == 3
    )


def solution(mesh):
    placed = (P(("groups", "gz"), "tile", None), P(), P(), P(), P(), P(), P())

    def run(volume, norm_gains, *weights):
        chosen = window_body if fits_windows(mesh, volume, norm_gains, weights[-1]) else general_body
        return jax.shard_map(
            chosen,
            mesh=mesh,
            in_specs=placed,
            out_specs=P(("groups", "gz"), "tile", None),
            check_vma=False,
        )(volume, norm_gains, *weights)

    return run
```

```python
import jax
import jax.numpy as jnp
import numpy as np
from jax import lax
from jax.experimental import pallas as pl
from jax.experimental.pallas import tpu as pltpu
from jax.sharding import PartitionSpec as P

epsilon = 1e-05


def shifted(array, axis, by):
    peers = lax.axis_size(axis)
    return lax.ppermute(array, axis, [(i, (i + by) % peers) for i in range(peers)])


def layer_norm(tokens, gain):
    values = tokens.astype(jnp.float32)
    average = jnp.mean(values, -1, keepdims=True)
    centered = values - average
    variance = jnp.mean(centered * centered, -1, keepdims=True)
    return (centered * lax.rsqrt(variance + epsilon) * gain).astype(jnp.bfloat16)


def feed_forward(tokens, gain, up_matrix, down_matrix):
    normed = layer_norm(tokens, gain)
    hidden = jax.nn.gelu(jnp.dot(normed, up_matrix, preferred_element_type=jnp.float32)).astype(
        jnp.bfloat16
    )
    total = tokens.astype(jnp.float32) + jnp.dot(
        hidden, down_matrix, preferred_element_type=jnp.float32
    )
    return total.astype(jnp.bfloat16)


def edge_label(index, extent):
    return jnp.where(index < 4, 2, jnp.where(index >= extent - 4, 1, 0)).astype(jnp.int32)


def head_masks(heads, channels):
    owner = jnp.arange(channels, dtype=jnp.int32) // (channels // heads)
    return (owner[None, :] == jnp.arange(heads, dtype=jnp.int32)[:, None]).astype(jnp.bfloat16)


def window_attention(
    row_block, first_row, height, channels, norm_gains, qkv_weight, out_weight, window_bias
):
    count = row_block.shape[0]
    columns = row_block.shape[1] // channels
    heads = window_bias.shape[0]
    head_size = channels // heads
    masks = head_masks(heads, channels)
    rolled = jnp.roll(row_block, -4 * channels, axis=1)
    windowed = rolled.reshape(count // 8, 8, columns // 8, 8 * channels).transpose(0, 2, 1, 3)
    normed = layer_norm(windowed.reshape(-1, channels), norm_gains[0])
    packed = jnp.dot(normed, qkv_weight[0], preferred_element_type=jnp.float32).astype(jnp.bfloat16)
    packed = packed.reshape(-1, 64, 3 * channels)
    queries = packed[:, :, :channels]
    keys = packed[:, :, channels : 2 * channels]
    values = packed[:, :, 2 * channels :]
    initial_rows = jnp.mod(first_row + jnp.arange(count, dtype=jnp.int32), height)
    initial_columns = jnp.mod(jnp.arange(columns, dtype=jnp.int32) + 4, columns)
    labels = (
        edge_label(initial_rows, height)[:, None] * 3
        + edge_label(initial_columns, columns)[None, :]
    )
    window_labels = (
        labels.reshape(count // 8, 8, columns // 8, 8).transpose(0, 2, 1, 3).reshape(-1, 64)
    )
    allowed = window_labels[:, :, None] == window_labels[:, None, :]
    head_queries = queries[:, None] * masks[None, :, None, :]
    scores = jnp.einsum("nhqc,nkc->nhqk", head_queries, keys, preferred_element_type=jnp.float32)
    scores = scores * head_size ** (-0.5) + window_bias[None]
    scores = jnp.where(allowed[:, None], scores, -jnp.inf)
    weights = jax.nn.softmax(scores, axis=-1).astype(jnp.bfloat16)
    head_values = values[:, None] * masks[None, :, None, :]
    attended = jnp.einsum(
        "nhqk,nhkc->nqc", weights, head_values, preferred_element_type=jnp.float32
    ).astype(jnp.bfloat16)
    lateral = jnp.dot(
        attended.reshape(-1, channels), out_weight[0], preferred_element_type=jnp.float32
    ).astype(jnp.bfloat16)
    lateral = lateral.reshape(count // 8, columns // 8, 8, 8 * channels).transpose(0, 2, 1, 3)
    return jnp.roll(lateral.reshape(count, columns * channels), 4 * channels, axis=1)


def axial_block(pencils, norm_gains, qkv_weight, out_weight, up_weight, down_weight, heads):
    planes, count, channels = pencils.shape
    head_size = channels // heads
    masks = head_masks(heads, channels)
    flat = jnp.transpose(pencils, (1, 0, 2)).reshape(-1, channels)
    normed = layer_norm(flat, norm_gains[2])
    packed = jnp.dot(normed, qkv_weight[1], preferred_element_type=jnp.float32).astype(jnp.bfloat16)
    packed = packed.reshape(count, planes, 3 * channels)
    queries = packed[:, :, :channels]
    keys = packed[:, :, channels : 2 * channels]
    values = packed[:, :, 2 * channels :]
    head_queries = queries[:, None] * masks[None, :, None, :]
    scores = jnp.einsum("phzc,pyc->phzy", head_queries, keys, preferred_element_type=jnp.float32)
    weights = jax.nn.softmax(scores * head_size ** (-0.5), axis=-1).astype(jnp.bfloat16)
    head_values = values[:, None] * masks[None, :, None, :]
    attended = jnp.einsum(
        "phzy,phyc->pzc", weights, head_values, preferred_element_type=jnp.float32
    ).astype(jnp.bfloat16)
    projected = jnp.dot(
        attended.reshape(-1, channels), out_weight[1], preferred_element_type=jnp.float32
    ).astype(jnp.bfloat16)
    after = (flat.astype(jnp.float32) + projected.astype(jnp.float32)).astype(jnp.bfloat16)
    mixed = feed_forward(after, norm_gains[3], up_weight[1], down_weight[1]).reshape(
        count, planes, channels
    )
    return jnp.transpose(mixed, (1, 0, 2))


def general_body(volume, norm_gains, qkv_weight, out_weight, up_weight, down_weight, window_bias):
    rows_here = volume.shape[1]
    row_width = volume.shape[2]
    channels = norm_gains.shape[1]
    heads = window_bias.shape[0]
    height = rows_here * lax.axis_size("tile")
    tile_start = lax.axis_index("tile") * rows_here
    plane = volume.reshape(rows_here, row_width)
    next_rows = shifted(plane[:4], "tile", -1)
    extended = jnp.concatenate([plane[4:], next_rows], 0)
    attended = window_attention(
        extended, tile_start + 4, height, channels, norm_gains, qkv_weight, out_weight, window_bias
    )
    tail_rows = shifted(attended[-4:], "tile", 1)
    lateral = jnp.concatenate([tail_rows, attended[:-4]], 0)
    middle = (
        (plane.astype(jnp.float32) + lateral.astype(jnp.float32))
        .astype(jnp.bfloat16)
        .reshape(-1, channels)
    )
    planes = lax.axis_size("gz")
    middle = feed_forward(middle, norm_gains[1], up_weight[0], down_weight[0])
    grouped = middle.reshape(planes, -1, channels)
    pencils = lax.all_to_all(grouped, "gz", split_axis=0, concat_axis=0, tiled=True)
    returned = lax.all_to_all(
        axial_block(pencils, norm_gains, qkv_weight, out_weight, up_weight, down_weight, heads),
        "gz",
        split_axis=0,
        concat_axis=0,
        tiled=True,
    )
    return returned.reshape(1, rows_here, row_width)


LOG2E = 1.4426950408889634


def normalised(tokens):
    average = jnp.mean(tokens, 0, keepdims=True)
    centered = tokens - average
    variance = jnp.mean(centered * centered, 0, keepdims=True)
    return (centered * lax.rsqrt(variance + epsilon)).astype(jnp.bfloat16)


def product(left, right):
    return jnp.dot(left, right, preferred_element_type=jnp.float32)


GELU_IN = 0.035677408136300125 ** (1 / 3)
GELU_LINEAR = 0.7978845608028654 / GELU_IN
GELU_OUT = 0.5 / GELU_IN


def across(left, right):
    return lax.dot_general(left, right, (((1,), (1,)), ((), ())), preferred_element_type=jnp.float32)


def gated(scaled):
    scaled = scaled.astype(jnp.bfloat16)
    return scaled + scaled * jnp.tanh(scaled * (GELU_LINEAR + scaled * scaled))


def pack_kernel(volume_ref, packed_ref):
    windows, channels, _ = packed_ref.shape
    width = 8 * channels
    half = width // 2
    for window in range(windows):
        start = window * width + half
        if window < windows - 1:
            chunk = volume_ref[:, start : start + width]
        else:
            chunk = jnp.concatenate([volume_ref[:, start:], volume_ref[:, :half]], axis=1)
        chunk = chunk.astype(jnp.float32)
        rolled = jnp.concatenate([chunk[4:], chunk[:4]], axis=0)
        pieces = [
            rolled[8 * part : 8 * part + 8, channels * column : channels * (column + 1)]
            for part in range(2)
            for column in range(8)
        ]
        tokens = jnp.concatenate(pieces, axis=0)
        packed_ref[window] = tokens.T.astype(jnp.bfloat16)


def unpack_kernel(packed_ref, volume_ref):
    windows, channels, _ = packed_ref.shape
    width = 8 * channels
    half = width // 2
    for window in range(windows):
        tokens = packed_ref[window].astype(jnp.float32).T
        parts = [
            jnp.concatenate(
                [tokens[64 * part + 8 * column : 64 * part + 8 * column + 8] for column in range(8)], axis=1
            )
            for part in range(2)
        ]
        rows = jnp.concatenate([parts[1][4:], parts[0], parts[1][:4]], axis=0).astype(jnp.bfloat16)
        start = window * width + half
        if window < windows - 1:
            volume_ref[:, start : start + width] = rows
        else:
            volume_ref[:, start:] = rows[:, :half]
            volume_ref[:, :half] = rows[:, half:]


def in_lockstep(stages, planes):
    for stage in stages:
        for plane in range(planes):
            stage(plane)


def blocks_kernel(
    tokens_ref,
    gains_ref,
    qkv_weight_ref,
    out_weight_ref,
    up_weight_ref,
    down_weight_ref,
    window_bias_ref,
    order_ref,
    placed_order_ref,
    gather_ref,
    result_ref,
    bias_ref,
    planar_ref,
    query_ref,
    key_ref,
    value_ref,
):
    channels = tokens_ref.shape[1]
    planes = tokens_ref.shape[0] // 2
    heads = window_bias_ref.shape[0] // 64
    head_size = channels // heads
    lane = lax.broadcasted_iota(jnp.int32, (1, 128), 1)
    own = (lane < 64) | (lane % 8 < 4)
    first = lane < 64
    blank = jnp.zeros((128 - channels, 128), jnp.bfloat16)
    blank_rows = jnp.zeros((128 - channels, 128), jnp.float32)

    def turned(ref, layer):
        return ref[layer].astype(jnp.float32).T

    def gain(norm, scale):
        return gains_ref[norm : norm + 1, :] * scale

    def turned_qkv(layer):
        matrix = turned(qkv_weight_ref, layer)
        queries = matrix[:channels] * gain(2 * layer, LOG2E * head_size ** (-0.5))
        return jnp.concatenate([queries, matrix[channels:] * gain(2 * layer, 1.0)], axis=0).astype(jnp.bfloat16)

    qkv = [turned_qkv(layer) for layer in range(2)]
    up = [(turned(up_weight_ref, layer) * gain(2 * layer + 1, GELU_IN)).astype(jnp.bfloat16) for layer in range(2)]
    down = [(down_weight_ref[layer].astype(jnp.float32) * GELU_OUT).astype(jnp.bfloat16) for layer in range(2)]
    out = turned(out_weight_ref, 0).astype(jnp.bfloat16)
    mix = jnp.concatenate([turned(out_weight_ref, 1).astype(jnp.bfloat16)] * planes, axis=1)

    high = window_bias_ref[...].astype(jnp.bfloat16)
    low = (window_bias_ref[...] - high.astype(jnp.float32)).astype(jnp.bfloat16)
    parts = [across(order_ref[...], part).astype(jnp.bfloat16) for part in (high, low)]
    position = lax.axis_index("gz") * lax.axis_size("tile") + lax.axis_index("tile")
    last = position == lax.axis_size("gz") * lax.axis_size("tile") - 1
    key_row = lax.broadcasted_iota(jnp.int32, (64, 128), 0)
    query_lane = lax.broadcasted_iota(jnp.int32, (64, 128), 1)
    column_cut = ((key_row < 32) != (query_lane % 64 < 32)) & last
    row_cut = ((key_row % 8 < 4) != (query_lane % 8 < 4)) & (query_lane >= 64)
    for head in range(heads):
        placed = placed_order_ref[128 * head : 128 * (head + 1), :]
        plain = (across(parts[0], placed) + across(parts[1], placed)) * LOG2E
        plain = jnp.where(column_cut, -jnp.inf, plain)
        bias_ref[0, 64 * head : 64 * (head + 1), :] = plain
        bias_ref[1, 64 * head : 64 * (head + 1), :] = jnp.where(row_cut, -jnp.inf, plain)

    held = [{} for _ in range(planes)]

    def rows_of(plane):
        return slice(plane * channels, (plane + 1) * channels)

    def load(plane):
        one, two = tokens_ref[2 * plane], tokens_ref[2 * plane + 1]
        tokens = jnp.concatenate([jnp.where(own, one, two), jnp.where(own, two, one)], axis=1)
        held[plane]["x"] = tokens.astype(jnp.float32)

    def norm(plane):
        held[plane]["n"] = normalised(held[plane]["x"])

    def lateral_qkv(plane):
        packed = product(qkv[0], held[plane].pop("n"))
        held[plane]["q"] = packed[:channels]
        held[plane]["k"] = packed[channels : 2 * channels]
        held[plane]["v"] = packed[2 * channels :].astype(jnp.bfloat16)

    def lateral_scores(plane):
        queries, keys = held[plane].pop("q"), held[plane].pop("k")
        scores = []
        for pair in range(2):
            lanes = slice(128 * pair, 128 * pair + 128)
            query = queries[:, lanes]
            right = jnp.concatenate(
                [
                    jnp.where(first, query, 0.0).astype(jnp.bfloat16),
                    blank,
                    jnp.where(first, 0.0, query).astype(jnp.bfloat16),
                    blank,
                ],
                axis=0,
            )
            key = jnp.concatenate([keys[:, lanes], blank_rows], axis=0).T
            left = []
            for head in range(heads):
                masked = jnp.where(lane // head_size == head, key, 0.0).astype(jnp.bfloat16)
                left.append(jnp.concatenate([masked[:64], masked[64:]], axis=1))
            scores.append(product(jnp.concatenate(left, axis=0), right) + bias_ref[pair])
        held[plane]["s"] = scores

    def lateral_weights(plane):
        scores = held[plane].pop("s")
        held[plane]["w"] = []
        for pair in range(2):
            for head in range(heads):
                own_scores = scores[pair][64 * head : 64 * head + 64]
                weights = jnp.exp2(own_scores - jnp.max(own_scores, axis=0, keepdims=True))
                total = jnp.sum(weights, axis=0, keepdims=True)
                spread = jnp.concatenate(
                    [
                        jnp.where(first, weights, 0.0).astype(jnp.bfloat16),
                        jnp.where(first, 0.0, weights).astype(jnp.bfloat16),
                    ],
                    axis=0,
                )
                held[plane]["w"].append((spread, 1.0 / total))

    def lateral_values(plane):
        weights, values = held[plane].pop("w"), held[plane].pop("v")
        attended = []
        for pair in range(2):
            lanes = slice(128 * pair, 128 * pair + 128)
            mixed = []
            for head in range(heads):
                spread, inverse = weights[heads * pair + head]
                own_mixed = product(values[head_size * head : head_size * (head + 1), lanes], spread)
                mixed.append((own_mixed * inverse).astype(jnp.bfloat16))
            attended.append(jnp.concatenate(mixed, axis=0))
        held[plane]["a"] = jnp.concatenate(attended, axis=1)

    def lateral_out(plane):
        held[plane]["x"] = held[plane]["x"] + product(out, held[plane].pop("a"))

    def raised(layer):
        def stage(plane):
            held[plane]["h"] = product(up[layer], held[plane].pop("n"))

        return stage

    def gelu(plane):
        held[plane]["g"] = gated(held[plane].pop("h"))

    def lowered(layer):
        def stage(plane):
            held[plane]["x"] = held[plane]["x"] + product(down[layer], held[plane].pop("g"))

        return stage

    def axial_qkv(plane):
        packed = product(qkv[1], held[plane].pop("n")).astype(jnp.bfloat16)
        planar_ref[rows_of(plane), :] = held[plane].pop("x")
        query_ref[rows_of(plane), :] = packed[:channels]
        key_ref[rows_of(plane), :] = packed[channels : 2 * channels]
        value_ref[rows_of(plane), :] = packed[2 * channels :]

    def axial_scores(plane):
        query = query_ref[rows_of(plane), :]
        pairs = jnp.concatenate([query * key_ref[rows_of(other), :] for other in range(planes)], axis=0)
        held[plane]["s"] = product(gather_ref[...], pairs)

    def axial_weights(plane):
        scores = held[plane].pop("s")
        weights = []
        for head in range(heads):
            own_scores = scores[planes * head : planes * (head + 1)]
            own_weights = jnp.exp2(own_scores - jnp.max(own_scores, axis=0, keepdims=True))
            weights.append(own_weights * (1.0 / jnp.sum(own_weights, axis=0, keepdims=True)))
        held[plane]["w"] = weights

    def axial_values(plane):
        weights = held[plane].pop("w")
        spread = []
        for other in range(planes):
            wide = jnp.concatenate(
                [
                    jnp.broadcast_to(weights[head][other : other + 1], (head_size, 256)).astype(jnp.bfloat16)
                    for head in range(heads)
                ],
                axis=0,
            )
            spread.append(wide * value_ref[rows_of(other), :])
        held[plane]["x"] = planar_ref[rows_of(plane), :] + product(mix, jnp.concatenate(spread, axis=0))

    def store(plane):
        mixed = held[plane].pop("x").astype(jnp.bfloat16)
        one, two = mixed[:, :128], mixed[:, 128:]
        result_ref[2 * plane] = jnp.where(own, one, two)
        result_ref[2 * plane + 1] = jnp.where(own, two, one)

    lateral = [load, norm, lateral_qkv, lateral_scores, lateral_weights, lateral_values, lateral_out]
    lateral += [norm, raised(0), gelu, lowered(0), norm, axial_qkv]
    axial = [axial_scores, axial_weights, axial_values, norm, raised(1), gelu, lowered(1), store]
    in_lockstep(lateral + axial, planes)


def pack(rows, windows, channels):
    return pl.pallas_call(
        pack_kernel,
        out_shape=jax.ShapeDtypeStruct((windows, channels, 128), jnp.bfloat16),
        compiler_params=pltpu.CompilerParams(vmem_limit_bytes=16 * 1024 * 1024),
        name="pack_windows",
    )(rows)


def unpack(packed, rows, width):
    return pl.pallas_call(
        unpack_kernel,
        out_shape=jax.ShapeDtypeStruct((rows, width), jnp.bfloat16),
        compiler_params=pltpu.CompilerParams(vmem_limit_bytes=16 * 1024 * 1024),
        name="unpack_windows",
    )(packed)


def blocks(tokens, *operands):
    sources, channels, _ = tokens.shape
    rows = sources // 2 * channels
    heads = operands[5].shape[0] // 64
    return pl.pallas_call(
        blocks_kernel,
        out_shape=jax.ShapeDtypeStruct(tokens.shape, jnp.bfloat16),
        scratch_shapes=[
            pltpu.VMEM((2, heads * 64, 128), jnp.float32),
            pltpu.VMEM((rows, 256), jnp.float32),
            pltpu.VMEM((rows, 256), jnp.bfloat16),
            pltpu.VMEM((rows, 256), jnp.bfloat16),
            pltpu.VMEM((rows, 256), jnp.bfloat16),
        ],
        compiler_params=pltpu.CompilerParams(vmem_limit_bytes=40 * 1024 * 1024),
        name="both_blocks",
    )(tokens, *operands)


def constants(heads, channels, planes):
    order = np.zeros((64, 64), np.float32)
    index = np.arange(64)
    order[index, index % 8 * 8 + index // 8] = 1.0
    placed = np.zeros((heads, 2, 64, heads, 64), np.float32)
    for head in range(heads):
        placed[head, :, :, head, :] = order
    row = np.arange(heads * planes)[:, None]
    column = np.arange(planes * channels)[None, :]
    gather = (row // planes == column % channels // (channels // heads)) & (row % planes == column // channels)
    placed = placed.reshape(heads * 128, heads * 64)
    return order.astype(jnp.bfloat16), placed.astype(jnp.bfloat16), gather.astype(jnp.bfloat16)


def window_body(volume, norm_gains, qkv_weight, out_weight, up_weight, down_weight, window_bias):
    rows = volume.shape[1]
    width = volume.shape[2]
    channels = norm_gains.shape[1]
    heads = window_bias.shape[0]
    planes = lax.axis_size("gz")
    windows = width // channels // 8
    packed = pack(volume.reshape(rows, width), windows, channels)
    tokens = lax.all_to_all(packed, ("gz", "tile"), split_axis=0, concat_axis=0, tiled=True)
    order, placed_order, gather = constants(heads, channels, planes)
    mixed = blocks(
        tokens,
        norm_gains,
        qkv_weight,
        out_weight,
        up_weight,
        jnp.transpose(down_weight, (0, 2, 1)),
        window_bias.reshape(heads * 64, 64),
        order,
        placed_order,
        gather,
    )
    returned = lax.all_to_all(mixed, ("gz", "tile"), split_axis=0, concat_axis=0, tiled=True)
    return unpack(returned, rows, width).reshape(1, rows, width)


def fits_windows(mesh, volume, norm_gains, window_bias):
    planes, tiles = mesh.shape["gz"], mesh.shape["tile"]
    channels, heads = norm_gains.shape[1], window_bias.shape[0]
    return (
        tiles == 2
        and planes == 8
        and volume.shape[1] == 16 * tiles
        and volume.shape[2] == 8 * channels * planes * tiles
        and channels == 96
        and heads == 3
    )


def solution(mesh):
    placed = (P(("groups", "gz"), "tile", None), P(), P(), P(), P(), P(), P())

    def run(volume, norm_gains, *weights):
        chosen = window_body if fits_windows(mesh, volume, norm_gains, weights[-1]) else general_body
        return jax.shard_map(
            chosen,
            mesh=mesh,
            in_specs=placed,
            out_specs=P(("groups", "gz"), "tile", None),
            check_vma=False,
        )(volume, norm_gains, *weights)

    return run
```

```python
import jax
import jax.numpy as jnp
import numpy as np
from jax import lax
from jax.experimental import pallas as pl
from jax.experimental.pallas import tpu as pltpu
from jax.sharding import PartitionSpec as P

epsilon = 1e-05


def shifted(array, axis, by):
    peers = lax.axis_size(axis)
    return lax.ppermute(array, axis, [(i, (i + by) % peers) for i in range(peers)])


def layer_norm(tokens, gain):
    values = tokens.astype(jnp.float32)
    average = jnp.mean(values, -1, keepdims=True)
    centered = values - average
    variance = jnp.mean(centered * centered, -1, keepdims=True)
    return (centered * lax.rsqrt(variance + epsilon) * gain).astype(jnp.bfloat16)


def feed_forward(tokens, gain, up_matrix, down_matrix):
    normed = layer_norm(tokens, gain)
    hidden = jax.nn.gelu(jnp.dot(normed, up_matrix, preferred_element_type=jnp.float32)).astype(
        jnp.bfloat16
    )
    total = tokens.astype(jnp.float32) + jnp.dot(
        hidden, down_matrix, preferred_element_type=jnp.float32
    )
    return total.astype(jnp.bfloat16)


def edge_label(index, extent):
    return jnp.where(index < 4, 2, jnp.where(index >= extent - 4, 1, 0)).astype(jnp.int32)


def head_masks(heads, channels):
    owner = jnp.arange(channels, dtype=jnp.int32) // (channels // heads)
    return (owner[None, :] == jnp.arange(heads, dtype=jnp.int32)[:, None]).astype(jnp.bfloat16)


def window_attention(
    row_block, first_row, height, channels, norm_gains, qkv_weight, out_weight, window_bias
):
    count = row_block.shape[0]
    columns = row_block.shape[1] // channels
    heads = window_bias.shape[0]
    head_size = channels // heads
    masks = head_masks(heads, channels)
    rolled = jnp.roll(row_block, -4 * channels, axis=1)
    windowed = rolled.reshape(count // 8, 8, columns // 8, 8 * channels).transpose(0, 2, 1, 3)
    normed = layer_norm(windowed.reshape(-1, channels), norm_gains[0])
    packed = jnp.dot(normed, qkv_weight[0], preferred_element_type=jnp.float32).astype(jnp.bfloat16)
    packed = packed.reshape(-1, 64, 3 * channels)
    queries = packed[:, :, :channels]
    keys = packed[:, :, channels : 2 * channels]
    values = packed[:, :, 2 * channels :]
    initial_rows = jnp.mod(first_row + jnp.arange(count, dtype=jnp.int32), height)
    initial_columns = jnp.mod(jnp.arange(columns, dtype=jnp.int32) + 4, columns)
    labels = (
        edge_label(initial_rows, height)[:, None] * 3
        + edge_label(initial_columns, columns)[None, :]
    )
    window_labels = (
        labels.reshape(count // 8, 8, columns // 8, 8).transpose(0, 2, 1, 3).reshape(-1, 64)
    )
    allowed = window_labels[:, :, None] == window_labels[:, None, :]
    head_queries = queries[:, None] * masks[None, :, None, :]
    scores = jnp.einsum("nhqc,nkc->nhqk", head_queries, keys, preferred_element_type=jnp.float32)
    scores = scores * head_size ** (-0.5) + window_bias[None]
    scores = jnp.where(allowed[:, None], scores, -jnp.inf)
    weights = jax.nn.softmax(scores, axis=-1).astype(jnp.bfloat16)
    head_values = values[:, None] * masks[None, :, None, :]
    attended = jnp.einsum(
        "nhqk,nhkc->nqc", weights, head_values, preferred_element_type=jnp.float32
    ).astype(jnp.bfloat16)
    lateral = jnp.dot(
        attended.reshape(-1, channels), out_weight[0], preferred_element_type=jnp.float32
    ).astype(jnp.bfloat16)
    lateral = lateral.reshape(count // 8, columns // 8, 8, 8 * channels).transpose(0, 2, 1, 3)
    return jnp.roll(lateral.reshape(count, columns * channels), 4 * channels, axis=1)


def axial_block(pencils, norm_gains, qkv_weight, out_weight, up_weight, down_weight, heads):
    planes, count, channels = pencils.shape
    head_size = channels // heads
    masks = head_masks(heads, channels)
    flat = jnp.transpose(pencils, (1, 0, 2)).reshape(-1, channels)
    normed = layer_norm(flat, norm_gains[2])
    packed = jnp.dot(normed, qkv_weight[1], preferred_element_type=jnp.float32).astype(jnp.bfloat16)
    packed = packed.reshape(count, planes, 3 * channels)
    queries = packed[:, :, :channels]
    keys = packed[:, :, channels : 2 * channels]
    values = packed[:, :, 2 * channels :]
    head_queries = queries[:, None] * masks[None, :, None, :]
    scores = jnp.einsum("phzc,pyc->phzy", head_queries, keys, preferred_element_type=jnp.float32)
    weights = jax.nn.softmax(scores * head_size ** (-0.5), axis=-1).astype(jnp.bfloat16)
    head_values = values[:, None] * masks[None, :, None, :]
    attended = jnp.einsum(
        "phzy,phyc->pzc", weights, head_values, preferred_element_type=jnp.float32
    ).astype(jnp.bfloat16)
    projected = jnp.dot(
        attended.reshape(-1, channels), out_weight[1], preferred_element_type=jnp.float32
    ).astype(jnp.bfloat16)
    after = (flat.astype(jnp.float32) + projected.astype(jnp.float32)).astype(jnp.bfloat16)
    mixed = feed_forward(after, norm_gains[3], up_weight[1], down_weight[1]).reshape(
        count, planes, channels
    )
    return jnp.transpose(mixed, (1, 0, 2))


def general_body(volume, norm_gains, qkv_weight, out_weight, up_weight, down_weight, window_bias):
    rows_here = volume.shape[1]
    row_width = volume.shape[2]
    channels = norm_gains.shape[1]
    heads = window_bias.shape[0]
    height = rows_here * lax.axis_size("tile")
    tile_start = lax.axis_index("tile") * rows_here
    plane = volume.reshape(rows_here, row_width)
    next_rows = shifted(plane[:4], "tile", -1)
    extended = jnp.concatenate([plane[4:], next_rows], 0)
    attended = window_attention(
        extended, tile_start + 4, height, channels, norm_gains, qkv_weight, out_weight, window_bias
    )
    tail_rows = shifted(attended[-4:], "tile", 1)
    lateral = jnp.concatenate([tail_rows, attended[:-4]], 0)
    middle = (
        (plane.astype(jnp.float32) + lateral.astype(jnp.float32))
        .astype(jnp.bfloat16)
        .reshape(-1, channels)
    )
    planes = lax.axis_size("gz")
    middle = feed_forward(middle, norm_gains[1], up_weight[0], down_weight[0])
    grouped = middle.reshape(planes, -1, channels)
    pencils = lax.all_to_all(grouped, "gz", split_axis=0, concat_axis=0, tiled=True)
    returned = lax.all_to_all(
        axial_block(pencils, norm_gains, qkv_weight, out_weight, up_weight, down_weight, heads),
        "gz",
        split_axis=0,
        concat_axis=0,
        tiled=True,
    )
    return returned.reshape(1, rows_here, row_width)


LOG2E = 1.4426950408889634


def normalised(tokens):
    average = jnp.mean(tokens, 0, keepdims=True)
    centered = tokens - average
    variance = jnp.mean(centered * centered, 0, keepdims=True)
    return (centered * lax.rsqrt(variance + epsilon)).astype(jnp.bfloat16)


def product(left, right):
    return jnp.dot(left, right, preferred_element_type=jnp.float32)


GELU_IN = 0.035677408136300125 ** (1 / 3)
GELU_LINEAR = 0.7978845608028654 / GELU_IN
GELU_OUT = 0.5 / GELU_IN


def across(left, right):
    return lax.dot_general(left, right, (((1,), (1,)), ((), ())), preferred_element_type=jnp.float32)


def gated(scaled):
    scaled = scaled.astype(jnp.bfloat16)
    return scaled + scaled * jnp.tanh(scaled * (GELU_LINEAR + scaled * scaled))


def pack_kernel(volume_ref, packed_ref):
    windows, channels, _ = packed_ref.shape
    width = 8 * channels
    half = width // 2
    for window in range(windows):
        start = window * width + half
        if window < windows - 1:
            chunk = volume_ref[:, start : start + width]
        else:
            chunk = jnp.concatenate([volume_ref[:, start:], volume_ref[:, :half]], axis=1)
        chunk = chunk.astype(jnp.float32)
        rolled = jnp.concatenate([chunk[4:], chunk[:4]], axis=0)
        pieces = [
            rolled[8 * part : 8 * part + 8, channels * column : channels * (column + 1)]
            for part in range(2)
            for column in range(8)
        ]
        tokens = jnp.concatenate(pieces, axis=0)
        packed_ref[window] = tokens.T.astype(jnp.bfloat16)


def unpack_kernel(packed_ref, volume_ref):
    windows, channels, _ = packed_ref.shape
    width = 8 * channels
    half = width // 2
    for window in range(windows):
        tokens = packed_ref[window].astype(jnp.float32).T
        parts = [
            jnp.concatenate(
                [tokens[64 * part + 8 * column : 64 * part + 8 * column + 8] for column in range(8)], axis=1
            )
            for part in range(2)
        ]
        rows = jnp.concatenate([parts[1][4:], parts[0], parts[1][:4]], axis=0).astype(jnp.bfloat16)
        start = window * width + half
        if window < windows - 1:
            volume_ref[:, start : start + width] = rows
        else:
            volume_ref[:, start:] = rows[:, :half]
            volume_ref[:, :half] = rows[:, half:]


def in_lockstep(stages, planes):
    for stage in stages:
        for plane in range(planes):
            stage(plane)


def blocks_kernel(
    tokens_ref,
    gains_ref,
    qkv_weight_ref,
    out_weight_ref,
    up_weight_ref,
    down_weight_ref,
    window_bias_ref,
    order_ref,
    result_ref,
    bias_ref,
    planar_ref,
    query_ref,
    key_ref,
    value_ref,
):
    channels = tokens_ref.shape[1]
    planes = tokens_ref.shape[0] // 2
    heads = window_bias_ref.shape[0] // 64
    head_size = channels // heads
    lane = lax.broadcasted_iota(jnp.int32, (1, 128), 1)
    own = (lane < 64) | (lane % 8 < 4)
    first = lane < 64
    blank = jnp.zeros((128 - channels, 128), jnp.bfloat16)
    blank_rows = jnp.zeros((128 - channels, 128), jnp.float32)

    def turned(ref, layer):
        return ref[layer].astype(jnp.float32).T

    def gain(norm, scale):
        return gains_ref[norm : norm + 1, :] * scale

    def turned_qkv(layer):
        matrix = turned(qkv_weight_ref, layer)
        queries = matrix[:channels] * gain(2 * layer, LOG2E * head_size ** (-0.5))
        return jnp.concatenate([queries, matrix[channels:] * gain(2 * layer, 1.0)], axis=0).astype(jnp.bfloat16)

    qkv = [turned_qkv(layer) for layer in range(2)]
    up = [(turned(up_weight_ref, layer) * gain(2 * layer + 1, GELU_IN)).astype(jnp.bfloat16) for layer in range(2)]
    down = [(down_weight_ref[layer].astype(jnp.float32) * GELU_OUT).astype(jnp.bfloat16) for layer in range(2)]
    out = turned(out_weight_ref, 0).astype(jnp.bfloat16)
    mix = jnp.concatenate([turned(out_weight_ref, 1).astype(jnp.bfloat16)] * 2, axis=1)

    shape = (heads * planes, planes * channels // 2)
    row = lax.broadcasted_iota(jnp.int32, shape, 0)
    column = lax.broadcasted_iota(jnp.int32, shape, 1)
    mine = lax.div(column, head_size // 2) == lax.rem(row, planes) * heads + lax.div(row, planes)
    gather = jnp.where(mine, 1.0, 0.0).astype(jnp.bfloat16)

    high = window_bias_ref[...].astype(jnp.bfloat16)
    low = (window_bias_ref[...] - high.astype(jnp.float32)).astype(jnp.bfloat16)
    parts = [across(order_ref[:64, :64], part).astype(jnp.bfloat16) for part in (high, low)]
    position = lax.axis_index("gz") * lax.axis_size("tile") + lax.axis_index("tile")
    last = position == lax.axis_size("gz") * lax.axis_size("tile") - 1
    key_row = lax.broadcasted_iota(jnp.int32, (64, 128), 0)
    query_lane = lax.broadcasted_iota(jnp.int32, (64, 128), 1)
    column_cut = ((key_row < 32) != (query_lane % 64 < 32)) & last
    row_cut = ((key_row % 8 < 4) != (query_lane % 8 < 4)) & (query_lane >= 64)
    for head in range(heads):
        placed = order_ref[128 * head : 128 * (head + 1), :]
        plain = (across(parts[0], placed) + across(parts[1], placed)) * LOG2E
        plain = jnp.where(column_cut, -jnp.inf, plain)
        bias_ref[0, 64 * head : 64 * (head + 1), :] = plain
        bias_ref[1, 64 * head : 64 * (head + 1), :] = jnp.where(row_cut, -jnp.inf, plain)

    held = [{} for _ in range(planes)]

    def rows_of(plane):
        return slice(plane * channels, (plane + 1) * channels)

    def load(plane):
        one, two = tokens_ref[2 * plane], tokens_ref[2 * plane + 1]
        tokens = jnp.concatenate([jnp.where(own, one, two), jnp.where(own, two, one)], axis=1)
        held[plane]["x"] = tokens.astype(jnp.float32)

    def norm(plane):
        held[plane]["n"] = normalised(held[plane]["x"])

    def lateral_qkv(plane):
        packed = product(qkv[0], held[plane].pop("n"))
        held[plane]["q"] = packed[:channels]
        held[plane]["k"] = packed[channels : 2 * channels]
        held[plane]["v"] = packed[2 * channels :].astype(jnp.bfloat16)

    def lateral_scores(plane):
        queries, keys = held[plane].pop("q"), held[plane].pop("k")
        scores = []
        for pair in range(2):
            lanes = slice(128 * pair, 128 * pair + 128)
            query = queries[:, lanes]
            right = jnp.concatenate(
                [
                    jnp.where(first, query, 0.0).astype(jnp.bfloat16),
                    blank,
                    jnp.where(first, 0.0, query).astype(jnp.bfloat16),
                    blank,
                ],
                axis=0,
            )
            key = jnp.concatenate([keys[:, lanes], blank_rows], axis=0).T
            left = []
            for head in range(heads):
                masked = jnp.where(lane // head_size == head, key, 0.0).astype(jnp.bfloat16)
                left.append(jnp.concatenate([masked[:64], masked[64:]], axis=1))
            scores.append((jnp.concatenate(left, axis=0), right))
        held[plane]["s"] = scores

    def lateral_weights(plane):
        scores = held[plane].pop("s")
        held[plane]["w"] = []
        for pair in range(2):
            for head in range(heads):
                own_scores = scores[pair][64 * head : 64 * head + 64]
                weights = jnp.exp2(own_scores - jnp.max(own_scores, axis=0, keepdims=True))
                total = jnp.sum(weights, axis=0, keepdims=True)
                spread = jnp.concatenate(
                    [
                        jnp.where(first, weights, 0.0).astype(jnp.bfloat16),
                        jnp.where(first, 0.0, weights).astype(jnp.bfloat16),
                    ],
                    axis=0,
                )
                held[plane]["w"].append((spread, 1.0 / total))

    def lateral_products(plane):
        held[plane]["s"] = [product(*held[plane]["s"][pair]) + bias_ref[pair] for pair in range(2)]

    def lateral_values(plane):
        weights, values = held[plane].pop("w"), held[plane].pop("v")
        attended = []
        for pair in range(2):
            lanes = slice(128 * pair, 128 * pair + 128)
            mixed = []
            for head in range(heads):
                spread, inverse = weights[heads * pair + head]
                own_mixed = product(values[head_size * head : head_size * (head + 1), lanes], spread)
                mixed.append((own_mixed * inverse).astype(jnp.bfloat16))
            attended.append(jnp.concatenate(mixed, axis=0))
        held[plane]["a"] = jnp.concatenate(attended, axis=1)

    def lateral_out(plane):
        held[plane]["x"] = held[plane]["x"] + product(out, held[plane].pop("a"))

    def raised(layer):
        def stage(plane):
            held[plane]["h"] = product(up[layer], held[plane].pop("n"))

        return stage

    def gelu(plane):
        held[plane]["g"] = gated(held[plane].pop("h"))

    def lowered(layer):
        def stage(plane):
            held[plane]["x"] = held[plane]["x"] + product(down[layer], held[plane].pop("g"))

        return stage

    def axial_qkv(plane):
        packed = product(qkv[1], held[plane].pop("n")).astype(jnp.bfloat16)
        planar_ref[rows_of(plane), :] = held[plane].pop("x")
        query_ref[rows_of(plane), :] = packed[:channels]
        key_ref[rows_of(plane), :] = packed[channels : 2 * channels]
        value_ref[rows_of(plane), :] = packed[2 * channels :]

    def axial_scores(plane):
        query = query_ref[rows_of(plane), :]
        half = head_size // 2
        pairs = []
        for other in range(planes):
            pair = query * key_ref[rows_of(other), :]
            for head in range(heads):
                top = head_size * head
                pairs.append(pair[top : top + half] + pair[top + half : top + head_size])
        pairs = jnp.concatenate(pairs, axis=0)
        held[plane]["s"] = product(gather, pairs)

    def axial_weights(plane):
        scores = held[plane].pop("s")
        weights = []
        for head in range(heads):
            own_scores = scores[planes * head : planes * (head + 1)]
            own_weights = jnp.exp2(own_scores - jnp.max(own_scores, axis=0, keepdims=True))
            weights.append(own_weights * (1.0 / jnp.sum(own_weights, axis=0, keepdims=True)))
        held[plane]["w"] = weights

    def axial_values(plane):
        weights = held[plane].pop("w")
        spread = []
        for other in range(planes):
            wide = jnp.concatenate(
                [
                    jnp.broadcast_to(weights[head][other : other + 1], (head_size, 256)).astype(jnp.bfloat16)
                    for head in range(heads)
                ],
                axis=0,
            )
            spread.append(wide * value_ref[rows_of(other), :])
        while len(spread) > 2:
            spread = [one + two for one, two in zip(spread[::2], spread[1::2])]
        spread = jnp.concatenate(spread, axis=0)
        held[plane]["x"] = planar_ref[rows_of(plane), :] + product(mix, spread)

    def store(plane):
        mixed = held[plane].pop("x").astype(jnp.bfloat16)
        one, two = mixed[:, :128], mixed[:, 128:]
        result_ref[2 * plane] = jnp.where(own, one, two)
        result_ref[2 * plane + 1] = jnp.where(own, two, one)

    lateral = [load, norm, lateral_qkv, lateral_scores, lateral_products, lateral_weights, lateral_values, lateral_out]
    lateral += [norm, raised(0), gelu, lowered(0), norm, axial_qkv]
    axial = [axial_scores, axial_weights, axial_values, norm, raised(1), gelu, lowered(1), store]
    in_lockstep(lateral + axial, planes)


def pack(rows, windows, channels):
    return pl.pallas_call(
        pack_kernel,
        out_shape=jax.ShapeDtypeStruct((windows, channels, 128), jnp.bfloat16),
        compiler_params=pltpu.CompilerParams(vmem_limit_bytes=16 * 1024 * 1024),
        name="pack_windows",
    )(rows)


def unpack(packed, rows, width):
    return pl.pallas_call(
        unpack_kernel,
        out_shape=jax.ShapeDtypeStruct((rows, width), jnp.bfloat16),
        compiler_params=pltpu.CompilerParams(vmem_limit_bytes=16 * 1024 * 1024),
        name="unpack_windows",
    )(packed)


def blocks(tokens, *operands):
    sources, channels, _ = tokens.shape
    rows = sources // 2 * channels
    heads = operands[5].shape[0] // 64
    return pl.pallas_call(
        blocks_kernel,
        out_shape=jax.ShapeDtypeStruct(tokens.shape, jnp.bfloat16),
        scratch_shapes=[
            pltpu.VMEM((2, heads * 64, 128), jnp.float32),
            pltpu.VMEM((rows, 256), jnp.float32),
            pltpu.VMEM((rows, 256), jnp.bfloat16),
            pltpu.VMEM((rows, 256), jnp.bfloat16),
            pltpu.VMEM((rows, 256), jnp.bfloat16),
        ],
        compiler_params=pltpu.CompilerParams(vmem_limit_bytes=40 * 1024 * 1024),
        name="both_blocks",
    )(tokens, *operands)


def token_order(heads):
    index = np.arange(64)
    placed = np.zeros((heads, 2, 64, heads, 64), np.float32)
    for head in range(heads):
        placed[head, :, index, head, index % 8 * 8 + index // 8] = 1.0
    return placed.reshape(heads * 128, heads * 64).astype(jnp.bfloat16)


def window_body(volume, norm_gains, qkv_weight, out_weight, up_weight, down_weight, window_bias):
    rows = volume.shape[1]
    width = volume.shape[2]
    channels = norm_gains.shape[1]
    heads = window_bias.shape[0]
    planes = lax.axis_size("gz")
    windows = width // channels // 8
    packed = pack(volume.reshape(rows, width), windows, channels)
    tokens = lax.all_to_all(packed, ("gz", "tile"), split_axis=0, concat_axis=0, tiled=True)
    mixed = blocks(
        tokens,
        norm_gains,
        qkv_weight,
        out_weight,
        up_weight,
        jnp.transpose(down_weight, (0, 2, 1)),
        window_bias.reshape(heads * 64, 64),
        token_order(heads),
    )
    returned = lax.all_to_all(mixed, ("gz", "tile"), split_axis=0, concat_axis=0, tiled=True)
    return unpack(returned, rows, width).reshape(1, rows, width)


def fits_windows(mesh, volume, norm_gains, window_bias):
    planes, tiles = mesh.shape["gz"], mesh.shape["tile"]
    channels, heads = norm_gains.shape[1], window_bias.shape[0]
    return (
        tiles == 2
        and planes == 8
        and volume.shape[1] == 16 * tiles
        and volume.shape[2] == 8 * channels * planes * tiles
        and channels == 96
        and heads == 3
    )


def solution(mesh):
    placed = (P(("groups", "gz"), "tile", None), P(), P(), P(), P(), P(), P())

    def run(volume, norm_gains, *weights):
        chosen = window_body if fits_windows(mesh, volume, norm_gains, weights[-1]) else general_body
        return jax.shard_map(
            chosen,
            mesh=mesh,
            in_specs=placed,
            out_specs=P(("groups", "gz"), "tile", None),
            check_vma=False,
        )(volume, norm_gains, *weights)

    return run
```

```python
import jax
import jax.numpy as jnp
import numpy as np
from jax import lax
from jax.experimental import pallas as pl
from jax.experimental.pallas import tpu as pltpu
from jax.sharding import PartitionSpec as P

epsilon = 1e-05


def shifted(array, axis, by):
    peers = lax.axis_size(axis)
    return lax.ppermute(array, axis, [(i, (i + by) % peers) for i in range(peers)])


def layer_norm(tokens, gain):
    values = tokens.astype(jnp.float32)
    average = jnp.mean(values, -1, keepdims=True)
    centered = values - average
    variance = jnp.mean(centered * centered, -1, keepdims=True)
    return (centered * lax.rsqrt(variance + epsilon) * gain).astype(jnp.bfloat16)


def feed_forward(tokens, gain, up_matrix, down_matrix):
    normed = layer_norm(tokens, gain)
    hidden = jax.nn.gelu(jnp.dot(normed, up_matrix, preferred_element_type=jnp.float32)).astype(
        jnp.bfloat16
    )
    total = tokens.astype(jnp.float32) + jnp.dot(
        hidden, down_matrix, preferred_element_type=jnp.float32
    )
    return total.astype(jnp.bfloat16)


def edge_label(index, extent):
    return jnp.where(index < 4, 2, jnp.where(index >= extent - 4, 1, 0)).astype(jnp.int32)


def head_masks(heads, channels):
    owner = jnp.arange(channels, dtype=jnp.int32) // (channels // heads)
    return (owner[None, :] == jnp.arange(heads, dtype=jnp.int32)[:, None]).astype(jnp.bfloat16)


def window_attention(
    row_block, first_row, height, channels, norm_gains, qkv_weight, out_weight, window_bias
):
    count = row_block.shape[0]
    columns = row_block.shape[1] // channels
    heads = window_bias.shape[0]
    head_size = channels // heads
    masks = head_masks(heads, channels)
    rolled = jnp.roll(row_block, -4 * channels, axis=1)
    windowed = rolled.reshape(count // 8, 8, columns // 8, 8 * channels).transpose(0, 2, 1, 3)
    normed = layer_norm(windowed.reshape(-1, channels), norm_gains[0])
    packed = jnp.dot(normed, qkv_weight[0], preferred_element_type=jnp.float32).astype(jnp.bfloat16)
    packed = packed.reshape(-1, 64, 3 * channels)
    queries = packed[:, :, :channels]
    keys = packed[:, :, channels : 2 * channels]
    values = packed[:, :, 2 * channels :]
    initial_rows = jnp.mod(first_row + jnp.arange(count, dtype=jnp.int32), height)
    initial_columns = jnp.mod(jnp.arange(columns, dtype=jnp.int32) + 4, columns)
    labels = (
        edge_label(initial_rows, height)[:, None] * 3
        + edge_label(initial_columns, columns)[None, :]
    )
    window_labels = (
        labels.reshape(count // 8, 8, columns // 8, 8).transpose(0, 2, 1, 3).reshape(-1, 64)
    )
    allowed = window_labels[:, :, None] == window_labels[:, None, :]
    head_queries = queries[:, None] * masks[None, :, None, :]
    scores = jnp.einsum("nhqc,nkc->nhqk", head_queries, keys, preferred_element_type=jnp.float32)
    scores = scores * head_size ** (-0.5) + window_bias[None]
    scores = jnp.where(allowed[:, None], scores, -jnp.inf)
    weights = jax.nn.softmax(scores, axis=-1).astype(jnp.bfloat16)
    head_values = values[:, None] * masks[None, :, None, :]
    attended = jnp.einsum(
        "nhqk,nhkc->nqc", weights, head_values, preferred_element_type=jnp.float32
    ).astype(jnp.bfloat16)
    lateral = jnp.dot(
        attended.reshape(-1, channels), out_weight[0], preferred_element_type=jnp.float32
    ).astype(jnp.bfloat16)
    lateral = lateral.reshape(count // 8, columns // 8, 8, 8 * channels).transpose(0, 2, 1, 3)
    return jnp.roll(lateral.reshape(count, columns * channels), 4 * channels, axis=1)


def axial_block(pencils, norm_gains, qkv_weight, out_weight, up_weight, down_weight, heads):
    planes, count, channels = pencils.shape
    head_size = channels // heads
    masks = head_masks(heads, channels)
    flat = jnp.transpose(pencils, (1, 0, 2)).reshape(-1, channels)
    normed = layer_norm(flat, norm_gains[2])
    packed = jnp.dot(normed, qkv_weight[1], preferred_element_type=jnp.float32).astype(jnp.bfloat16)
    packed = packed.reshape(count, planes, 3 * channels)
    queries = packed[:, :, :channels]
    keys = packed[:, :, channels : 2 * channels]
    values = packed[:, :, 2 * channels :]
    head_queries = queries[:, None] * masks[None, :, None, :]
    scores = jnp.einsum("phzc,pyc->phzy", head_queries, keys, preferred_element_type=jnp.float32)
    weights = jax.nn.softmax(scores * head_size ** (-0.5), axis=-1).astype(jnp.bfloat16)
    head_values = values[:, None] * masks[None, :, None, :]
    attended = jnp.einsum(
        "phzy,phyc->pzc", weights, head_values, preferred_element_type=jnp.float32
    ).astype(jnp.bfloat16)
    projected = jnp.dot(
        attended.reshape(-1, channels), out_weight[1], preferred_element_type=jnp.float32
    ).astype(jnp.bfloat16)
    after = (flat.astype(jnp.float32) + projected.astype(jnp.float32)).astype(jnp.bfloat16)
    mixed = feed_forward(after, norm_gains[3], up_weight[1], down_weight[1]).reshape(
        count, planes, channels
    )
    return jnp.transpose(mixed, (1, 0, 2))


def general_body(volume, norm_gains, qkv_weight, out_weight, up_weight, down_weight, window_bias):
    rows_here = volume.shape[1]
    row_width = volume.shape[2]
    channels = norm_gains.shape[1]
    heads = window_bias.shape[0]
    height = rows_here * lax.axis_size("tile")
    tile_start = lax.axis_index("tile") * rows_here
    plane = volume.reshape(rows_here, row_width)
    next_rows = shifted(plane[:4], "tile", -1)
    extended = jnp.concatenate([plane[4:], next_rows], 0)
    attended = window_attention(
        extended, tile_start + 4, height, channels, norm_gains, qkv_weight, out_weight, window_bias
    )
    tail_rows = shifted(attended[-4:], "tile", 1)
    lateral = jnp.concatenate([tail_rows, attended[:-4]], 0)
    middle = (
        (plane.astype(jnp.float32) + lateral.astype(jnp.float32))
        .astype(jnp.bfloat16)
        .reshape(-1, channels)
    )
    planes = lax.axis_size("gz")
    middle = feed_forward(middle, norm_gains[1], up_weight[0], down_weight[0])
    grouped = middle.reshape(planes, -1, channels)
    pencils = lax.all_to_all(grouped, "gz", split_axis=0, concat_axis=0, tiled=True)
    returned = lax.all_to_all(
        axial_block(pencils, norm_gains, qkv_weight, out_weight, up_weight, down_weight, heads),
        "gz",
        split_axis=0,
        concat_axis=0,
        tiled=True,
    )
    return returned.reshape(1, rows_here, row_width)


LOG2E = 1.4426950408889634


def normalised(tokens):
    average = jnp.mean(tokens, 0, keepdims=True)
    centered = tokens - average
    variance = jnp.mean(centered * centered, 0, keepdims=True)
    return (centered * lax.rsqrt(variance + epsilon)).astype(jnp.bfloat16)


def product(left, right):
    return jnp.dot(left, right, preferred_element_type=jnp.float32)


GELU_IN = 0.035677408136300125 ** (1 / 3)
GELU_LINEAR = 0.7978845608028654 / GELU_IN
GELU_OUT = 0.5 / GELU_IN


def across(left, right):
    return lax.dot_general(left, right, (((1,), (1,)), ((), ())), preferred_element_type=jnp.float32)


def gated(scaled):
    scaled = scaled.astype(jnp.bfloat16)
    return scaled + scaled * jnp.tanh(scaled * (GELU_LINEAR + scaled * scaled))


def run_copies(source_ref, target_ref, sems, cut):
    width = source_ref.shape[1]
    runs = (pl.ds(0, cut), pl.ds(cut, width - cut))
    return [
        pltpu.make_async_copy(source_ref.at[:, run], target_ref.at[:, run], sems.at[index])
        for index, run in enumerate(runs)
    ]


def pack_kernel(volume_ref, gains_ref, packed_ref, held_gains_ref, rows_ref, sems):
    windows, channels, _ = packed_ref.shape
    width = 8 * channels
    half = width // 2
    copies = run_copies(volume_ref, rows_ref, sems, windows // 2 * width + half)
    copies.append(pltpu.make_async_copy(gains_ref, held_gains_ref, sems.at[2]))
    for copy in copies:
        copy.start()
    copies[0].wait()
    for window in range(windows):
        if window == windows // 2:
            copies[1].wait()
        start = window * width + half
        if window < windows - 1:
            chunk = rows_ref[:, start : start + width]
        else:
            chunk = jnp.concatenate([rows_ref[:, start:], rows_ref[:, :half]], axis=1)
        chunk = chunk.astype(jnp.float32)
        rolled = jnp.concatenate([chunk[4:], chunk[:4]], axis=0)
        pieces = [
            rolled[8 * part : 8 * part + 8, channels * column : channels * (column + 1)]
            for part in range(2)
            for column in range(8)
        ]
        packed_ref[window] = jnp.concatenate(pieces, axis=0).T.astype(jnp.bfloat16)
    copies[2].wait()


def unpack_kernel(packed_ref, volume_ref, rows_ref, sems):
    windows, channels, _ = packed_ref.shape
    width = 8 * channels
    half = width // 2
    copies = run_copies(rows_ref, volume_ref, sems, windows // 2 * width + half)
    for window in [windows - 1, *range(windows - 1)]:
        tokens = packed_ref[window].astype(jnp.float32).T
        parts = [
            jnp.concatenate(
                [tokens[64 * part + 8 * column : 64 * part + 8 * column + 8] for column in range(8)], axis=1
            )
            for part in range(2)
        ]
        rows = jnp.concatenate([parts[1][4:], parts[0], parts[1][:4]], axis=0).astype(jnp.bfloat16)
        start = window * width + half
        if window < windows - 1:
            rows_ref[:, start : start + width] = rows
        else:
            rows_ref[:, start:] = rows[:, :half]
            rows_ref[:, :half] = rows[:, half:]
        if window == windows // 2 - 1:
            copies[0].start()
    copies[1].start()
    for copy in copies:
        copy.wait()


def in_lockstep(stages, planes):
    for stage in stages:
        for plane in range(planes):
            stage(plane)


def blocks_kernel(
    tokens_ref,
    gains_ref,
    qkv_weight_ref,
    out_weight_ref,
    up_weight_ref,
    down_weight_ref,
    window_bias_ref,
    order_ref,
    result_ref,
    bias_ref,
    planar_ref,
    query_ref,
    key_ref,
    value_ref,
):
    channels = tokens_ref.shape[1]
    planes = tokens_ref.shape[0] // 2
    heads = window_bias_ref.shape[0] // 64
    head_size = channels // heads
    lane = lax.broadcasted_iota(jnp.int32, (1, 128), 1)
    own = (lane < 64) | (lane % 8 < 4)
    first = lane < 64
    blank = jnp.zeros((128 - channels, 128), jnp.bfloat16)
    blank_rows = jnp.zeros((128 - channels, 128), jnp.float32)

    def turned(ref, layer):
        return ref[layer].astype(jnp.float32).T

    def gain(norm, scale):
        return gains_ref[norm : norm + 1, :] * scale

    def turned_qkv(layer):
        matrix = turned(qkv_weight_ref, layer)
        queries = matrix[:channels] * gain(2 * layer, LOG2E * head_size ** (-0.5))
        return jnp.concatenate([queries, matrix[channels:] * gain(2 * layer, 1.0)], axis=0).astype(jnp.bfloat16)

    qkv = [turned_qkv(layer) for layer in range(2)]
    up = [(turned(up_weight_ref, layer) * gain(2 * layer + 1, GELU_IN)).astype(jnp.bfloat16) for layer in range(2)]
    down = [(down_weight_ref[layer].astype(jnp.float32) * GELU_OUT).astype(jnp.bfloat16) for layer in range(2)]
    out = turned(out_weight_ref, 0).astype(jnp.bfloat16)
    mix = jnp.concatenate([turned(out_weight_ref, 1).astype(jnp.bfloat16)] * 2, axis=1)

    shape = (heads * planes, planes * channels // 2)
    row = lax.broadcasted_iota(jnp.int32, shape, 0)
    column = lax.broadcasted_iota(jnp.int32, shape, 1)
    mine = lax.div(column, head_size // 2) == lax.rem(row, planes) * heads + lax.div(row, planes)
    gather = jnp.where(mine, 1.0, 0.0).astype(jnp.bfloat16)

    high = window_bias_ref[...].astype(jnp.bfloat16)
    low = (window_bias_ref[...] - high.astype(jnp.float32)).astype(jnp.bfloat16)
    parts = [across(order_ref[:64, :64], part).astype(jnp.bfloat16) for part in (high, low)]
    position = lax.axis_index("gz") * lax.axis_size("tile") + lax.axis_index("tile")
    last = position == lax.axis_size("gz") * lax.axis_size("tile") - 1
    key_row = lax.broadcasted_iota(jnp.int32, (64, 128), 0)
    query_lane = lax.broadcasted_iota(jnp.int32, (64, 128), 1)
    column_cut = ((key_row < 32) != (query_lane % 64 < 32)) & last
    row_cut = ((key_row % 8 < 4) != (query_lane % 8 < 4)) & (query_lane >= 64)
    for head in range(heads):
        placed = order_ref[128 * head : 128 * (head + 1), :]
        plain = (across(parts[0], placed) + across(parts[1], placed)) * LOG2E
        plain = jnp.where(column_cut, -jnp.inf, plain)
        bias_ref[0, 64 * head : 64 * (head + 1), :] = plain
        bias_ref[1, 64 * head : 64 * (head + 1), :] = jnp.where(row_cut, -jnp.inf, plain)

    held = [{} for _ in range(planes)]

    def rows_of(plane):
        return slice(plane * channels, (plane + 1) * channels)

    def load(plane):
        one, two = tokens_ref[2 * plane], tokens_ref[2 * plane + 1]
        tokens = jnp.concatenate([jnp.where(own, one, two), jnp.where(own, two, one)], axis=1)
        held[plane]["x"] = tokens.astype(jnp.float32)

    def norm(plane):
        held[plane]["n"] = normalised(held[plane]["x"])

    def lateral_qkv(plane):
        packed = product(qkv[0], held[plane].pop("n"))
        held[plane]["q"] = packed[:channels]
        held[plane]["k"] = packed[channels : 2 * channels]
        held[plane]["v"] = packed[2 * channels :].astype(jnp.bfloat16)

    def lateral_scores(plane):
        queries, keys = held[plane].pop("q"), held[plane].pop("k")
        scores = []
        for pair in range(2):
            lanes = slice(128 * pair, 128 * pair + 128)
            query = queries[:, lanes]
            right = jnp.concatenate(
                [
                    jnp.where(first, query, 0.0).astype(jnp.bfloat16),
                    blank,
                    jnp.where(first, 0.0, query).astype(jnp.bfloat16),
                    blank,
                ],
                axis=0,
            )
            key = jnp.concatenate([keys[:, lanes], blank_rows], axis=0).T
            left = []
            for head in range(heads):
                masked = jnp.where(lane // head_size == head, key, 0.0).astype(jnp.bfloat16)
                left.append(jnp.concatenate([masked[:64], masked[64:]], axis=1))
            scores.append((jnp.concatenate(left, axis=0), right))
        held[plane]["s"] = scores

    def lateral_weights(plane):
        scores = held[plane].pop("s")
        held[plane]["w"] = []
        for pair in range(2):
            for head in range(heads):
                own_scores = scores[pair][64 * head : 64 * head + 64]
                weights = jnp.exp2(own_scores - jnp.max(own_scores, axis=0, keepdims=True))
                total = jnp.sum(weights, axis=0, keepdims=True)
                spread = jnp.concatenate(
                    [
                        jnp.where(first, weights, 0.0).astype(jnp.bfloat16),
                        jnp.where(first, 0.0, weights).astype(jnp.bfloat16),
                    ],
                    axis=0,
                )
                held[plane]["w"].append((spread, 1.0 / total))

    def lateral_products(plane):
        held[plane]["s"] = [product(*held[plane]["s"][pair]) + bias_ref[pair] for pair in range(2)]

    def lateral_values(plane):
        weights, values = held[plane].pop("w"), held[plane].pop("v")
        attended = []
        for pair in range(2):
            lanes = slice(128 * pair, 128 * pair + 128)
            mixed = []
            for head in range(heads):
                spread, inverse = weights[heads * pair + head]
                own_mixed = product(values[head_size * head : head_size * (head + 1), lanes], spread)
                mixed.append((own_mixed * inverse).astype(jnp.bfloat16))
            attended.append(jnp.concatenate(mixed, axis=0))
        held[plane]["a"] = jnp.concatenate(attended, axis=1)

    def lateral_out(plane):
        held[plane]["x"] = held[plane]["x"] + product(out, held[plane].pop("a"))

    def raised(layer):
        def stage(plane):
            held[plane]["h"] = product(up[layer], held[plane].pop("n"))

        return stage

    def gelu(plane):
        held[plane]["g"] = gated(held[plane].pop("h"))

    def lowered(layer):
        def stage(plane):
            held[plane]["x"] = held[plane]["x"] + product(down[layer], held[plane].pop("g"))

        return stage

    def axial_qkv(plane):
        packed = product(qkv[1], held[plane].pop("n")).astype(jnp.bfloat16)
        planar_ref[rows_of(plane), :] = held[plane].pop("x")
        query_ref[rows_of(plane), :] = packed[:channels]
        key_ref[rows_of(plane), :] = packed[channels : 2 * channels]
        value_ref[rows_of(plane), :] = packed[2 * channels :]

    def axial_scores(plane):
        query = query_ref[rows_of(plane), :]
        half = head_size // 2
        pairs = []
        for other in range(planes):
            pair = query * key_ref[rows_of(other), :]
            for head in range(heads):
                top = head_size * head
                pairs.append(pair[top : top + half] + pair[top + half : top + head_size])
        pairs = jnp.concatenate(pairs, axis=0)
        held[plane]["s"] = product(gather, pairs)

    def axial_weights(plane):
        scores = held[plane].pop("s")
        weights = []
        for head in range(heads):
            own_scores = scores[planes * head : planes * (head + 1)]
            own_weights = jnp.exp2(own_scores - jnp.max(own_scores, axis=0, keepdims=True))
            weights.append(own_weights * (1.0 / jnp.sum(own_weights, axis=0, keepdims=True)))
        held[plane]["w"] = weights

    def axial_values(plane):
        weights = held[plane].pop("w")
        spread = []
        for other in range(planes):
            wide = jnp.concatenate(
                [
                    jnp.broadcast_to(weights[head][other : other + 1], (head_size, 256)).astype(jnp.bfloat16)
                    for head in range(heads)
                ],
                axis=0,
            )
            spread.append(wide * value_ref[rows_of(other), :])
        while len(spread) > 2:
            spread = [one + two for one, two in zip(spread[::2], spread[1::2])]
        spread = jnp.concatenate(spread, axis=0)
        held[plane]["x"] = planar_ref[rows_of(plane), :] + product(mix, spread)

    def store(plane):
        mixed = held[plane].pop("x").astype(jnp.bfloat16)
        one, two = mixed[:, :128], mixed[:, 128:]
        result_ref[2 * plane] = jnp.where(own, one, two)
        result_ref[2 * plane + 1] = jnp.where(own, two, one)

    lateral = [load, norm, lateral_qkv, lateral_scores, lateral_products, lateral_weights, lateral_values, lateral_out]
    lateral += [norm, raised(0), gelu, lowered(0), norm, axial_qkv]
    axial = [axial_scores, axial_weights, axial_values, norm, raised(1), gelu, lowered(1), store]
    in_lockstep(lateral + axial, planes)


def pack(rows, gains, windows):
    return pl.pallas_call(
        pack_kernel,
        out_shape=(
            jax.ShapeDtypeStruct((windows, gains.shape[1], 128), jnp.bfloat16),
            jax.ShapeDtypeStruct(gains.shape, gains.dtype),
        ),
        in_specs=[pl.BlockSpec(memory_space=pltpu.HBM)] * 2,
        scratch_shapes=[pltpu.VMEM(rows.shape, rows.dtype), pltpu.SemaphoreType.DMA((3,))],
        compiler_params=pltpu.CompilerParams(vmem_limit_bytes=16 * 1024 * 1024),
        name="pack_windows",
    )(*(pltpu.with_memory_space_constraint(operand, pltpu.HBM) for operand in (rows, gains)))


def unpack(packed, rows, width):
    return pl.pallas_call(
        unpack_kernel,
        out_shape=jax.ShapeDtypeStruct((rows, width), jnp.bfloat16),
        out_specs=pl.BlockSpec(memory_space=pltpu.HBM),
        scratch_shapes=[pltpu.VMEM((rows, width), jnp.bfloat16), pltpu.SemaphoreType.DMA((2,))],
        compiler_params=pltpu.CompilerParams(vmem_limit_bytes=16 * 1024 * 1024),
        name="unpack_windows",
    )(packed)


def blocks(tokens, *operands):
    sources, channels, _ = tokens.shape
    rows = sources // 2 * channels
    heads = operands[5].shape[0] // 64
    return pl.pallas_call(
        blocks_kernel,
        out_shape=jax.ShapeDtypeStruct(tokens.shape, jnp.bfloat16),
        scratch_shapes=[
            pltpu.VMEM((2, heads * 64, 128), jnp.float32),
            pltpu.VMEM((rows, 256), jnp.float32),
            pltpu.VMEM((rows, 256), jnp.bfloat16),
            pltpu.VMEM((rows, 256), jnp.bfloat16),
            pltpu.VMEM((rows, 256), jnp.bfloat16),
        ],
        compiler_params=pltpu.CompilerParams(vmem_limit_bytes=40 * 1024 * 1024),
        name="both_blocks",
    )(tokens, *operands)


def token_order(heads):
    index = np.arange(64)
    placed = np.zeros((heads, 2, 64, heads, 64), np.float32)
    for head in range(heads):
        placed[head, :, index, head, index % 8 * 8 + index // 8] = 1.0
    return placed.reshape(heads * 128, heads * 64).astype(jnp.bfloat16)


def window_body(volume, norm_gains, qkv_weight, out_weight, up_weight, down_weight, window_bias):
    rows = volume.shape[1]
    width = volume.shape[2]
    channels = norm_gains.shape[1]
    heads = window_bias.shape[0]
    planes = lax.axis_size("gz")
    windows = width // channels // 8
    packed, held_gains = pack(volume.reshape(rows, width), norm_gains, windows)
    tokens = lax.all_to_all(packed, ("gz", "tile"), split_axis=0, concat_axis=0, tiled=True)
    mixed = blocks(
        tokens,
        held_gains,
        qkv_weight,
        out_weight,
        up_weight,
        jnp.transpose(down_weight, (0, 2, 1)),
        window_bias.reshape(heads * 64, 64),
        token_order(heads),
    )
    returned = lax.all_to_all(mixed, ("gz", "tile"), split_axis=0, concat_axis=0, tiled=True)
    return unpack(returned, rows, width).reshape(1, rows, width)


def fits_windows(mesh, volume, norm_gains, window_bias):
    planes, tiles = mesh.shape["gz"], mesh.shape["tile"]
    channels, heads = norm_gains.shape[1], window_bias.shape[0]
    return (
        tiles == 2
        and planes == 8
        and volume.shape[1] == 16 * tiles
        and volume.shape[2] == 8 * channels * planes * tiles
        and channels == 96
        and heads == 3
    )


def solution(mesh):
    placed = (P(("groups", "gz"), "tile", None), P(), P(), P(), P(), P(), P())

    def run(volume, norm_gains, *weights):
        chosen = window_body if fits_windows(mesh, volume, norm_gains, weights[-1]) else general_body
        return jax.shard_map(
            chosen,
            mesh=mesh,
            in_specs=placed,
            out_specs=P(("groups", "gz"), "tile", None),
            check_vma=False,
        )(volume, norm_gains, *weights)

    return run
```

```python
import jax
import jax.numpy as jnp
import numpy as np
from jax import lax
from jax.experimental import pallas as pl
from jax.experimental.pallas import tpu as pltpu
from jax.sharding import PartitionSpec as P

epsilon = 1e-05


def shifted(array, axis, by):
    peers = lax.axis_size(axis)
    return lax.ppermute(array, axis, [(i, (i + by) % peers) for i in range(peers)])


def layer_norm(tokens, gain):
    values = tokens.astype(jnp.float32)
    average = jnp.mean(values, -1, keepdims=True)
    centered = values - average
    variance = jnp.mean(centered * centered, -1, keepdims=True)
    return (centered * lax.rsqrt(variance + epsilon) * gain).astype(jnp.bfloat16)


def feed_forward(tokens, gain, up_matrix, down_matrix):
    normed = layer_norm(tokens, gain)
    hidden = jax.nn.gelu(jnp.dot(normed, up_matrix, preferred_element_type=jnp.float32)).astype(
        jnp.bfloat16
    )
    total = tokens.astype(jnp.float32) + jnp.dot(
        hidden, down_matrix, preferred_element_type=jnp.float32
    )
    return total.astype(jnp.bfloat16)


def edge_label(index, extent):
    return jnp.where(index < 4, 2, jnp.where(index >= extent - 4, 1, 0)).astype(jnp.int32)


def head_masks(heads, channels):
    owner = jnp.arange(channels, dtype=jnp.int32) // (channels // heads)
    return (owner[None, :] == jnp.arange(heads, dtype=jnp.int32)[:, None]).astype(jnp.bfloat16)


def window_attention(
    row_block, first_row, height, channels, norm_gains, qkv_weight, out_weight, window_bias
):
    count = row_block.shape[0]
    columns = row_block.shape[1] // channels
    heads = window_bias.shape[0]
    head_size = channels // heads
    masks = head_masks(heads, channels)
    rolled = jnp.roll(row_block, -4 * channels, axis=1)
    windowed = rolled.reshape(count // 8, 8, columns // 8, 8 * channels).transpose(0, 2, 1, 3)
    normed = layer_norm(windowed.reshape(-1, channels), norm_gains[0])
    packed = jnp.dot(normed, qkv_weight[0], preferred_element_type=jnp.float32).astype(jnp.bfloat16)
    packed = packed.reshape(-1, 64, 3 * channels)
    queries = packed[:, :, :channels]
    keys = packed[:, :, channels : 2 * channels]
    values = packed[:, :, 2 * channels :]
    initial_rows = jnp.mod(first_row + jnp.arange(count, dtype=jnp.int32), height)
    initial_columns = jnp.mod(jnp.arange(columns, dtype=jnp.int32) + 4, columns)
    labels = (
        edge_label(initial_rows, height)[:, None] * 3
        + edge_label(initial_columns, columns)[None, :]
    )
    window_labels = (
        labels.reshape(count // 8, 8, columns // 8, 8).transpose(0, 2, 1, 3).reshape(-1, 64)
    )
    allowed = window_labels[:, :, None] == window_labels[:, None, :]
    head_queries = queries[:, None] * masks[None, :, None, :]
    scores = jnp.einsum("nhqc,nkc->nhqk", head_queries, keys, preferred_element_type=jnp.float32)
    scores = scores * head_size ** (-0.5) + window_bias[None]
    scores = jnp.where(allowed[:, None], scores, -jnp.inf)
    weights = jax.nn.softmax(scores, axis=-1).astype(jnp.bfloat16)
    head_values = values[:, None] * masks[None, :, None, :]
    attended = jnp.einsum(
        "nhqk,nhkc->nqc", weights, head_values, preferred_element_type=jnp.float32
    ).astype(jnp.bfloat16)
    lateral = jnp.dot(
        attended.reshape(-1, channels), out_weight[0], preferred_element_type=jnp.float32
    ).astype(jnp.bfloat16)
    lateral = lateral.reshape(count // 8, columns // 8, 8, 8 * channels).transpose(0, 2, 1, 3)
    return jnp.roll(lateral.reshape(count, columns * channels), 4 * channels, axis=1)


def axial_block(pencils, norm_gains, qkv_weight, out_weight, up_weight, down_weight, heads):
    planes, count, channels = pencils.shape
    head_size = channels // heads
    masks = head_masks(heads, channels)
    flat = jnp.transpose(pencils, (1, 0, 2)).reshape(-1, channels)
    normed = layer_norm(flat, norm_gains[2])
    packed = jnp.dot(normed, qkv_weight[1], preferred_element_type=jnp.float32).astype(jnp.bfloat16)
    packed = packed.reshape(count, planes, 3 * channels)
    queries = packed[:, :, :channels]
    keys = packed[:, :, channels : 2 * channels]
    values = packed[:, :, 2 * channels :]
    head_queries = queries[:, None] * masks[None, :, None, :]
    scores = jnp.einsum("phzc,pyc->phzy", head_queries, keys, preferred_element_type=jnp.float32)
    weights = jax.nn.softmax(scores * head_size ** (-0.5), axis=-1).astype(jnp.bfloat16)
    head_values = values[:, None] * masks[None, :, None, :]
    attended = jnp.einsum(
        "phzy,phyc->pzc", weights, head_values, preferred_element_type=jnp.float32
    ).astype(jnp.bfloat16)
    projected = jnp.dot(
        attended.reshape(-1, channels), out_weight[1], preferred_element_type=jnp.float32
    ).astype(jnp.bfloat16)
    after = (flat.astype(jnp.float32) + projected.astype(jnp.float32)).astype(jnp.bfloat16)
    mixed = feed_forward(after, norm_gains[3], up_weight[1], down_weight[1]).reshape(
        count, planes, channels
    )
    return jnp.transpose(mixed, (1, 0, 2))


def general_body(volume, norm_gains, qkv_weight, out_weight, up_weight, down_weight, window_bias):
    rows_here = volume.shape[1]
    row_width = volume.shape[2]
    channels = norm_gains.shape[1]
    heads = window_bias.shape[0]
    height = rows_here * lax.axis_size("tile")
    tile_start = lax.axis_index("tile") * rows_here
    plane = volume.reshape(rows_here, row_width)
    next_rows = shifted(plane[:4], "tile", -1)
    extended = jnp.concatenate([plane[4:], next_rows], 0)
    attended = window_attention(
        extended, tile_start + 4, height, channels, norm_gains, qkv_weight, out_weight, window_bias
    )
    tail_rows = shifted(attended[-4:], "tile", 1)
    lateral = jnp.concatenate([tail_rows, attended[:-4]], 0)
    middle = (
        (plane.astype(jnp.float32) + lateral.astype(jnp.float32))
        .astype(jnp.bfloat16)
        .reshape(-1, channels)
    )
    planes = lax.axis_size("gz")
    middle = feed_forward(middle, norm_gains[1], up_weight[0], down_weight[0])
    grouped = middle.reshape(planes, -1, channels)
    pencils = lax.all_to_all(grouped, "gz", split_axis=0, concat_axis=0, tiled=True)
    returned = lax.all_to_all(
        axial_block(pencils, norm_gains, qkv_weight, out_weight, up_weight, down_weight, heads),
        "gz",
        split_axis=0,
        concat_axis=0,
        tiled=True,
    )
    return returned.reshape(1, rows_here, row_width)


LOG2E = 1.4426950408889634


def normalised(tokens):
    average = jnp.mean(tokens, 0, keepdims=True)
    centered = tokens - average
    variance = jnp.mean(centered * centered, 0, keepdims=True)
    return (centered * lax.rsqrt(variance + epsilon)).astype(jnp.bfloat16)


def product(left, right):
    return jnp.dot(left, right, preferred_element_type=jnp.float32)


GELU_IN = 0.035677408136300125 ** (1 / 3)
GELU_LINEAR = 0.7978845608028654 / GELU_IN
GELU_OUT = 0.5 / GELU_IN


def across(left, right):
    return lax.dot_general(left, right, (((1,), (1,)), ((), ())), preferred_element_type=jnp.float32)


def gated(scaled):
    scaled = scaled.astype(jnp.bfloat16)
    return scaled + scaled * jnp.tanh(scaled * (GELU_LINEAR + scaled * scaled))


def pack_kernel(volume_ref, gains_ref, packed_ref, held_gains_ref, rows_ref, sems):
    windows, channels, _ = packed_ref.shape
    width = 8 * channels
    half = width // 2
    copies = [
        pltpu.make_async_copy(volume_ref, rows_ref, sems.at[0]),
        pltpu.make_async_copy(gains_ref, held_gains_ref, sems.at[1]),
    ]
    for copy in copies:
        copy.start()
    for copy in copies:
        copy.wait()
    tokens = []
    for window in range(windows):
        start = window * width + half
        if window < windows - 1:
            chunk = rows_ref[:, start : start + width]
        else:
            chunk = jnp.concatenate([rows_ref[:, start:], rows_ref[:, :half]], axis=1)
        rolled = jnp.concatenate([chunk[4:], chunk[:4]], axis=0)
        pieces = [rolled[:, channels * column : channels * (column + 1)] for column in range(8)]
        tokens.append(jnp.concatenate(pieces, axis=0))
    for window in range(windows):
        packed_ref[window] = tokens[window].T


def unpack_kernel(packed_ref, volume_ref, rows_ref, sems):
    windows, channels, _ = packed_ref.shape
    width = 8 * channels
    half = width // 2
    tokens = [packed_ref[window].T for window in range(windows)]
    for window in range(windows):
        rows = jnp.concatenate([tokens[window][16 * column : 16 * column + 16] for column in range(8)], axis=1)
        rows = jnp.concatenate([rows[12:], rows[:12]], axis=0)
        start = window * width + half
        if window < windows - 1:
            rows_ref[:, start : start + width] = rows
        else:
            rows_ref[:, start:] = rows[:, :half]
            rows_ref[:, :half] = rows[:, half:]
    copy = pltpu.make_async_copy(rows_ref, volume_ref, sems.at[0])
    copy.start()
    copy.wait()


def in_lockstep(stages, planes):
    for stage in stages:
        for plane in range(planes):
            stage(plane)


def blocks_kernel(
    tokens_ref,
    gains_ref,
    qkv_weight_ref,
    out_weight_ref,
    up_weight_ref,
    down_weight_ref,
    window_bias_ref,
    order_ref,
    result_ref,
    bias_ref,
    planar_ref,
    query_ref,
    key_ref,
    value_ref,
):
    channels = tokens_ref.shape[1]
    planes = tokens_ref.shape[0] // 2
    heads = window_bias_ref.shape[0] // 64
    head_size = channels // heads
    lane = lax.broadcasted_iota(jnp.int32, (1, 128), 1)
    own = lane % 16 < 12
    first = lane % 16 < 8
    shape = (128, 128)
    same = lax.broadcasted_iota(jnp.int32, shape, 0) % 16 // 8 == lax.broadcasted_iota(jnp.int32, shape, 1) % 16 // 8
    blank = jnp.zeros((128 - channels, 128), jnp.bfloat16)
    blank_rows = jnp.zeros((128 - channels, 128), jnp.float32)

    def turned(ref, layer):
        return ref[layer].astype(jnp.float32).T

    def gain(norm, scale):
        return gains_ref[norm : norm + 1, :] * scale

    def turned_qkv(layer):
        matrix = turned(qkv_weight_ref, layer)
        queries = matrix[:channels] * gain(2 * layer, LOG2E * head_size ** (-0.5))
        return jnp.concatenate([queries, matrix[channels:] * gain(2 * layer, 1.0)], axis=0).astype(jnp.bfloat16)

    qkv = [turned_qkv(layer) for layer in range(2)]
    up = [(turned(up_weight_ref, layer) * gain(2 * layer + 1, GELU_IN)).astype(jnp.bfloat16) for layer in range(2)]
    down = [(down_weight_ref[layer].astype(jnp.float32) * GELU_OUT).astype(jnp.bfloat16) for layer in range(2)]
    out = turned(out_weight_ref, 0).astype(jnp.bfloat16)
    mix = jnp.concatenate([turned(out_weight_ref, 1).astype(jnp.bfloat16)] * 2, axis=1)

    shape = (heads * planes, planes * channels // 2)
    row = lax.broadcasted_iota(jnp.int32, shape, 0)
    column = lax.broadcasted_iota(jnp.int32, shape, 1)
    mine = lax.div(column, head_size // 2) == lax.rem(row, planes) * heads + lax.div(row, planes)
    gather = jnp.where(mine, 1.0, 0.0).astype(jnp.bfloat16)

    high = window_bias_ref[...].astype(jnp.bfloat16)
    low = (window_bias_ref[...] - high.astype(jnp.float32)).astype(jnp.bfloat16)
    parts = [across(order_ref[:64, :64], part).astype(jnp.bfloat16) for part in (high, low)]
    position = lax.axis_index("gz") * lax.axis_size("tile") + lax.axis_index("tile")
    last = position == lax.axis_size("gz") * lax.axis_size("tile") - 1
    key_row = lax.broadcasted_iota(jnp.int32, (64, 128), 0)
    query_lane = lax.broadcasted_iota(jnp.int32, (64, 128), 1)
    column_cut = ((key_row < 32) != (query_lane < 64)) & last
    row_cut = ((key_row % 8 < 4) != (query_lane % 8 < 4)) & (query_lane % 16 >= 8)
    for head in range(heads):
        placed = order_ref[64 + 128 * head : 64 + 128 * (head + 1), :]
        plain = (across(parts[0], placed) + across(parts[1], placed)) * LOG2E
        plain = jnp.where(column_cut, -jnp.inf, plain)
        bias_ref[0, 64 * head : 64 * (head + 1), :] = plain
        bias_ref[1, 64 * head : 64 * (head + 1), :] = jnp.where(row_cut, -jnp.inf, plain)

    held = [{} for _ in range(planes)]

    def rows_of(plane):
        return slice(plane * channels, (plane + 1) * channels)

    def load(plane):
        one, two = tokens_ref[2 * plane], tokens_ref[2 * plane + 1]
        tokens = jnp.concatenate([jnp.where(own, one, two), jnp.where(own, two, one)], axis=1)
        held[plane]["x"] = tokens.astype(jnp.float32)

    def norm(plane):
        held[plane]["n"] = normalised(held[plane]["x"])

    def lateral_qkv(plane):
        packed = product(qkv[0], held[plane].pop("n"))
        held[plane]["q"] = packed[:channels]
        held[plane]["k"] = packed[channels : 2 * channels]
        held[plane]["v"] = packed[2 * channels :].astype(jnp.bfloat16)

    def lateral_scores(plane):
        queries, keys = held[plane].pop("q"), held[plane].pop("k")
        scores = []
        for pair in range(2):
            lanes = slice(128 * pair, 128 * pair + 128)
            query = queries[:, lanes]
            right = jnp.concatenate(
                [
                    jnp.where(first, query, 0.0).astype(jnp.bfloat16),
                    blank,
                    jnp.where(first, 0.0, query).astype(jnp.bfloat16),
                    blank,
                ],
                axis=0,
            )
            key = jnp.concatenate([keys[:, lanes], blank_rows], axis=0).T
            left = []
            for head in range(heads):
                masked = jnp.where(lane // head_size == head, key, 0.0).reshape(8, 2, 8, 128)
                windows = [masked[:, window].reshape(64, 128).astype(jnp.bfloat16) for window in range(2)]
                left.append(jnp.concatenate(windows, axis=1))
            scores.append((jnp.concatenate(left, axis=0), right))
        held[plane]["s"] = scores

    def lateral_weights(plane):
        scores = held[plane].pop("s")
        held[plane]["w"] = []
        for pair in range(2):
            for head in range(heads):
                own_scores = scores[pair][64 * head : 64 * head + 64]
                weights = jnp.exp2(own_scores - jnp.max(own_scores, axis=0, keepdims=True))
                total = jnp.sum(weights, axis=0, keepdims=True)
                columns = weights.reshape(8, 1, 8, 128)
                both = jnp.concatenate([columns, columns], axis=1).reshape(128, 128).astype(jnp.bfloat16)
                spread = jnp.where(same, both, jnp.bfloat16(0))
                held[plane]["w"].append((spread, 1.0 / total))

    def lateral_products(plane):
        held[plane]["s"] = [product(*held[plane]["s"][pair]) + bias_ref[pair] for pair in range(2)]

    def lateral_values(plane):
        weights, values = held[plane].pop("w"), held[plane].pop("v")
        attended = []
        for pair in range(2):
            lanes = slice(128 * pair, 128 * pair + 128)
            mixed = []
            for head in range(heads):
                spread, inverse = weights[heads * pair + head]
                own_mixed = product(values[head_size * head : head_size * (head + 1), lanes], spread)
                mixed.append((own_mixed * inverse).astype(jnp.bfloat16))
            attended.append(jnp.concatenate(mixed, axis=0))
        held[plane]["a"] = jnp.concatenate(attended, axis=1)

    def lateral_out(plane):
        held[plane]["x"] = held[plane]["x"] + product(out, held[plane].pop("a"))

    def raised(layer):
        def stage(plane):
            held[plane]["h"] = product(up[layer], held[plane].pop("n"))

        return stage

    def gelu(plane):
        held[plane]["g"] = gated(held[plane].pop("h"))

    def lowered(layer):
        def stage(plane):
            held[plane]["x"] = held[plane]["x"] + product(down[layer], held[plane].pop("g"))

        return stage

    def axial_qkv(plane):
        packed = product(qkv[1], held[plane].pop("n")).astype(jnp.bfloat16)
        planar_ref[rows_of(plane), :] = held[plane].pop("x")
        query_ref[rows_of(plane), :] = packed[:channels]
        key_ref[rows_of(plane), :] = packed[channels : 2 * channels]
        value_ref[rows_of(plane), :] = packed[2 * channels :]

    def axial_scores(plane):
        query = query_ref[rows_of(plane), :]
        half = head_size // 2
        pairs = []
        for other in range(planes):
            pair = query * key_ref[rows_of(other), :]
            for head in range(heads):
                top = head_size * head
                pairs.append(pair[top : top + half] + pair[top + half : top + head_size])
        pairs = jnp.concatenate(pairs, axis=0)
        held[plane]["s"] = product(gather, pairs)

    def axial_weights(plane):
        scores = held[plane].pop("s")
        weights = []
        for head in range(heads):
            own_scores = scores[planes * head : planes * (head + 1)]
            own_weights = jnp.exp2(own_scores - jnp.max(own_scores, axis=0, keepdims=True))
            weights.append(own_weights * (1.0 / jnp.sum(own_weights, axis=0, keepdims=True)))
        held[plane]["w"] = weights

    def axial_values(plane):
        weights = held[plane].pop("w")
        spread = []
        for other in range(planes):
            wide = jnp.concatenate(
                [
                    jnp.broadcast_to(weights[head][other : other + 1], (head_size, 256)).astype(jnp.bfloat16)
                    for head in range(heads)
                ],
                axis=0,
            )
            spread.append(wide * value_ref[rows_of(other), :])
        while len(spread) > 2:
            spread = [one + two for one, two in zip(spread[::2], spread[1::2])]
        spread = jnp.concatenate(spread, axis=0)
        held[plane]["x"] = planar_ref[rows_of(plane), :] + product(mix, spread)

    def store(plane):
        mixed = held[plane].pop("x").astype(jnp.bfloat16)
        one, two = mixed[:, :128], mixed[:, 128:]
        result_ref[2 * plane] = jnp.where(own, one, two)
        result_ref[2 * plane + 1] = jnp.where(own, two, one)

    lateral = [load, norm, lateral_qkv, lateral_scores, lateral_products, lateral_weights, lateral_values, lateral_out]
    lateral += [norm, raised(0), gelu, lowered(0), norm, axial_qkv]
    axial = [axial_scores, axial_weights, axial_values, norm, raised(1), gelu, lowered(1), store]
    in_lockstep(lateral + axial, planes)


def pack(rows, gains, windows):
    return pl.pallas_call(
        pack_kernel,
        out_shape=(
            jax.ShapeDtypeStruct((windows, gains.shape[1], 128), jnp.bfloat16),
            jax.ShapeDtypeStruct(gains.shape, gains.dtype),
        ),
        in_specs=[pl.BlockSpec(memory_space=pltpu.HBM)] * 2,
        scratch_shapes=[pltpu.VMEM(rows.shape, rows.dtype), pltpu.SemaphoreType.DMA((2,))],
        compiler_params=pltpu.CompilerParams(vmem_limit_bytes=16 * 1024 * 1024),
        name="pack_windows",
    )(*(pltpu.with_memory_space_constraint(operand, pltpu.HBM) for operand in (rows, gains)))


def unpack(packed, rows, width):
    return pl.pallas_call(
        unpack_kernel,
        out_shape=jax.ShapeDtypeStruct((rows, width), jnp.bfloat16),
        out_specs=pl.BlockSpec(memory_space=pltpu.HBM),
        scratch_shapes=[pltpu.VMEM((rows, width), jnp.bfloat16), pltpu.SemaphoreType.DMA((1,))],
        compiler_params=pltpu.CompilerParams(vmem_limit_bytes=16 * 1024 * 1024),
        name="unpack_windows",
    )(packed)


def blocks(tokens, *operands):
    sources, channels, _ = tokens.shape
    rows = sources // 2 * channels
    heads = operands[5].shape[0] // 64
    return pl.pallas_call(
        blocks_kernel,
        out_shape=jax.ShapeDtypeStruct(tokens.shape, jnp.bfloat16),
        scratch_shapes=[
            pltpu.VMEM((2, heads * 64, 128), jnp.float32),
            pltpu.VMEM((rows, 256), jnp.float32),
            pltpu.VMEM((rows, 256), jnp.bfloat16),
            pltpu.VMEM((rows, 256), jnp.bfloat16),
            pltpu.VMEM((rows, 256), jnp.bfloat16),
        ],
        compiler_params=pltpu.CompilerParams(vmem_limit_bytes=40 * 1024 * 1024),
        name="both_blocks",
    )(tokens, *operands)


def token_order(heads):
    index = np.arange(64)
    order = np.zeros((64, heads * 64), np.float32)
    order[index, index % 8 * 8 + index // 8] = 1.0
    lane = np.arange(128)
    placed = np.zeros((heads, 128, heads, 64), np.float32)
    for head in range(heads):
        placed[head, lane, head, lane % 8 * 8 + lane // 16] = 1.0
    return np.concatenate([order, placed.reshape(heads * 128, heads * 64)]).astype(jnp.bfloat16)


def window_body(volume, norm_gains, qkv_weight, out_weight, up_weight, down_weight, window_bias):
    rows = volume.shape[1]
    width = volume.shape[2]
    channels = norm_gains.shape[1]
    heads = window_bias.shape[0]
    planes = lax.axis_size("gz")
    windows = width // channels // 8
    packed, held_gains = pack(volume.reshape(rows, width), norm_gains, windows)
    tokens = lax.all_to_all(packed, ("gz", "tile"), split_axis=0, concat_axis=0, tiled=True)
    mixed = blocks(
        tokens,
        held_gains,
        qkv_weight,
        out_weight,
        up_weight,
        jnp.transpose(down_weight, (0, 2, 1)),
        window_bias.reshape(heads * 64, 64),
        token_order(heads),
    )
    returned = lax.all_to_all(mixed, ("gz", "tile"), split_axis=0, concat_axis=0, tiled=True)
    return unpack(returned, rows, width).reshape(1, rows, width)


def fits_windows(mesh, volume, norm_gains, window_bias):
    planes, tiles = mesh.shape["gz"], mesh.shape["tile"]
    channels, heads = norm_gains.shape[1], window_bias.shape[0]
    return (
        tiles == 2
        and planes == 8
        and volume.shape[1] == 16 * tiles
        and volume.shape[2] == 8 * channels * planes * tiles
        and channels == 96
        and heads == 3
    )


def solution(mesh):
    placed = (P(("groups", "gz"), "tile", None), P(), P(), P(), P(), P(), P())

    def run(volume, norm_gains, *weights):
        chosen = window_body if fits_windows(mesh, volume, norm_gains, weights[-1]) else general_body
        return jax.shard_map(
            chosen,
            mesh=mesh,
            in_specs=placed,
            out_specs=P(("groups", "gz"), "tile", None),
            check_vma=False,
        )(volume, norm_gains, *weights)

    return run
```

```python
import jax
import jax.numpy as jnp
import numpy as np
from jax import lax
from jax.experimental import pallas as pl
from jax.experimental.pallas import tpu as pltpu
from jax.sharding import PartitionSpec as P

epsilon = 1e-05


def shifted(array, axis, by):
    peers = lax.axis_size(axis)
    return lax.ppermute(array, axis, [(i, (i + by) % peers) for i in range(peers)])


def layer_norm(tokens, gain):
    values = tokens.astype(jnp.float32)
    average = jnp.mean(values, -1, keepdims=True)
    centered = values - average
    variance = jnp.mean(centered * centered, -1, keepdims=True)
    return (centered * lax.rsqrt(variance + epsilon) * gain).astype(jnp.bfloat16)


def feed_forward(tokens, gain, up_matrix, down_matrix):
    normed = layer_norm(tokens, gain)
    hidden = jax.nn.gelu(jnp.dot(normed, up_matrix, preferred_element_type=jnp.float32)).astype(
        jnp.bfloat16
    )
    total = tokens.astype(jnp.float32) + jnp.dot(
        hidden, down_matrix, preferred_element_type=jnp.float32
    )
    return total.astype(jnp.bfloat16)


def edge_label(index, extent):
    return jnp.where(index < 4, 2, jnp.where(index >= extent - 4, 1, 0)).astype(jnp.int32)


def head_masks(heads, channels):
    owner = jnp.arange(channels, dtype=jnp.int32) // (channels // heads)
    return (owner[None, :] == jnp.arange(heads, dtype=jnp.int32)[:, None]).astype(jnp.bfloat16)


def window_attention(
    row_block, first_row, height, channels, norm_gains, qkv_weight, out_weight, window_bias
):
    count = row_block.shape[0]
    columns = row_block.shape[1] // channels
    heads = window_bias.shape[0]
    head_size = channels // heads
    masks = head_masks(heads, channels)
    rolled = jnp.roll(row_block, -4 * channels, axis=1)
    windowed = rolled.reshape(count // 8, 8, columns // 8, 8 * channels).transpose(0, 2, 1, 3)
    normed = layer_norm(windowed.reshape(-1, channels), norm_gains[0])
    packed = jnp.dot(normed, qkv_weight[0], preferred_element_type=jnp.float32).astype(jnp.bfloat16)
    packed = packed.reshape(-1, 64, 3 * channels)
    queries = packed[:, :, :channels]
    keys = packed[:, :, channels : 2 * channels]
    values = packed[:, :, 2 * channels :]
    initial_rows = jnp.mod(first_row + jnp.arange(count, dtype=jnp.int32), height)
    initial_columns = jnp.mod(jnp.arange(columns, dtype=jnp.int32) + 4, columns)
    labels = (
        edge_label(initial_rows, height)[:, None] * 3
        + edge_label(initial_columns, columns)[None, :]
    )
    window_labels = (
        labels.reshape(count // 8, 8, columns // 8, 8).transpose(0, 2, 1, 3).reshape(-1, 64)
    )
    allowed = window_labels[:, :, None] == window_labels[:, None, :]
    head_queries = queries[:, None] * masks[None, :, None, :]
    scores = jnp.einsum("nhqc,nkc->nhqk", head_queries, keys, preferred_element_type=jnp.float32)
    scores = scores * head_size ** (-0.5) + window_bias[None]
    scores = jnp.where(allowed[:, None], scores, -jnp.inf)
    weights = jax.nn.softmax(scores, axis=-1).astype(jnp.bfloat16)
    head_values = values[:, None] * masks[None, :, None, :]
    attended = jnp.einsum(
        "nhqk,nhkc->nqc", weights, head_values, preferred_element_type=jnp.float32
    ).astype(jnp.bfloat16)
    lateral = jnp.dot(
        attended.reshape(-1, channels), out_weight[0], preferred_element_type=jnp.float32
    ).astype(jnp.bfloat16)
    lateral = lateral.reshape(count // 8, columns // 8, 8, 8 * channels).transpose(0, 2, 1, 3)
    return jnp.roll(lateral.reshape(count, columns * channels), 4 * channels, axis=1)


def axial_block(pencils, norm_gains, qkv_weight, out_weight, up_weight, down_weight, heads):
    planes, count, channels = pencils.shape
    head_size = channels // heads
    masks = head_masks(heads, channels)
    flat = jnp.transpose(pencils, (1, 0, 2)).reshape(-1, channels)
    normed = layer_norm(flat, norm_gains[2])
    packed = jnp.dot(normed, qkv_weight[1], preferred_element_type=jnp.float32).astype(jnp.bfloat16)
    packed = packed.reshape(count, planes, 3 * channels)
    queries = packed[:, :, :channels]
    keys = packed[:, :, channels : 2 * channels]
    values = packed[:, :, 2 * channels :]
    head_queries = queries[:, None] * masks[None, :, None, :]
    scores = jnp.einsum("phzc,pyc->phzy", head_queries, keys, preferred_element_type=jnp.float32)
    weights = jax.nn.softmax(scores * head_size ** (-0.5), axis=-1).astype(jnp.bfloat16)
    head_values = values[:, None] * masks[None, :, None, :]
    attended = jnp.einsum(
        "phzy,phyc->pzc", weights, head_values, preferred_element_type=jnp.float32
    ).astype(jnp.bfloat16)
    projected = jnp.dot(
        attended.reshape(-1, channels), out_weight[1], preferred_element_type=jnp.float32
    ).astype(jnp.bfloat16)
    after = (flat.astype(jnp.float32) + projected.astype(jnp.float32)).astype(jnp.bfloat16)
    mixed = feed_forward(after, norm_gains[3], up_weight[1], down_weight[1]).reshape(
        count, planes, channels
    )
    return jnp.transpose(mixed, (1, 0, 2))


def general_body(volume, norm_gains, qkv_weight, out_weight, up_weight, down_weight, window_bias):
    rows_here = volume.shape[1]
    row_width = volume.shape[2]
    channels = norm_gains.shape[1]
    heads = window_bias.shape[0]
    height = rows_here * lax.axis_size("tile")
    tile_start = lax.axis_index("tile") * rows_here
    plane = volume.reshape(rows_here, row_width)
    next_rows = shifted(plane[:4], "tile", -1)
    extended = jnp.concatenate([plane[4:], next_rows], 0)
    attended = window_attention(
        extended, tile_start + 4, height, channels, norm_gains, qkv_weight, out_weight, window_bias
    )
    tail_rows = shifted(attended[-4:], "tile", 1)
    lateral = jnp.concatenate([tail_rows, attended[:-4]], 0)
    middle = (
        (plane.astype(jnp.float32) + lateral.astype(jnp.float32))
        .astype(jnp.bfloat16)
        .reshape(-1, channels)
    )
    planes = lax.axis_size("gz")
    middle = feed_forward(middle, norm_gains[1], up_weight[0], down_weight[0])
    grouped = middle.reshape(planes, -1, channels)
    pencils = lax.all_to_all(grouped, "gz", split_axis=0, concat_axis=0, tiled=True)
    returned = lax.all_to_all(
        axial_block(pencils, norm_gains, qkv_weight, out_weight, up_weight, down_weight, heads),
        "gz",
        split_axis=0,
        concat_axis=0,
        tiled=True,
    )
    return returned.reshape(1, rows_here, row_width)


LOG2E = 1.4426950408889634


def normalised(tokens):
    average = jnp.mean(tokens, 0, keepdims=True)
    centered = tokens - average
    variance = jnp.mean(centered * centered, 0, keepdims=True)
    return (centered * lax.rsqrt(variance + epsilon)).astype(jnp.bfloat16)


def product(left, right):
    return jnp.dot(left, right, preferred_element_type=jnp.float32)


GELU_IN = 0.035677408136300125 ** (1 / 3)
GELU_LINEAR = 0.7978845608028654 / GELU_IN
GELU_OUT = 0.5 / GELU_IN


def across(left, right):
    return lax.dot_general(left, right, (((1,), (1,)), ((), ())), preferred_element_type=jnp.float32)


def gated(scaled):
    scaled = scaled.astype(jnp.bfloat16)
    return scaled + scaled * jnp.tanh(scaled * (GELU_LINEAR + scaled * scaled))


def pack_kernel(volume_ref, gains_ref, packed_ref, held_gains_ref, rows_ref, sems):
    windows, channels, _ = packed_ref.shape
    width = 8 * channels
    half = width // 2
    copies = [
        pltpu.make_async_copy(volume_ref, rows_ref, sems.at[0]),
        pltpu.make_async_copy(gains_ref, held_gains_ref, sems.at[1]),
    ]
    for copy in copies:
        copy.start()
    for copy in copies:
        copy.wait()
    tokens = []
    for window in range(windows):
        start = window * width + half
        if window < windows - 1:
            chunk = rows_ref[:, start : start + width]
        else:
            chunk = jnp.concatenate([rows_ref[:, start:], rows_ref[:, :half]], axis=1)
        rolled = jnp.concatenate([chunk[4:], chunk[:4]], axis=0)
        pieces = [rolled[:, channels * column : channels * (column + 1)] for column in range(8)]
        tokens.append(jnp.concatenate(pieces, axis=0))
    for window in range(windows):
        packed_ref[window] = tokens[window].T


def unpack_kernel(packed_ref, volume_ref, rows_ref, sems):
    windows, channels, _ = packed_ref.shape
    width = 8 * channels
    half = width // 2
    tokens = [packed_ref[window].T for window in range(windows)]
    for window in range(windows):
        rows = jnp.concatenate([tokens[window][16 * column : 16 * column + 16] for column in range(8)], axis=1)
        rows = jnp.concatenate([rows[12:], rows[:12]], axis=0)
        start = window * width + half
        if window < windows - 1:
            rows_ref[:, start : start + width] = rows
        else:
            rows_ref[:, start:] = rows[:, :half]
            rows_ref[:, :half] = rows[:, half:]
    copy = pltpu.make_async_copy(rows_ref, volume_ref, sems.at[0])
    copy.start()
    copy.wait()


LAG = 4


def in_lockstep(stages, planes):
    for group in stages:
        group = group if isinstance(group, tuple) else (group,)
        for step in range(planes + LAG * (len(group) - 1)):
            for index, stage in enumerate(group):
                if 0 <= step - LAG * index < planes:
                    stage(step - LAG * index)


def blocks_kernel(
    tokens_ref,
    gains_ref,
    qkv_weight_ref,
    out_weight_ref,
    up_weight_ref,
    down_weight_ref,
    window_bias_ref,
    order_ref,
    result_ref,
    bias_ref,
    planar_ref,
    query_ref,
    key_ref,
    value_ref,
):
    channels = tokens_ref.shape[1]
    planes = tokens_ref.shape[0] // 2
    heads = window_bias_ref.shape[0] // 64
    head_size = channels // heads
    lane = lax.broadcasted_iota(jnp.int32, (1, 128), 1)
    own = lane % 16 < 12
    first = lane % 16 < 8
    place = lax.broadcasted_iota(jnp.int32, (channels, 128), 1)
    by_window = place % 64 // 8 * 16 + place // 64 * 8 + place % 8
    blank = jnp.zeros((128 - channels, 128), jnp.bfloat16)
    blank_rows = jnp.zeros((128 - channels, 128), jnp.float32)

    def turned(ref, layer):
        return ref[layer].astype(jnp.float32).T

    def gain(norm, scale):
        return gains_ref[norm : norm + 1, :] * scale

    def turned_qkv(layer):
        matrix = turned(qkv_weight_ref, layer)
        queries = matrix[:channels] * gain(2 * layer, LOG2E * head_size ** (-0.5))
        return jnp.concatenate([queries, matrix[channels:] * gain(2 * layer, 1.0)], axis=0).astype(jnp.bfloat16)

    qkv = [turned_qkv(layer) for layer in range(2)]
    up = [(turned(up_weight_ref, layer) * gain(2 * layer + 1, GELU_IN)).astype(jnp.bfloat16) for layer in range(2)]
    down = [(down_weight_ref[layer].astype(jnp.float32) * GELU_OUT).astype(jnp.bfloat16) for layer in range(2)]
    out = turned(out_weight_ref, 0).astype(jnp.bfloat16)
    mix = jnp.concatenate([turned(out_weight_ref, 1).astype(jnp.bfloat16)] * 2, axis=1)

    shape = (heads * planes, planes * channels // 2)
    row = lax.broadcasted_iota(jnp.int32, shape, 0)
    column = lax.broadcasted_iota(jnp.int32, shape, 1)
    mine = lax.div(column, head_size // 2) == lax.rem(row, planes) * heads + lax.div(row, planes)
    gather = jnp.where(mine, 1.0, 0.0).astype(jnp.bfloat16)

    high = window_bias_ref[...].astype(jnp.bfloat16)
    low = (window_bias_ref[...] - high.astype(jnp.float32)).astype(jnp.bfloat16)
    parts = [across(order_ref[:64, :64], part).astype(jnp.bfloat16) for part in (high, low)]
    position = lax.axis_index("gz") * lax.axis_size("tile") + lax.axis_index("tile")
    last = position == lax.axis_size("gz") * lax.axis_size("tile") - 1
    key_row = lax.broadcasted_iota(jnp.int32, (64, 128), 0)
    query_lane = lax.broadcasted_iota(jnp.int32, (64, 128), 1)
    column_cut = ((key_row < 32) != (query_lane < 64)) & last
    row_cut = ((key_row % 8 < 4) != (query_lane % 8 < 4)) & (query_lane % 16 >= 8)
    for head in range(heads):
        placed = order_ref[64 + 128 * head : 64 + 128 * (head + 1), :]
        plain = (across(parts[0], placed) + across(parts[1], placed)) * LOG2E
        plain = jnp.where(column_cut, -jnp.inf, plain)
        bias_ref[0, 64 * head : 64 * (head + 1), :] = plain
        bias_ref[1, 64 * head : 64 * (head + 1), :] = jnp.where(row_cut, -jnp.inf, plain)

    held = [{} for _ in range(planes)]
    tops, totals = [], []

    def rows_of(plane):
        return slice(plane * channels, (plane + 1) * channels)

    def load(plane):
        one, two = tokens_ref[2 * plane], tokens_ref[2 * plane + 1]
        tokens = jnp.concatenate([jnp.where(own, one, two), jnp.where(own, two, one)], axis=1)
        held[plane]["x"] = tokens.astype(jnp.float32)

    def norm(plane):
        held[plane]["n"] = normalised(held[plane]["x"])

    def lateral_qkv(plane):
        packed = product(qkv[0], held[plane].pop("n"))
        held[plane]["q"] = packed[:channels]
        held[plane]["k"] = packed[channels : 2 * channels]
        values = packed[2 * channels :]
        held[plane]["v"] = []
        for lanes in (slice(0, 128), slice(128, 256)):
            ordered = jnp.take_along_axis(values[:, lanes], by_window, axis=1, mode="promise_in_bounds")
            held[plane]["v"].append((ordered[:, :64].astype(jnp.bfloat16), ordered[:, 64:].astype(jnp.bfloat16)))

    def lateral_scores(plane):
        queries, keys = held[plane].pop("q"), held[plane].pop("k")
        scores = []
        for pair in range(2):
            lanes = slice(128 * pair, 128 * pair + 128)
            query = queries[:, lanes]
            right = jnp.concatenate(
                [
                    jnp.where(first, query, 0.0).astype(jnp.bfloat16),
                    blank,
                    jnp.where(first, 0.0, query).astype(jnp.bfloat16),
                    blank,
                ],
                axis=0,
            )
            key = jnp.concatenate([keys[:, lanes], blank_rows], axis=0).T
            left = []
            for head in range(heads):
                masked = jnp.where(lane // head_size == head, key, 0.0).reshape(8, 2, 8, 128)
                windows = [masked[:, window].reshape(64, 128).astype(jnp.bfloat16) for window in range(2)]
                left.append(jnp.concatenate(windows, axis=1))
            scores.append((jnp.concatenate(left, axis=0), right))
        held[plane]["s"] = scores

    def lateral_weights(plane):
        scores = held[plane].pop("s")
        held[plane]["w"] = []
        for pair in range(2):
            for head in range(heads):
                own_scores = scores[pair][64 * head : 64 * head + 64]
                weights = jnp.exp2(own_scores - jnp.max(own_scores, axis=0, keepdims=True))
                total = jnp.sum(weights, axis=0, keepdims=True)
                held[plane]["w"].append((weights.astype(jnp.bfloat16), 1.0 / total))

    def lateral_products(plane):
        held[plane]["s"] = [product(*held[plane]["s"][pair]) + bias_ref[pair] for pair in range(2)]

    def lateral_values(plane):
        weights, values = held[plane].pop("w"), held[plane].pop("v")
        attended = []
        for pair in range(2):
            mixed = []
            for head in range(heads):
                own_weights, inverse = weights[heads * pair + head]
                rows = slice(head_size * head, head_size * (head + 1))
                both = product(jnp.concatenate([values[pair][0][rows], values[pair][1][rows]], axis=0), own_weights)
                own_mixed = jnp.where(first, both[:head_size], both[head_size:])
                mixed.append((own_mixed * inverse).astype(jnp.bfloat16))
            attended.append(jnp.concatenate(mixed, axis=0))
        held[plane]["a"] = jnp.concatenate(attended, axis=1)

    def lateral_out(plane):
        held[plane]["x"] = held[plane]["x"] + product(out, held[plane].pop("a"))

    def raised(layer):
        def stage(plane):
            held[plane]["h"] = product(up[layer], held[plane].pop("n"))

        return stage

    def gelu(plane):
        held[plane]["g"] = gated(held[plane].pop("h"))

    def lowered(layer):
        def stage(plane):
            held[plane]["x"] = held[plane]["x"] + product(down[layer], held[plane].pop("g"))

        return stage

    def axial_qkv(plane):
        packed = product(qkv[1], held[plane].pop("n")).astype(jnp.bfloat16)
        planar_ref[rows_of(plane), :] = held[plane].pop("x")
        query_ref[rows_of(plane), :] = packed[:channels]
        key_ref[rows_of(plane), :] = packed[channels : 2 * channels]
        value_ref[rows_of(plane), :] = packed[2 * channels :]

    def axial_scores(other):
        key = key_ref[rows_of(other), :]
        half = head_size // 2
        pairs = []
        for plane in range(planes):
            pair = query_ref[rows_of(plane), :] * key
            for head in range(heads):
                top = head_size * head
                pairs.append(pair[top : top + half] + pair[top + half : top + head_size])
        held[other]["s"] = product(gather, jnp.concatenate(pairs, axis=0))

    def axial_top(plane):
        scores = held[plane]["s"]
        tops.append(scores if plane == 0 else jnp.maximum(tops[-1], scores))

    def axial_exponentials(plane):
        held[plane]["s"] = jnp.exp2(held[plane]["s"] - tops[-1])
        totals.append(held[plane]["s"] if plane == 0 else totals[-1] + held[plane]["s"])

    def axial_weights(plane):
        if plane == 0:
            totals.append(1.0 / totals[-1])
        held[plane]["w"] = held[plane].pop("s") * totals[-1]

    def axial_values(plane):
        spread = []
        for other in range(planes):
            weights = held[other]["w"]
            wide = jnp.concatenate(
                [
                    jnp.broadcast_to(weights[planes * head + plane][None], (head_size, 256)).astype(jnp.bfloat16)
                    for head in range(heads)
                ],
                axis=0,
            )
            spread.append(wide * value_ref[rows_of(other), :])
        while len(spread) > 2:
            spread = [one + two for one, two in zip(spread[::2], spread[1::2])]
        spread = jnp.concatenate(spread, axis=0)
        held[plane]["x"] = planar_ref[rows_of(plane), :] + product(mix, spread)

    def store(plane):
        mixed = held[plane].pop("x").astype(jnp.bfloat16)
        one, two = mixed[:, :128], mixed[:, 128:]
        result_ref[2 * plane] = jnp.where(own, one, two)
        result_ref[2 * plane + 1] = jnp.where(own, two, one)

    lateral = [load, norm, lateral_qkv, lateral_scores, (lateral_products, lateral_weights, lateral_values, lateral_out)]
    lateral += [norm, (raised(0), gelu, lowered(0)), norm, axial_qkv]
    axial = [axial_scores, axial_top, axial_exponentials, axial_weights, axial_values, norm, (raised(1), gelu, lowered(1)), store]
    in_lockstep(lateral + axial, planes)


def pack(rows, gains, windows):
    return pl.pallas_call(
        pack_kernel,
        out_shape=(
            jax.ShapeDtypeStruct((windows, gains.shape[1], 128), jnp.bfloat16),
            jax.ShapeDtypeStruct(gains.shape, gains.dtype),
        ),
        in_specs=[pl.BlockSpec(memory_space=pltpu.HBM)] * 2,
        scratch_shapes=[pltpu.VMEM(rows.shape, rows.dtype), pltpu.SemaphoreType.DMA((2,))],
        compiler_params=pltpu.CompilerParams(vmem_limit_bytes=16 * 1024 * 1024),
        name="pack_windows",
    )(*(pltpu.with_memory_space_constraint(operand, pltpu.HBM) for operand in (rows, gains)))


def unpack(packed, rows, width):
    return pl.pallas_call(
        unpack_kernel,
        out_shape=jax.ShapeDtypeStruct((rows, width), jnp.bfloat16),
        out_specs=pl.BlockSpec(memory_space=pltpu.HBM),
        scratch_shapes=[pltpu.VMEM((rows, width), jnp.bfloat16), pltpu.SemaphoreType.DMA((1,))],
        compiler_params=pltpu.CompilerParams(vmem_limit_bytes=16 * 1024 * 1024),
        name="unpack_windows",
    )(packed)


def blocks(tokens, *operands):
    sources, channels, _ = tokens.shape
    rows = sources // 2 * channels
    heads = operands[5].shape[0] // 64
    return pl.pallas_call(
        blocks_kernel,
        out_shape=jax.ShapeDtypeStruct(tokens.shape, jnp.bfloat16),
        scratch_shapes=[
            pltpu.VMEM((2, heads * 64, 128), jnp.float32),
            pltpu.VMEM((rows, 256), jnp.float32),
            pltpu.VMEM((rows, 256), jnp.bfloat16),
            pltpu.VMEM((rows, 256), jnp.bfloat16),
            pltpu.VMEM((rows, 256), jnp.bfloat16),
        ],
        compiler_params=pltpu.CompilerParams(vmem_limit_bytes=40 * 1024 * 1024),
        name="both_blocks",
    )(tokens, *operands)


def token_order(heads):
    index = np.arange(64)
    order = np.zeros((64, heads * 64), np.float32)
    order[index, index % 8 * 8 + index // 8] = 1.0
    lane = np.arange(128)
    placed = np.zeros((heads, 128, heads, 64), np.float32)
    for head in range(heads):
        placed[head, lane, head, lane % 8 * 8 + lane // 16] = 1.0
    return np.concatenate([order, placed.reshape(heads * 128, heads * 64)]).astype(jnp.bfloat16)


def window_body(volume, norm_gains, qkv_weight, out_weight, up_weight, down_weight, window_bias):
    rows = volume.shape[1]
    width = volume.shape[2]
    channels = norm_gains.shape[1]
    heads = window_bias.shape[0]
    planes = lax.axis_size("gz")
    windows = width // channels // 8
    packed, held_gains = pack(volume.reshape(rows, width), norm_gains, windows)
    tokens = lax.all_to_all(packed, ("gz", "tile"), split_axis=0, concat_axis=0, tiled=True)
    mixed = blocks(
        tokens,
        held_gains,
        qkv_weight,
        out_weight,
        up_weight,
        jnp.transpose(down_weight, (0, 2, 1)),
        window_bias.reshape(heads * 64, 64),
        token_order(heads),
    )
    returned = lax.all_to_all(mixed, ("gz", "tile"), split_axis=0, concat_axis=0, tiled=True)
    return unpack(returned, rows, width).reshape(1, rows, width)


def fits_windows(mesh, volume, norm_gains, window_bias):
    planes, tiles = mesh.shape["gz"], mesh.shape["tile"]
    channels, heads = norm_gains.shape[1], window_bias.shape[0]
    return (
        tiles == 2
        and planes == 8
        and volume.shape[1] == 16 * tiles
        and volume.shape[2] == 8 * channels * planes * tiles
        and channels == 96
        and heads == 3
    )


def solution(mesh):
    placed = (P(("groups", "gz"), "tile", None), P(), P(), P(), P(), P(), P())

    def run(volume, norm_gains, *weights):
        chosen = window_body if fits_windows(mesh, volume, norm_gains, weights[-1]) else general_body
        return jax.shard_map(
            chosen,
            mesh=mesh,
            in_specs=placed,
            out_specs=P(("groups", "gz"), "tile", None),
            check_vma=False,
        )(volume, norm_gains, *weights)

    return run
```

```python
import jax
import jax.numpy as jnp
import numpy as np
from jax import lax
from jax.experimental import pallas as pl
from jax.experimental.pallas import tpu as pltpu
from jax.sharding import PartitionSpec as P

epsilon = 1e-05


def shifted(array, axis, by):
    peers = lax.axis_size(axis)
    return lax.ppermute(array, axis, [(i, (i + by) % peers) for i in range(peers)])


def layer_norm(tokens, gain):
    values = tokens.astype(jnp.float32)
    average = jnp.mean(values, -1, keepdims=True)
    centered = values - average
    variance = jnp.mean(centered * centered, -1, keepdims=True)
    return (centered * lax.rsqrt(variance + epsilon) * gain).astype(jnp.bfloat16)


def feed_forward(tokens, gain, up_matrix, down_matrix):
    normed = layer_norm(tokens, gain)
    hidden = jax.nn.gelu(jnp.dot(normed, up_matrix, preferred_element_type=jnp.float32)).astype(
        jnp.bfloat16
    )
    total = tokens.astype(jnp.float32) + jnp.dot(
        hidden, down_matrix, preferred_element_type=jnp.float32
    )
    return total.astype(jnp.bfloat16)


def edge_label(index, extent):
    return jnp.where(index < 4, 2, jnp.where(index >= extent - 4, 1, 0)).astype(jnp.int32)


def head_masks(heads, channels):
    owner = jnp.arange(channels, dtype=jnp.int32) // (channels // heads)
    return (owner[None, :] == jnp.arange(heads, dtype=jnp.int32)[:, None]).astype(jnp.bfloat16)


def window_attention(
    row_block, first_row, height, channels, norm_gains, qkv_weight, out_weight, window_bias
):
    count = row_block.shape[0]
    columns = row_block.shape[1] // channels
    heads = window_bias.shape[0]
    head_size = channels // heads
    masks = head_masks(heads, channels)
    rolled = jnp.roll(row_block, -4 * channels, axis=1)
    windowed = rolled.reshape(count // 8, 8, columns // 8, 8 * channels).transpose(0, 2, 1, 3)
    normed = layer_norm(windowed.reshape(-1, channels), norm_gains[0])
    packed = jnp.dot(normed, qkv_weight[0], preferred_element_type=jnp.float32).astype(jnp.bfloat16)
    packed = packed.reshape(-1, 64, 3 * channels)
    queries = packed[:, :, :channels]
    keys = packed[:, :, channels : 2 * channels]
    values = packed[:, :, 2 * channels :]
    initial_rows = jnp.mod(first_row + jnp.arange(count, dtype=jnp.int32), height)
    initial_columns = jnp.mod(jnp.arange(columns, dtype=jnp.int32) + 4, columns)
    labels = (
        edge_label(initial_rows, height)[:, None] * 3
        + edge_label(initial_columns, columns)[None, :]
    )
    window_labels = (
        labels.reshape(count // 8, 8, columns // 8, 8).transpose(0, 2, 1, 3).reshape(-1, 64)
    )
    allowed = window_labels[:, :, None] == window_labels[:, None, :]
    head_queries = queries[:, None] * masks[None, :, None, :]
    scores = jnp.einsum("nhqc,nkc->nhqk", head_queries, keys, preferred_element_type=jnp.float32)
    scores = scores * head_size ** (-0.5) + window_bias[None]
    scores = jnp.where(allowed[:, None], scores, -jnp.inf)
    weights = jax.nn.softmax(scores, axis=-1).astype(jnp.bfloat16)
    head_values = values[:, None] * masks[None, :, None, :]
    attended = jnp.einsum(
        "nhqk,nhkc->nqc", weights, head_values, preferred_element_type=jnp.float32
    ).astype(jnp.bfloat16)
    lateral = jnp.dot(
        attended.reshape(-1, channels), out_weight[0], preferred_element_type=jnp.float32
    ).astype(jnp.bfloat16)
    lateral = lateral.reshape(count // 8, columns // 8, 8, 8 * channels).transpose(0, 2, 1, 3)
    return jnp.roll(lateral.reshape(count, columns * channels), 4 * channels, axis=1)


def axial_block(pencils, norm_gains, qkv_weight, out_weight, up_weight, down_weight, heads):
    planes, count, channels = pencils.shape
    head_size = channels // heads
    masks = head_masks(heads, channels)
    flat = jnp.transpose(pencils, (1, 0, 2)).reshape(-1, channels)
    normed = layer_norm(flat, norm_gains[2])
    packed = jnp.dot(normed, qkv_weight[1], preferred_element_type=jnp.float32).astype(jnp.bfloat16)
    packed = packed.reshape(count, planes, 3 * channels)
    queries = packed[:, :, :channels]
    keys = packed[:, :, channels : 2 * channels]
    values = packed[:, :, 2 * channels :]
    head_queries = queries[:, None] * masks[None, :, None, :]
    scores = jnp.einsum("phzc,pyc->phzy", head_queries, keys, preferred_element_type=jnp.float32)
    weights = jax.nn.softmax(scores * head_size ** (-0.5), axis=-1).astype(jnp.bfloat16)
    head_values = values[:, None] * masks[None, :, None, :]
    attended = jnp.einsum(
        "phzy,phyc->pzc", weights, head_values, preferred_element_type=jnp.float32
    ).astype(jnp.bfloat16)
    projected = jnp.dot(
        attended.reshape(-1, channels), out_weight[1], preferred_element_type=jnp.float32
    ).astype(jnp.bfloat16)
    after = (flat.astype(jnp.float32) + projected.astype(jnp.float32)).astype(jnp.bfloat16)
    mixed = feed_forward(after, norm_gains[3], up_weight[1], down_weight[1]).reshape(
        count, planes, channels
    )
    return jnp.transpose(mixed, (1, 0, 2))


def general_body(volume, norm_gains, qkv_weight, out_weight, up_weight, down_weight, window_bias):
    rows_here = volume.shape[1]
    row_width = volume.shape[2]
    channels = norm_gains.shape[1]
    heads = window_bias.shape[0]
    height = rows_here * lax.axis_size("tile")
    tile_start = lax.axis_index("tile") * rows_here
    plane = volume.reshape(rows_here, row_width)
    next_rows = shifted(plane[:4], "tile", -1)
    extended = jnp.concatenate([plane[4:], next_rows], 0)
    attended = window_attention(
        extended, tile_start + 4, height, channels, norm_gains, qkv_weight, out_weight, window_bias
    )
    tail_rows = shifted(attended[-4:], "tile", 1)
    lateral = jnp.concatenate([tail_rows, attended[:-4]], 0)
    middle = (
        (plane.astype(jnp.float32) + lateral.astype(jnp.float32))
        .astype(jnp.bfloat16)
        .reshape(-1, channels)
    )
    planes = lax.axis_size("gz")
    middle = feed_forward(middle, norm_gains[1], up_weight[0], down_weight[0])
    grouped = middle.reshape(planes, -1, channels)
    pencils = lax.all_to_all(grouped, "gz", split_axis=0, concat_axis=0, tiled=True)
    returned = lax.all_to_all(
        axial_block(pencils, norm_gains, qkv_weight, out_weight, up_weight, down_weight, heads),
        "gz",
        split_axis=0,
        concat_axis=0,
        tiled=True,
    )
    return returned.reshape(1, rows_here, row_width)


LOG2E = 1.4426950408889634


def normalised(tokens):
    average = jnp.mean(tokens, 0, keepdims=True)
    centered = tokens - average
    variance = jnp.mean(centered * centered, 0, keepdims=True)
    return (centered * lax.rsqrt(variance + epsilon)).astype(jnp.bfloat16)


def product(left, right):
    return jnp.dot(left, right, preferred_element_type=jnp.float32)


GELU_IN = 0.035677408136300125 ** (1 / 3)
GELU_LINEAR = 0.7978845608028654 / GELU_IN
GELU_OUT = 0.5 / GELU_IN


def across(left, right):
    return lax.dot_general(left, right, (((1,), (1,)), ((), ())), preferred_element_type=jnp.float32)


def gated(scaled):
    scaled = scaled.astype(jnp.bfloat16)
    return scaled + scaled * jnp.tanh(scaled * (GELU_LINEAR + scaled * scaled))


def pack_kernel(volume_ref, gains_ref, packed_ref, held_gains_ref, rows_ref, sems):
    windows, _, width = packed_ref.shape
    half = width // 2
    copies = [
        pltpu.make_async_copy(volume_ref, rows_ref, sems.at[0]),
        pltpu.make_async_copy(gains_ref, held_gains_ref, sems.at[1]),
    ]
    for copy in copies:
        copy.start()
    for copy in copies:
        copy.wait()
    for window in range(windows):
        start = window * width + half
        if window < windows - 1:
            chunk = rows_ref[:, start : start + width]
        else:
            chunk = jnp.concatenate([rows_ref[:, start:], rows_ref[:, :half]], axis=1)
        packed_ref[window] = jnp.concatenate([chunk[4:], chunk[:4]], axis=0)


def unpack_kernel(packed_ref, volume_ref, rows_ref, sems):
    windows, _, width = packed_ref.shape
    half = width // 2
    for window in range(windows):
        chunk = packed_ref[window]
        rows = jnp.concatenate([chunk[12:], chunk[:12]], axis=0)
        start = window * width + half
        if window < windows - 1:
            rows_ref[:, start : start + width] = rows
        else:
            rows_ref[:, start:] = rows[:, :half]
            rows_ref[:, :half] = rows[:, half:]
    copy = pltpu.make_async_copy(rows_ref, volume_ref, sems.at[0])
    copy.start()
    copy.wait()


LAG = 4


def in_lockstep(stages, planes):
    for group in stages:
        group = group if isinstance(group, tuple) else (group,)
        for step in range(planes + LAG * (len(group) - 1)):
            for index, stage in enumerate(group):
                if 0 <= step - LAG * index < planes:
                    stage(step - LAG * index)


def blocks_kernel(
    tokens_ref,
    gains_ref,
    qkv_weight_ref,
    out_weight_ref,
    up_weight_ref,
    down_weight_ref,
    window_bias_ref,
    order_ref,
    result_ref,
    bias_ref,
    planar_ref,
    query_ref,
    key_ref,
    value_ref,
):
    channels = gains_ref.shape[1]
    planes = tokens_ref.shape[0] // 2
    heads = window_bias_ref.shape[0] // 64
    head_size = channels // heads
    lane = lax.broadcasted_iota(jnp.int32, (1, 128), 1)
    own = lane % 16 < 12
    first = lane % 16 < 8
    place = lax.broadcasted_iota(jnp.int32, (channels, 128), 1)
    by_window = place % 64 // 8 * 16 + place // 64 * 8 + place % 8
    blank = jnp.zeros((128 - channels, 128), jnp.bfloat16)
    blank_rows = jnp.zeros((128 - channels, 128), jnp.float32)

    def turned(ref, layer):
        return ref[layer].astype(jnp.float32).T

    def gain(norm, scale):
        return gains_ref[norm : norm + 1, :] * scale

    def turned_qkv(layer):
        matrix = turned(qkv_weight_ref, layer)
        queries = matrix[:channels] * gain(2 * layer, LOG2E * head_size ** (-0.5))
        return jnp.concatenate([queries, matrix[channels:] * gain(2 * layer, 1.0)], axis=0).astype(jnp.bfloat16)

    qkv = [turned_qkv(layer) for layer in range(2)]
    up = [(turned(up_weight_ref, layer) * gain(2 * layer + 1, GELU_IN)).astype(jnp.bfloat16) for layer in range(2)]
    down = [(down_weight_ref[layer].astype(jnp.float32) * GELU_OUT).astype(jnp.bfloat16) for layer in range(2)]
    out = turned(out_weight_ref, 0).astype(jnp.bfloat16)
    mix = jnp.concatenate([turned(out_weight_ref, 1).astype(jnp.bfloat16)] * 2, axis=1)

    shape = (heads * planes, planes * channels // 2)
    row = lax.broadcasted_iota(jnp.int32, shape, 0)
    column = lax.broadcasted_iota(jnp.int32, shape, 1)
    mine = lax.div(column, head_size // 2) == lax.rem(row, planes) * heads + lax.div(row, planes)
    gather = jnp.where(mine, 1.0, 0.0).astype(jnp.bfloat16)

    high = window_bias_ref[...].astype(jnp.bfloat16)
    low = (window_bias_ref[...] - high.astype(jnp.float32)).astype(jnp.bfloat16)
    parts = [across(order_ref[:64, :64], part).astype(jnp.bfloat16) for part in (high, low)]
    position = lax.axis_index("gz") * lax.axis_size("tile") + lax.axis_index("tile")
    last = position == lax.axis_size("gz") * lax.axis_size("tile") - 1
    key_row = lax.broadcasted_iota(jnp.int32, (64, 128), 0)
    query_lane = lax.broadcasted_iota(jnp.int32, (64, 128), 1)
    column_cut = ((key_row < 32) != (query_lane < 64)) & last
    row_cut = ((key_row % 8 < 4) != (query_lane % 8 < 4)) & (query_lane % 16 >= 8)
    for head in range(heads):
        placed = order_ref[64 + 128 * head : 64 + 128 * (head + 1), :]
        plain = (across(parts[0], placed) + across(parts[1], placed)) * LOG2E
        plain = jnp.where(column_cut, -jnp.inf, plain)
        bias_ref[0, 64 * head : 64 * (head + 1), :] = plain
        bias_ref[1, 64 * head : 64 * (head + 1), :] = jnp.where(row_cut, -jnp.inf, plain)

    held = [{} for _ in range(planes)]
    tops, totals = [], []

    def rows_of(plane):
        return slice(plane * channels, (plane + 1) * channels)

    def gather_columns(plane):
        held[plane]["x"] = [
            jnp.concatenate([tokens_ref[source, :, channels * c : channels * (c + 1)] for c in range(8)], axis=0)
            for source in (2 * plane, 2 * plane + 1)
        ]

    def load(plane):
        one, two = (tokens.T for tokens in held[plane]["x"])
        tokens = jnp.concatenate([jnp.where(own, one, two), jnp.where(own, two, one)], axis=1)
        held[plane]["x"] = tokens.astype(jnp.float32)

    def norm(plane):
        held[plane]["n"] = normalised(held[plane]["x"])

    def lateral_qkv(plane):
        packed = product(qkv[0], held[plane].pop("n"))
        held[plane]["q"] = packed[:channels]
        held[plane]["k"] = packed[channels : 2 * channels]
        values = packed[2 * channels :]
        held[plane]["v"] = []
        for lanes in (slice(0, 128), slice(128, 256)):
            ordered = jnp.take_along_axis(values[:, lanes], by_window, axis=1, mode="promise_in_bounds")
            held[plane]["v"].append((ordered[:, :64].astype(jnp.bfloat16), ordered[:, 64:].astype(jnp.bfloat16)))

    def lateral_scores(plane):
        queries, keys = held[plane].pop("q"), held[plane].pop("k")
        scores = []
        for pair in range(2):
            lanes = slice(128 * pair, 128 * pair + 128)
            query = queries[:, lanes]
            right = jnp.concatenate(
                [
                    jnp.where(first, query, 0.0).astype(jnp.bfloat16),
                    blank,
                    jnp.where(first, 0.0, query).astype(jnp.bfloat16),
                    blank,
                ],
                axis=0,
            )
            key = jnp.concatenate([keys[:, lanes], blank_rows], axis=0).T
            left = []
            for head in range(heads):
                masked = jnp.where(lane // head_size == head, key, 0.0).reshape(8, 2, 8, 128)
                windows = [masked[:, window].reshape(64, 128).astype(jnp.bfloat16) for window in range(2)]
                left.append(jnp.concatenate(windows, axis=1))
            scores.append((jnp.concatenate(left, axis=0), right))
        held[plane]["s"] = scores

    def lateral_weights(plane):
        scores = held[plane].pop("s")
        held[plane]["w"] = []
        for pair in range(2):
            for head in range(heads):
                own_scores = scores[pair][64 * head : 64 * head + 64]
                weights = jnp.exp2(own_scores - jnp.max(own_scores, axis=0, keepdims=True))
                total = jnp.sum(weights, axis=0, keepdims=True)
                held[plane]["w"].append((weights.astype(jnp.bfloat16), 1.0 / total))

    def lateral_products(plane):
        held[plane]["s"] = [product(*held[plane]["s"][pair]) + bias_ref[pair] for pair in range(2)]

    def lateral_values(plane):
        weights, values = held[plane].pop("w"), held[plane].pop("v")
        attended = []
        for pair in range(2):
            mixed = []
            for head in range(heads):
                own_weights, inverse = weights[heads * pair + head]
                rows = slice(head_size * head, head_size * (head + 1))
                both = product(jnp.concatenate([values[pair][0][rows], values[pair][1][rows]], axis=0), own_weights)
                own_mixed = jnp.where(first, both[:head_size], both[head_size:])
                mixed.append((own_mixed * inverse).astype(jnp.bfloat16))
            attended.append(jnp.concatenate(mixed, axis=0))
        held[plane]["a"] = jnp.concatenate(attended, axis=1)

    def lateral_out(plane):
        held[plane]["x"] = held[plane]["x"] + product(out, held[plane].pop("a"))

    def raised(layer):
        def stage(plane):
            held[plane]["h"] = product(up[layer], held[plane].pop("n"))

        return stage

    def gelu(plane):
        held[plane]["g"] = gated(held[plane].pop("h"))

    def lowered(layer):
        def stage(plane):
            held[plane]["x"] = held[plane]["x"] + product(down[layer], held[plane].pop("g"))

        return stage

    def axial_qkv(plane):
        packed = product(qkv[1], held[plane].pop("n")).astype(jnp.bfloat16)
        planar_ref[rows_of(plane), :] = held[plane].pop("x")
        query_ref[rows_of(plane), :] = packed[:channels]
        key_ref[rows_of(plane), :] = packed[channels : 2 * channels]
        value_ref[rows_of(plane), :] = packed[2 * channels :]

    def axial_scores(other):
        key = key_ref[rows_of(other), :]
        half = head_size // 2
        pairs = []
        for plane in range(planes):
            pair = query_ref[rows_of(plane), :] * key
            for head in range(heads):
                top = head_size * head
                pairs.append(pair[top : top + half] + pair[top + half : top + head_size])
        held[other]["s"] = product(gather, jnp.concatenate(pairs, axis=0))

    def axial_top(plane):
        scores = held[plane]["s"]
        tops.append(scores if plane == 0 else jnp.maximum(tops[-1], scores))

    def axial_exponentials(plane):
        held[plane]["s"] = jnp.exp2(held[plane]["s"] - tops[-1])
        totals.append(held[plane]["s"] if plane == 0 else totals[-1] + held[plane]["s"])

    def axial_weights(plane):
        if plane == 0:
            totals.append(1.0 / totals[-1])
        held[plane]["w"] = held[plane].pop("s") * totals[-1]

    def axial_values(plane):
        spread = []
        for other in range(planes):
            weights = held[other]["w"]
            wide = jnp.concatenate(
                [
                    jnp.broadcast_to(weights[planes * head + plane][None], (head_size, 256)).astype(jnp.bfloat16)
                    for head in range(heads)
                ],
                axis=0,
            )
            spread.append(wide * value_ref[rows_of(other), :])
        while len(spread) > 2:
            spread = [one + two for one, two in zip(spread[::2], spread[1::2])]
        spread = jnp.concatenate(spread, axis=0)
        held[plane]["x"] = planar_ref[rows_of(plane), :] + product(mix, spread)

    def turn(plane):
        mixed = held[plane].pop("x").astype(jnp.bfloat16)
        one, two = mixed[:, :128], mixed[:, 128:]
        held[plane]["x"] = [jnp.where(own, one, two).T, jnp.where(own, two, one).T]

    def store(plane):
        for tile, tokens in enumerate(held[plane].pop("x")):
            rows = jnp.concatenate([tokens[16 * c : 16 * (c + 1)] for c in range(8)], axis=1)
            result_ref[2 * plane + tile] = rows

    lateral = [gather_columns, load, norm, lateral_qkv, lateral_scores, (lateral_products, lateral_weights, lateral_values, lateral_out)]
    lateral += [norm, (raised(0), gelu, lowered(0)), norm, axial_qkv]
    axial = [axial_scores, axial_top, axial_exponentials, axial_weights, axial_values, norm, (raised(1), gelu, lowered(1)), turn, store]
    in_lockstep(lateral + axial, planes)


def pack(rows, gains, windows):
    return pl.pallas_call(
        pack_kernel,
        out_shape=(
            jax.ShapeDtypeStruct((windows, rows.shape[0], rows.shape[1] // windows), jnp.bfloat16),
            jax.ShapeDtypeStruct(gains.shape, gains.dtype),
        ),
        in_specs=[pl.BlockSpec(memory_space=pltpu.HBM)] * 2,
        scratch_shapes=[pltpu.VMEM(rows.shape, rows.dtype), pltpu.SemaphoreType.DMA((2,))],
        compiler_params=pltpu.CompilerParams(vmem_limit_bytes=16 * 1024 * 1024),
        name="pack_windows",
    )(*(pltpu.with_memory_space_constraint(operand, pltpu.HBM) for operand in (rows, gains)))


def unpack(packed, rows, width):
    return pl.pallas_call(
        unpack_kernel,
        out_shape=jax.ShapeDtypeStruct((rows, width), jnp.bfloat16),
        out_specs=pl.BlockSpec(memory_space=pltpu.HBM),
        scratch_shapes=[pltpu.VMEM((rows, width), jnp.bfloat16), pltpu.SemaphoreType.DMA((1,))],
        compiler_params=pltpu.CompilerParams(vmem_limit_bytes=16 * 1024 * 1024),
        name="unpack_windows",
    )(packed)


def blocks(tokens, *operands):
    rows = tokens.shape[0] // 2 * operands[0].shape[1]
    heads = operands[5].shape[0] // 64
    return pl.pallas_call(
        blocks_kernel,
        out_shape=jax.ShapeDtypeStruct(tokens.shape, jnp.bfloat16),
        scratch_shapes=[
            pltpu.VMEM((2, heads * 64, 128), jnp.float32),
            pltpu.VMEM((rows, 256), jnp.float32),
            pltpu.VMEM((rows, 256), jnp.bfloat16),
            pltpu.VMEM((rows, 256), jnp.bfloat16),
            pltpu.VMEM((rows, 256), jnp.bfloat16),
        ],
        compiler_params=pltpu.CompilerParams(vmem_limit_bytes=40 * 1024 * 1024),
        name="both_blocks",
    )(tokens, *operands)


def token_order(heads):
    index = np.arange(64)
    order = np.zeros((64, heads * 64), np.float32)
    order[index, index % 8 * 8 + index // 8] = 1.0
    lane = np.arange(128)
    placed = np.zeros((heads, 128, heads, 64), np.float32)
    for head in range(heads):
        placed[head, lane, head, lane % 8 * 8 + lane // 16] = 1.0
    return np.concatenate([order, placed.reshape(heads * 128, heads * 64)]).astype(jnp.bfloat16)


def window_body(volume, norm_gains, qkv_weight, out_weight, up_weight, down_weight, window_bias):
    rows = volume.shape[1]
    width = volume.shape[2]
    channels = norm_gains.shape[1]
    heads = window_bias.shape[0]
    planes = lax.axis_size("gz")
    windows = width // channels // 8
    packed, held_gains = pack(volume.reshape(rows, width), norm_gains, windows)
    tokens = lax.all_to_all(packed, ("gz", "tile"), split_axis=0, concat_axis=0, tiled=True)
    mixed = blocks(
        tokens,
        held_gains,
        qkv_weight,
        out_weight,
        up_weight,
        jnp.transpose(down_weight, (0, 2, 1)),
        window_bias.reshape(heads * 64, 64),
        token_order(heads),
    )
    returned = lax.all_to_all(mixed, ("gz", "tile"), split_axis=0, concat_axis=0, tiled=True)
    return unpack(returned, rows, width).reshape(1, rows, width)


def fits_windows(mesh, volume, norm_gains, window_bias):
    planes, tiles = mesh.shape["gz"], mesh.shape["tile"]
    channels, heads = norm_gains.shape[1], window_bias.shape[0]
    return (
        tiles == 2
        and planes == 8
        and volume.shape[1] == 16 * tiles
        and volume.shape[2] == 8 * channels * planes * tiles
        and channels == 96
        and heads == 3
    )


def solution(mesh):
    placed = (P(("groups", "gz"), "tile", None), P(), P(), P(), P(), P(), P())

    def run(volume, norm_gains, *weights):
        chosen = window_body if fits_windows(mesh, volume, norm_gains, weights[-1]) else general_body
        return jax.shard_map(
            chosen,
            mesh=mesh,
            in_specs=placed,
            out_specs=P(("groups", "gz"), "tile", None),
            check_vma=False,
        )(volume, norm_gains, *weights)

    return run
```

```python
import jax
import jax.numpy as jnp
import numpy as np
from jax import lax
from jax.experimental import pallas as pl
from jax.experimental.pallas import tpu as pltpu
from jax.sharding import PartitionSpec as P

epsilon = 1e-05


def shifted(array, axis, by):
    peers = lax.axis_size(axis)
    return lax.ppermute(array, axis, [(i, (i + by) % peers) for i in range(peers)])


def layer_norm(tokens, gain):
    values = tokens.astype(jnp.float32)
    average = jnp.mean(values, -1, keepdims=True)
    centered = values - average
    variance = jnp.mean(centered * centered, -1, keepdims=True)
    return (centered * lax.rsqrt(variance + epsilon) * gain).astype(jnp.bfloat16)


def feed_forward(tokens, gain, up_matrix, down_matrix):
    normed = layer_norm(tokens, gain)
    hidden = jax.nn.gelu(jnp.dot(normed, up_matrix, preferred_element_type=jnp.float32)).astype(
        jnp.bfloat16
    )
    total = tokens.astype(jnp.float32) + jnp.dot(
        hidden, down_matrix, preferred_element_type=jnp.float32
    )
    return total.astype(jnp.bfloat16)


def edge_label(index, extent):
    return jnp.where(index < 4, 2, jnp.where(index >= extent - 4, 1, 0)).astype(jnp.int32)


def head_masks(heads, channels):
    owner = jnp.arange(channels, dtype=jnp.int32) // (channels // heads)
    return (owner[None, :] == jnp.arange(heads, dtype=jnp.int32)[:, None]).astype(jnp.bfloat16)


def window_attention(
    row_block, first_row, height, channels, norm_gains, qkv_weight, out_weight, window_bias
):
    count = row_block.shape[0]
    columns = row_block.shape[1] // channels
    heads = window_bias.shape[0]
    head_size = channels // heads
    masks = head_masks(heads, channels)
    rolled = jnp.roll(row_block, -4 * channels, axis=1)
    windowed = rolled.reshape(count // 8, 8, columns // 8, 8 * channels).transpose(0, 2, 1, 3)
    normed = layer_norm(windowed.reshape(-1, channels), norm_gains[0])
    packed = jnp.dot(normed, qkv_weight[0], preferred_element_type=jnp.float32).astype(jnp.bfloat16)
    packed = packed.reshape(-1, 64, 3 * channels)
    queries = packed[:, :, :channels]
    keys = packed[:, :, channels : 2 * channels]
    values = packed[:, :, 2 * channels :]
    initial_rows = jnp.mod(first_row + jnp.arange(count, dtype=jnp.int32), height)
    initial_columns = jnp.mod(jnp.arange(columns, dtype=jnp.int32) + 4, columns)
    labels = (
        edge_label(initial_rows, height)[:, None] * 3
        + edge_label(initial_columns, columns)[None, :]
    )
    window_labels = (
        labels.reshape(count // 8, 8, columns // 8, 8).transpose(0, 2, 1, 3).reshape(-1, 64)
    )
    allowed = window_labels[:, :, None] == window_labels[:, None, :]
    head_queries = queries[:, None] * masks[None, :, None, :]
    scores = jnp.einsum("nhqc,nkc->nhqk", head_queries, keys, preferred_element_type=jnp.float32)
    scores = scores * head_size ** (-0.5) + window_bias[None]
    scores = jnp.where(allowed[:, None], scores, -jnp.inf)
    weights = jax.nn.softmax(scores, axis=-1).astype(jnp.bfloat16)
    head_values = values[:, None] * masks[None, :, None, :]
    attended = jnp.einsum(
        "nhqk,nhkc->nqc", weights, head_values, preferred_element_type=jnp.float32
    ).astype(jnp.bfloat16)
    lateral = jnp.dot(
        attended.reshape(-1, channels), out_weight[0], preferred_element_type=jnp.float32
    ).astype(jnp.bfloat16)
    lateral = lateral.reshape(count // 8, columns // 8, 8, 8 * channels).transpose(0, 2, 1, 3)
    return jnp.roll(lateral.reshape(count, columns * channels), 4 * channels, axis=1)


def axial_block(pencils, norm_gains, qkv_weight, out_weight, up_weight, down_weight, heads):
    planes, count, channels = pencils.shape
    head_size = channels // heads
    masks = head_masks(heads, channels)
    flat = jnp.transpose(pencils, (1, 0, 2)).reshape(-1, channels)
    normed = layer_norm(flat, norm_gains[2])
    packed = jnp.dot(normed, qkv_weight[1], preferred_element_type=jnp.float32).astype(jnp.bfloat16)
    packed = packed.reshape(count, planes, 3 * channels)
    queries = packed[:, :, :channels]
    keys = packed[:, :, channels : 2 * channels]
    values = packed[:, :, 2 * channels :]
    head_queries = queries[:, None] * masks[None, :, None, :]
    scores = jnp.einsum("phzc,pyc->phzy", head_queries, keys, preferred_element_type=jnp.float32)
    weights = jax.nn.softmax(scores * head_size ** (-0.5), axis=-1).astype(jnp.bfloat16)
    head_values = values[:, None] * masks[None, :, None, :]
    attended = jnp.einsum(
        "phzy,phyc->pzc", weights, head_values, preferred_element_type=jnp.float32
    ).astype(jnp.bfloat16)
    projected = jnp.dot(
        attended.reshape(-1, channels), out_weight[1], preferred_element_type=jnp.float32
    ).astype(jnp.bfloat16)
    after = (flat.astype(jnp.float32) + projected.astype(jnp.float32)).astype(jnp.bfloat16)
    mixed = feed_forward(after, norm_gains[3], up_weight[1], down_weight[1]).reshape(
        count, planes, channels
    )
    return jnp.transpose(mixed, (1, 0, 2))


def general_body(volume, norm_gains, qkv_weight, out_weight, up_weight, down_weight, window_bias):
    rows_here = volume.shape[1]
    row_width = volume.shape[2]
    channels = norm_gains.shape[1]
    heads = window_bias.shape[0]
    height = rows_here * lax.axis_size("tile")
    tile_start = lax.axis_index("tile") * rows_here
    plane = volume.reshape(rows_here, row_width)
    next_rows = shifted(plane[:4], "tile", -1)
    extended = jnp.concatenate([plane[4:], next_rows], 0)
    attended = window_attention(
        extended, tile_start + 4, height, channels, norm_gains, qkv_weight, out_weight, window_bias
    )
    tail_rows = shifted(attended[-4:], "tile", 1)
    lateral = jnp.concatenate([tail_rows, attended[:-4]], 0)
    middle = (
        (plane.astype(jnp.float32) + lateral.astype(jnp.float32))
        .astype(jnp.bfloat16)
        .reshape(-1, channels)
    )
    planes = lax.axis_size("gz")
    middle = feed_forward(middle, norm_gains[1], up_weight[0], down_weight[0])
    grouped = middle.reshape(planes, -1, channels)
    pencils = lax.all_to_all(grouped, "gz", split_axis=0, concat_axis=0, tiled=True)
    returned = lax.all_to_all(
        axial_block(pencils, norm_gains, qkv_weight, out_weight, up_weight, down_weight, heads),
        "gz",
        split_axis=0,
        concat_axis=0,
        tiled=True,
    )
    return returned.reshape(1, rows_here, row_width)


LOG2E = 1.4426950408889634


def normalised(tokens):
    average = jnp.mean(tokens, 0, keepdims=True)
    centered = tokens - average
    variance = jnp.mean(centered * centered, 0, keepdims=True)
    return (centered * lax.rsqrt(variance + epsilon)).astype(jnp.bfloat16)


def product(left, right):
    return jnp.dot(left, right, preferred_element_type=jnp.float32)


GELU_IN = 0.035677408136300125 ** (1 / 3)
GELU_LINEAR = 0.7978845608028654 / GELU_IN
GELU_OUT = 0.5 / GELU_IN


def across(left, right):
    return lax.dot_general(left, right, (((1,), (1,)), ((), ())), preferred_element_type=jnp.float32)


def gated(scaled):
    scaled = scaled.astype(jnp.bfloat16)
    return scaled + scaled * jnp.tanh(scaled * (GELU_LINEAR + scaled * scaled))


def pack_kernel(volume_ref, gains_ref, packed_ref, held_gains_ref, rows_ref, sems):
    windows, _, width = packed_ref.shape
    half = width // 2
    copies = [
        pltpu.make_async_copy(volume_ref, rows_ref, sems.at[0]),
        pltpu.make_async_copy(gains_ref, held_gains_ref, sems.at[1]),
    ]
    for copy in copies:
        copy.start()
    for copy in copies:
        copy.wait()
    for window in range(windows):
        start = window * width + half
        if window < windows - 1:
            chunk = rows_ref[:, start : start + width]
        else:
            chunk = jnp.concatenate([rows_ref[:, start:], rows_ref[:, :half]], axis=1)
        packed_ref[window] = jnp.concatenate([chunk[4:], chunk[:4]], axis=0)


def unpack_kernel(packed_ref, volume_ref, rows_ref, sems):
    windows, _, width = packed_ref.shape
    half = width // 2
    for window in range(windows):
        chunk = packed_ref[window]
        rows = jnp.concatenate([chunk[12:], chunk[:12]], axis=0)
        start = window * width + half
        if window < windows - 1:
            rows_ref[:, start : start + width] = rows
        else:
            rows_ref[:, start:] = rows[:, :half]
            rows_ref[:, :half] = rows[:, half:]
    copy = pltpu.make_async_copy(rows_ref, volume_ref, sems.at[0])
    copy.start()
    copy.wait()


LAG = 4


def in_lockstep(stages, planes):
    for group in stages:
        group = group if isinstance(group, tuple) else (group,)
        for step in range(planes + LAG * (len(group) - 1)):
            for index, stage in enumerate(group):
                if 0 <= step - LAG * index < planes:
                    stage(step - LAG * index)


def blocks_kernel(
    tokens_ref,
    gains_ref,
    qkv_weight_ref,
    out_weight_ref,
    up_weight_ref,
    down_weight_ref,
    window_bias_ref,
    order_ref,
    result_ref,
    bias_ref,
    planar_ref,
    query_ref,
    key_ref,
    value_ref,
):
    channels = gains_ref.shape[1]
    planes = tokens_ref.shape[0] // 2
    heads = window_bias_ref.shape[0] // 64
    head_size = channels // heads
    lane = lax.broadcasted_iota(jnp.int32, (1, 128), 1)
    own = lane % 16 < 12
    first = lane % 16 < 8
    place = lax.broadcasted_iota(jnp.int32, (channels, 128), 1)
    by_window = place % 64 // 8 * 16 + place // 64 * 8 + place % 8
    blank = jnp.zeros((128 - channels, 128), jnp.bfloat16)
    blank_rows = jnp.zeros((128 - channels, 128), jnp.float32)

    def turned(ref, layer):
        return ref[layer].astype(jnp.float32).T

    def gain(norm, scale):
        return gains_ref[norm : norm + 1, :] * scale

    def turned_qkv(layer):
        matrix = turned(qkv_weight_ref, layer)
        queries = matrix[:channels] * gain(2 * layer, LOG2E * head_size ** (-0.5))
        return jnp.concatenate([queries, matrix[channels:] * gain(2 * layer, 1.0)], axis=0).astype(jnp.bfloat16)

    qkv = [turned_qkv(layer) for layer in range(2)]
    up = [(turned(up_weight_ref, layer) * gain(2 * layer + 1, GELU_IN)).astype(jnp.bfloat16) for layer in range(2)]
    down = [(down_weight_ref[layer].astype(jnp.float32) * GELU_OUT).astype(jnp.bfloat16) for layer in range(2)]
    out = turned(out_weight_ref, 0).astype(jnp.bfloat16)
    mix = jnp.concatenate([turned(out_weight_ref, 1).astype(jnp.bfloat16)] * 4, axis=1)

    shape = (heads * planes, planes * channels // 2)
    row = lax.broadcasted_iota(jnp.int32, shape, 0)
    column = lax.broadcasted_iota(jnp.int32, shape, 1)
    mine = lax.div(column, head_size // 2) == lax.rem(row, planes) * heads + lax.div(row, planes)
    gather = jnp.where(mine, 1.0, 0.0).astype(jnp.bfloat16)

    high = window_bias_ref[...].astype(jnp.bfloat16)
    low = (window_bias_ref[...] - high.astype(jnp.float32)).astype(jnp.bfloat16)
    parts = [across(order_ref[:64, :64], part).astype(jnp.bfloat16) for part in (high, low)]
    position = lax.axis_index("gz") * lax.axis_size("tile") + lax.axis_index("tile")
    last = position == lax.axis_size("gz") * lax.axis_size("tile") - 1
    key_row = lax.broadcasted_iota(jnp.int32, (64, 128), 0)
    query_lane = lax.broadcasted_iota(jnp.int32, (64, 128), 1)
    column_cut = ((key_row < 32) != (query_lane < 64)) & last
    row_cut = ((key_row % 8 < 4) != (query_lane % 8 < 4)) & (query_lane % 16 >= 8)
    for head in range(heads):
        placed = order_ref[64 + 128 * head : 64 + 128 * (head + 1), :]
        plain = (across(parts[0], placed) + across(parts[1], placed)) * LOG2E
        plain = jnp.where(column_cut, -jnp.inf, plain)
        bias_ref[0, 64 * head : 64 * (head + 1), :] = plain
        bias_ref[1, 64 * head : 64 * (head + 1), :] = jnp.where(row_cut, -jnp.inf, plain)

    held = [{} for _ in range(planes)]
    tops, totals = [], []

    def rows_of(plane):
        return slice(plane * channels, (plane + 1) * channels)

    def gather_columns(plane):
        held[plane]["x"] = [
            jnp.concatenate([tokens_ref[source, :, channels * c : channels * (c + 1)] for c in range(8)], axis=0)
            for source in (2 * plane, 2 * plane + 1)
        ]

    def load(plane):
        one, two = (tokens.T for tokens in held[plane]["x"])
        tokens = jnp.concatenate([jnp.where(own, one, two), jnp.where(own, two, one)], axis=1)
        held[plane]["x"] = tokens.astype(jnp.float32)

    def norm(plane):
        held[plane]["n"] = normalised(held[plane]["x"])

    def lateral_qkv(plane):
        packed = product(qkv[0], held[plane].pop("n"))
        held[plane]["q"] = packed[:channels]
        held[plane]["k"] = packed[channels : 2 * channels]
        values = packed[2 * channels :]
        held[plane]["v"] = []
        for lanes in (slice(0, 128), slice(128, 256)):
            ordered = jnp.take_along_axis(values[:, lanes], by_window, axis=1, mode="promise_in_bounds")
            held[plane]["v"].append((ordered[:, :64].astype(jnp.bfloat16), ordered[:, 64:].astype(jnp.bfloat16)))

    def lateral_scores(plane):
        queries, keys = held[plane].pop("q"), held[plane].pop("k")
        scores = []
        for pair in range(2):
            lanes = slice(128 * pair, 128 * pair + 128)
            query = queries[:, lanes]
            right = jnp.concatenate(
                [
                    jnp.where(first, query, 0.0).astype(jnp.bfloat16),
                    blank,
                    jnp.where(first, 0.0, query).astype(jnp.bfloat16),
                    blank,
                ],
                axis=0,
            )
            key = jnp.concatenate([keys[:, lanes], blank_rows], axis=0).T
            left = []
            for head in range(heads):
                masked = jnp.where(lane // head_size == head, key, 0.0).reshape(8, 2, 8, 128)
                windows = [masked[:, window].reshape(64, 128).astype(jnp.bfloat16) for window in range(2)]
                left.append(jnp.concatenate(windows, axis=1))
            scores.append((jnp.concatenate(left, axis=0), right))
        held[plane]["s"] = scores

    def lateral_weights(plane):
        scores = held[plane].pop("s")
        held[plane]["w"] = []
        for pair in range(2):
            for head in range(heads):
                own_scores = scores[pair][64 * head : 64 * head + 64]
                weights = jnp.exp2(own_scores - jnp.max(own_scores, axis=0, keepdims=True))
                total = jnp.sum(weights, axis=0, keepdims=True)
                held[plane]["w"].append((weights.astype(jnp.bfloat16), 1.0 / total))

    def lateral_products(plane):
        held[plane]["s"] = [product(*held[plane]["s"][pair]) + bias_ref[pair] for pair in range(2)]

    def lateral_values(plane):
        weights, values = held[plane].pop("w"), held[plane].pop("v")
        attended = []
        for pair in range(2):
            mixed = []
            for head in range(heads):
                own_weights, inverse = weights[heads * pair + head]
                rows = slice(head_size * head, head_size * (head + 1))
                both = product(jnp.concatenate([values[pair][0][rows], values[pair][1][rows]], axis=0), own_weights)
                own_mixed = jnp.where(first, both[:head_size], both[head_size:])
                mixed.append((own_mixed * inverse).astype(jnp.bfloat16))
            attended.append(jnp.concatenate(mixed, axis=0))
        held[plane]["a"] = jnp.concatenate(attended, axis=1)

    def lateral_out(plane):
        held[plane]["x"] = held[plane]["x"] + product(out, held[plane].pop("a"))

    def raised(layer):
        def stage(plane):
            held[plane]["h"] = product(up[layer], held[plane].pop("n"))

        return stage

    def gelu(plane):
        held[plane]["g"] = gated(held[plane].pop("h"))

    def lowered(layer):
        def stage(plane):
            held[plane]["x"] = held[plane]["x"] + product(down[layer], held[plane].pop("g"))

        return stage

    def axial_qkv(plane):
        packed = product(qkv[1], held[plane].pop("n")).astype(jnp.bfloat16)
        planar_ref[rows_of(plane), :] = held[plane].pop("x")
        query_ref[rows_of(plane), :] = packed[:channels]
        key_ref[rows_of(plane), :] = packed[channels : 2 * channels]
        value_ref[rows_of(plane), :] = packed[2 * channels :]

    def axial_scores(other):
        key = key_ref[rows_of(other), :]
        half = head_size // 2
        pairs = []
        for plane in range(planes):
            pair = query_ref[rows_of(plane), :] * key
            for head in range(heads):
                top = head_size * head
                pairs.append(pair[top : top + half] + pair[top + half : top + head_size])
        held[other]["s"] = product(gather, jnp.concatenate(pairs, axis=0))

    def axial_top(plane):
        scores = held[plane]["s"]
        tops.append(scores if plane == 0 else jnp.maximum(tops[-1], scores))

    def axial_exponentials(plane):
        held[plane]["s"] = jnp.exp2(held[plane]["s"] - tops[-1])
        totals.append(held[plane]["s"] if plane == 0 else totals[-1] + held[plane]["s"])

    def axial_weights(plane):
        if plane == 0:
            totals.append(1.0 / totals[-1])
        held[plane]["w"] = held[plane].pop("s") * totals[-1]

    def axial_values(plane):
        spread = []
        for other in range(planes):
            weights = held[other]["w"]
            wide = jnp.concatenate(
                [
                    jnp.broadcast_to(weights[planes * head + plane][None], (head_size, 256)).astype(jnp.bfloat16)
                    for head in range(heads)
                ],
                axis=0,
            )
            spread.append(wide * value_ref[rows_of(other), :])
        while len(spread) > 4:
            spread = [one + two for one, two in zip(spread[::2], spread[1::2])]
        spread = jnp.concatenate(spread, axis=0)
        held[plane]["x"] = planar_ref[rows_of(plane), :] + product(mix, spread)

    def turn(plane):
        mixed = held[plane].pop("x").astype(jnp.bfloat16)
        one, two = mixed[:, :128], mixed[:, 128:]
        held[plane]["x"] = [jnp.where(own, one, two).T, jnp.where(own, two, one).T]

    def store(plane):
        for tile, tokens in enumerate(held[plane].pop("x")):
            rows = jnp.concatenate([tokens[16 * c : 16 * (c + 1)] for c in range(8)], axis=1)
            result_ref[2 * plane + tile] = rows

    lateral = [gather_columns, load, norm, lateral_qkv, lateral_scores, (lateral_products, lateral_weights, lateral_values, lateral_out)]
    lateral += [norm, (raised(0), gelu, lowered(0)), norm, axial_qkv]
    axial = [axial_scores, axial_top, axial_exponentials, axial_weights, axial_values, norm, (raised(1), gelu, lowered(1)), turn, store]
    in_lockstep(lateral + axial, planes)


def pack(rows, gains, windows):
    return pl.pallas_call(
        pack_kernel,
        out_shape=(
            jax.ShapeDtypeStruct((windows, rows.shape[0], rows.shape[1] // windows), jnp.bfloat16),
            jax.ShapeDtypeStruct(gains.shape, gains.dtype),
        ),
        in_specs=[pl.BlockSpec(memory_space=pltpu.HBM)] * 2,
        scratch_shapes=[pltpu.VMEM(rows.shape, rows.dtype), pltpu.SemaphoreType.DMA((2,))],
        compiler_params=pltpu.CompilerParams(vmem_limit_bytes=16 * 1024 * 1024),
        name="pack_windows",
    )(*(pltpu.with_memory_space_constraint(operand, pltpu.HBM) for operand in (rows, gains)))


def unpack(packed, rows, width):
    return pl.pallas_call(
        unpack_kernel,
        out_shape=jax.ShapeDtypeStruct((rows, width), jnp.bfloat16),
        out_specs=pl.BlockSpec(memory_space=pltpu.HBM),
        scratch_shapes=[pltpu.VMEM((rows, width), jnp.bfloat16), pltpu.SemaphoreType.DMA((1,))],
        compiler_params=pltpu.CompilerParams(vmem_limit_bytes=16 * 1024 * 1024),
        name="unpack_windows",
    )(packed)


def blocks(tokens, *operands):
    rows = tokens.shape[0] // 2 * operands[0].shape[1]
    heads = operands[5].shape[0] // 64
    return pl.pallas_call(
        blocks_kernel,
        out_shape=jax.ShapeDtypeStruct(tokens.shape, jnp.bfloat16),
        scratch_shapes=[
            pltpu.VMEM((2, heads * 64, 128), jnp.float32),
            pltpu.VMEM((rows, 256), jnp.float32),
            pltpu.VMEM((rows, 256), jnp.bfloat16),
            pltpu.VMEM((rows, 256), jnp.bfloat16),
            pltpu.VMEM((rows, 256), jnp.bfloat16),
        ],
        compiler_params=pltpu.CompilerParams(vmem_limit_bytes=40 * 1024 * 1024),
        name="both_blocks",
    )(tokens, *operands)


def token_order(heads):
    index = np.arange(64)
    order = np.zeros((64, heads * 64), np.float32)
    order[index, index % 8 * 8 + index // 8] = 1.0
    lane = np.arange(128)
    placed = np.zeros((heads, 128, heads, 64), np.float32)
    for head in range(heads):
        placed[head, lane, head, lane % 8 * 8 + lane // 16] = 1.0
    return np.concatenate([order, placed.reshape(heads * 128, heads * 64)]).astype(jnp.bfloat16)


def window_body(volume, norm_gains, qkv_weight, out_weight, up_weight, down_weight, window_bias):
    rows = volume.shape[1]
    width = volume.shape[2]
    channels = norm_gains.shape[1]
    heads = window_bias.shape[0]
    planes = lax.axis_size("gz")
    windows = width // channels // 8
    packed, held_gains = pack(volume.reshape(rows, width), norm_gains, windows)
    tokens = lax.all_to_all(packed, ("gz", "tile"), split_axis=0, concat_axis=0, tiled=True)
    mixed = blocks(
        tokens,
        held_gains,
        qkv_weight,
        out_weight,
        up_weight,
        jnp.transpose(down_weight, (0, 2, 1)),
        window_bias.reshape(heads * 64, 64),
        token_order(heads),
    )
    returned = lax.all_to_all(mixed, ("gz", "tile"), split_axis=0, concat_axis=0, tiled=True)
    return unpack(returned, rows, width).reshape(1, rows, width)


def fits_windows(mesh, volume, norm_gains, window_bias):
    planes, tiles = mesh.shape["gz"], mesh.shape["tile"]
    channels, heads = norm_gains.shape[1], window_bias.shape[0]
    return (
        tiles == 2
        and planes == 8
        and volume.shape[1] == 16 * tiles
        and volume.shape[2] == 8 * channels * planes * tiles
        and channels == 96
        and heads == 3
    )


def solution(mesh):
    placed = (P(("groups", "gz"), "tile", None), P(), P(), P(), P(), P(), P())

    def run(volume, norm_gains, *weights):
        chosen = window_body if fits_windows(mesh, volume, norm_gains, weights[-1]) else general_body
        return jax.shard_map(
            chosen,
            mesh=mesh,
            in_specs=placed,
            out_specs=P(("groups", "gz"), "tile", None),
            check_vma=False,
        )(volume, norm_gains, *weights)

    return run
```

```python
import jax
import jax.numpy as jnp
import numpy as np
from jax import lax
from jax.experimental import pallas as pl
from jax.experimental.pallas import tpu as pltpu
from jax.sharding import PartitionSpec as P

epsilon = 1e-05


def shifted(array, axis, by):
    peers = lax.axis_size(axis)
    return lax.ppermute(array, axis, [(i, (i + by) % peers) for i in range(peers)])


def layer_norm(tokens, gain):
    values = tokens.astype(jnp.float32)
    average = jnp.mean(values, -1, keepdims=True)
    centered = values - average
    variance = jnp.mean(centered * centered, -1, keepdims=True)
    return (centered * lax.rsqrt(variance + epsilon) * gain).astype(jnp.bfloat16)


def feed_forward(tokens, gain, up_matrix, down_matrix):
    normed = layer_norm(tokens, gain)
    hidden = jax.nn.gelu(jnp.dot(normed, up_matrix, preferred_element_type=jnp.float32)).astype(
        jnp.bfloat16
    )
    total = tokens.astype(jnp.float32) + jnp.dot(
        hidden, down_matrix, preferred_element_type=jnp.float32
    )
    return total.astype(jnp.bfloat16)


def edge_label(index, extent):
    return jnp.where(index < 4, 2, jnp.where(index >= extent - 4, 1, 0)).astype(jnp.int32)


def head_masks(heads, channels):
    owner = jnp.arange(channels, dtype=jnp.int32) // (channels // heads)
    return (owner[None, :] == jnp.arange(heads, dtype=jnp.int32)[:, None]).astype(jnp.bfloat16)


def window_attention(
    row_block, first_row, height, channels, norm_gains, qkv_weight, out_weight, window_bias
):
    count = row_block.shape[0]
    columns = row_block.shape[1] // channels
    heads = window_bias.shape[0]
    head_size = channels // heads
    masks = head_masks(heads, channels)
    rolled = jnp.roll(row_block, -4 * channels, axis=1)
    windowed = rolled.reshape(count // 8, 8, columns // 8, 8 * channels).transpose(0, 2, 1, 3)
    normed = layer_norm(windowed.reshape(-1, channels), norm_gains[0])
    packed = jnp.dot(normed, qkv_weight[0], preferred_element_type=jnp.float32).astype(jnp.bfloat16)
    packed = packed.reshape(-1, 64, 3 * channels)
    queries = packed[:, :, :channels]
    keys = packed[:, :, channels : 2 * channels]
    values = packed[:, :, 2 * channels :]
    initial_rows = jnp.mod(first_row + jnp.arange(count, dtype=jnp.int32), height)
    initial_columns = jnp.mod(jnp.arange(columns, dtype=jnp.int32) + 4, columns)
    labels = (
        edge_label(initial_rows, height)[:, None] * 3
        + edge_label(initial_columns, columns)[None, :]
    )
    window_labels = (
        labels.reshape(count // 8, 8, columns // 8, 8).transpose(0, 2, 1, 3).reshape(-1, 64)
    )
    allowed = window_labels[:, :, None] == window_labels[:, None, :]
    head_queries = queries[:, None] * masks[None, :, None, :]
    scores = jnp.einsum("nhqc,nkc->nhqk", head_queries, keys, preferred_element_type=jnp.float32)
    scores = scores * head_size ** (-0.5) + window_bias[None]
    scores = jnp.where(allowed[:, None], scores, -jnp.inf)
    weights = jax.nn.softmax(scores, axis=-1).astype(jnp.bfloat16)
    head_values = values[:, None] * masks[None, :, None, :]
    attended = jnp.einsum(
        "nhqk,nhkc->nqc", weights, head_values, preferred_element_type=jnp.float32
    ).astype(jnp.bfloat16)
    lateral = jnp.dot(
        attended.reshape(-1, channels), out_weight[0], preferred_element_type=jnp.float32
    ).astype(jnp.bfloat16)
    lateral = lateral.reshape(count // 8, columns // 8, 8, 8 * channels).transpose(0, 2, 1, 3)
    return jnp.roll(lateral.reshape(count, columns * channels), 4 * channels, axis=1)


def axial_block(pencils, norm_gains, qkv_weight, out_weight, up_weight, down_weight, heads):
    planes, count, channels = pencils.shape
    head_size = channels // heads
    masks = head_masks(heads, channels)
    flat = jnp.transpose(pencils, (1, 0, 2)).reshape(-1, channels)
    normed = layer_norm(flat, norm_gains[2])
    packed = jnp.dot(normed, qkv_weight[1], preferred_element_type=jnp.float32).astype(jnp.bfloat16)
    packed = packed.reshape(count, planes, 3 * channels)
    queries = packed[:, :, :channels]
    keys = packed[:, :, channels : 2 * channels]
    values = packed[:, :, 2 * channels :]
    head_queries = queries[:, None] * masks[None, :, None, :]
    scores = jnp.einsum("phzc,pyc->phzy", head_queries, keys, preferred_element_type=jnp.float32)
    weights = jax.nn.softmax(scores * head_size ** (-0.5), axis=-1).astype(jnp.bfloat16)
    head_values = values[:, None] * masks[None, :, None, :]
    attended = jnp.einsum(
        "phzy,phyc->pzc", weights, head_values, preferred_element_type=jnp.float32
    ).astype(jnp.bfloat16)
    projected = jnp.dot(
        attended.reshape(-1, channels), out_weight[1], preferred_element_type=jnp.float32
    ).astype(jnp.bfloat16)
    after = (flat.astype(jnp.float32) + projected.astype(jnp.float32)).astype(jnp.bfloat16)
    mixed = feed_forward(after, norm_gains[3], up_weight[1], down_weight[1]).reshape(
        count, planes, channels
    )
    return jnp.transpose(mixed, (1, 0, 2))


def general_body(volume, norm_gains, qkv_weight, out_weight, up_weight, down_weight, window_bias):
    rows_here = volume.shape[1]
    row_width = volume.shape[2]
    channels = norm_gains.shape[1]
    heads = window_bias.shape[0]
    height = rows_here * lax.axis_size("tile")
    tile_start = lax.axis_index("tile") * rows_here
    plane = volume.reshape(rows_here, row_width)
    next_rows = shifted(plane[:4], "tile", -1)
    extended = jnp.concatenate([plane[4:], next_rows], 0)
    attended = window_attention(
        extended, tile_start + 4, height, channels, norm_gains, qkv_weight, out_weight, window_bias
    )
    tail_rows = shifted(attended[-4:], "tile", 1)
    lateral = jnp.concatenate([tail_rows, attended[:-4]], 0)
    middle = (
        (plane.astype(jnp.float32) + lateral.astype(jnp.float32))
        .astype(jnp.bfloat16)
        .reshape(-1, channels)
    )
    planes = lax.axis_size("gz")
    middle = feed_forward(middle, norm_gains[1], up_weight[0], down_weight[0])
    grouped = middle.reshape(planes, -1, channels)
    pencils = lax.all_to_all(grouped, "gz", split_axis=0, concat_axis=0, tiled=True)
    returned = lax.all_to_all(
        axial_block(pencils, norm_gains, qkv_weight, out_weight, up_weight, down_weight, heads),
        "gz",
        split_axis=0,
        concat_axis=0,
        tiled=True,
    )
    return returned.reshape(1, rows_here, row_width)


LOG2E = 1.4426950408889634


def normalised(tokens):
    average = jnp.mean(tokens, 0, keepdims=True)
    centered = tokens - average
    variance = jnp.mean(centered * centered, 0, keepdims=True)
    return (centered * lax.rsqrt(variance + epsilon)).astype(jnp.bfloat16)


def product(left, right):
    return jnp.dot(left, right, preferred_element_type=jnp.float32)


GELU_IN = 0.035677408136300125 ** (1 / 3)
GELU_LINEAR = 0.7978845608028654 / GELU_IN
GELU_OUT = 0.5 / GELU_IN


def across(left, right):
    return lax.dot_general(left, right, (((1,), (1,)), ((), ())), preferred_element_type=jnp.float32)


def gated(scaled):
    scaled = scaled.astype(jnp.bfloat16)
    return scaled + scaled * jnp.tanh(scaled * (GELU_LINEAR + scaled * scaled))


def pack_kernel(volume_ref, gains_ref, packed_ref, held_gains_ref, rows_ref, sems):
    windows, _, width = packed_ref.shape
    half = width // 2
    copies = [
        pltpu.make_async_copy(volume_ref, rows_ref, sems.at[0]),
        pltpu.make_async_copy(gains_ref, held_gains_ref, sems.at[1]),
    ]
    for copy in copies:
        copy.start()
    for copy in copies:
        copy.wait()
    for window in range(windows):
        start = window * width + half
        if window < windows - 1:
            chunk = rows_ref[:, start : start + width]
        else:
            chunk = jnp.concatenate([rows_ref[:, start:], rows_ref[:, :half]], axis=1)
        packed_ref[window] = jnp.concatenate([chunk[4:], chunk[:4]], axis=0)


def unpack_kernel(packed_ref, volume_ref, rows_ref, sems):
    windows, _, width = packed_ref.shape
    half = width // 2
    cut = windows // 2 * width + half
    runs = (pl.ds(0, cut), pl.ds(cut, windows * width - cut))
    copies = [
        pltpu.make_async_copy(rows_ref.at[:, run], volume_ref.at[:, run], sems.at[index])
        for index, run in enumerate(runs)
    ]
    for window in [windows - 1, *range(windows - 1)]:
        chunk = packed_ref[window]
        rows = jnp.concatenate([chunk[12:], chunk[:12]], axis=0)
        start = window * width + half
        if window < windows - 1:
            rows_ref[:, start : start + width] = rows
        else:
            rows_ref[:, start:] = rows[:, :half]
            rows_ref[:, :half] = rows[:, half:]
        if window == windows // 2 - 1:
            copies[0].start()
    copies[1].start()
    for copy in copies:
        copy.wait()


LAG = 4


def in_lockstep(stages, planes):
    for group in stages:
        group = group if isinstance(group, tuple) else (group,)
        for step in range(planes + LAG * (len(group) - 1)):
            for index, stage in enumerate(group):
                if 0 <= step - LAG * index < planes:
                    stage(step - LAG * index)


def blocks_kernel(
    tokens_ref,
    gains_ref,
    qkv_weight_ref,
    out_weight_ref,
    up_weight_ref,
    down_weight_ref,
    window_bias_ref,
    order_ref,
    result_ref,
    bias_ref,
    planar_ref,
    query_ref,
    key_ref,
    value_ref,
):
    channels = gains_ref.shape[1]
    planes = tokens_ref.shape[0] // 2
    heads = window_bias_ref.shape[0] // 64
    head_size = channels // heads
    lane = lax.broadcasted_iota(jnp.int32, (1, 128), 1)
    own = lane % 16 < 12
    first = lane % 16 < 8
    place = lax.broadcasted_iota(jnp.int32, (channels, 128), 1)
    by_window = place % 64 // 8 * 16 + place // 64 * 8 + place % 8
    blank = jnp.zeros((128 - channels, 128), jnp.bfloat16)
    blank_rows = jnp.zeros((128 - channels, 128), jnp.float32)

    def turned(ref, layer):
        return ref[layer].astype(jnp.float32).T

    def gain(norm, scale):
        return gains_ref[norm : norm + 1, :] * scale

    def turned_qkv(layer):
        matrix = turned(qkv_weight_ref, layer)
        queries = matrix[:channels] * gain(2 * layer, LOG2E * head_size ** (-0.5))
        return jnp.concatenate([queries, matrix[channels:] * gain(2 * layer, 1.0)], axis=0).astype(jnp.bfloat16)

    qkv = [turned_qkv(layer) for layer in range(2)]
    up = [(turned(up_weight_ref, layer) * gain(2 * layer + 1, GELU_IN)).astype(jnp.bfloat16) for layer in range(2)]
    down = [(down_weight_ref[layer].astype(jnp.float32) * GELU_OUT).astype(jnp.bfloat16) for layer in range(2)]
    out = turned(out_weight_ref, 0).astype(jnp.bfloat16)
    mix = jnp.concatenate([turned(out_weight_ref, 1).astype(jnp.bfloat16)] * 4, axis=1)

    shape = (heads * planes, planes * channels // 2)
    row = lax.broadcasted_iota(jnp.int32, shape, 0)
    column = lax.broadcasted_iota(jnp.int32, shape, 1)
    mine = lax.div(column, head_size // 2) == lax.rem(row, planes) * heads + lax.div(row, planes)
    gather = jnp.where(mine, 1.0, 0.0).astype(jnp.bfloat16)

    high = window_bias_ref[...].astype(jnp.bfloat16)
    low = (window_bias_ref[...] - high.astype(jnp.float32)).astype(jnp.bfloat16)
    parts = [across(order_ref[:64, :64], part).astype(jnp.bfloat16) for part in (high, low)]
    position = lax.axis_index("gz") * lax.axis_size("tile") + lax.axis_index("tile")
    last = position == lax.axis_size("gz") * lax.axis_size("tile") - 1
    key_row = lax.broadcasted_iota(jnp.int32, (64, 128), 0)
    query_lane = lax.broadcasted_iota(jnp.int32, (64, 128), 1)
    column_cut = ((key_row < 32) != (query_lane < 64)) & last
    row_cut = ((key_row % 8 < 4) != (query_lane % 8 < 4)) & (query_lane % 16 >= 8)
    for head in range(heads):
        placed = order_ref[64 + 128 * head : 64 + 128 * (head + 1), :]
        plain = (across(parts[0], placed) + across(parts[1], placed)) * LOG2E
        plain = jnp.where(column_cut, -jnp.inf, plain)
        bias_ref[0, 64 * head : 64 * (head + 1), :] = plain
        bias_ref[1, 64 * head : 64 * (head + 1), :] = jnp.where(row_cut, -jnp.inf, plain)

    held = [{} for _ in range(planes)]
    tops, totals = [], []

    def rows_of(plane):
        return slice(plane * channels, (plane + 1) * channels)

    def gather_columns(plane):
        held[plane]["x"] = [
            jnp.concatenate([tokens_ref[source, :, channels * c : channels * (c + 1)] for c in range(8)], axis=0)
            for source in (2 * plane, 2 * plane + 1)
        ]

    def load(plane):
        one, two = (tokens.T for tokens in held[plane]["x"])
        tokens = jnp.concatenate([jnp.where(own, one, two), jnp.where(own, two, one)], axis=1)
        held[plane]["x"] = tokens.astype(jnp.float32)

    def norm(plane):
        held[plane]["n"] = normalised(held[plane]["x"])

    def lateral_qkv(plane):
        packed = product(qkv[0], held[plane].pop("n"))
        held[plane]["q"] = packed[:channels]
        held[plane]["k"] = packed[channels : 2 * channels]
        values = packed[2 * channels :]
        held[plane]["v"] = []
        for lanes in (slice(0, 128), slice(128, 256)):
            ordered = jnp.take_along_axis(values[:, lanes], by_window, axis=1, mode="promise_in_bounds")
            held[plane]["v"].append((ordered[:, :64].astype(jnp.bfloat16), ordered[:, 64:].astype(jnp.bfloat16)))

    def lateral_scores(plane):
        queries, keys = held[plane].pop("q"), held[plane].pop("k")
        scores = []
        for pair in range(2):
            lanes = slice(128 * pair, 128 * pair + 128)
            query = queries[:, lanes]
            right = jnp.concatenate(
                [
                    jnp.where(first, query, 0.0).astype(jnp.bfloat16),
                    blank,
                    jnp.where(first, 0.0, query).astype(jnp.bfloat16),
                    blank,
                ],
                axis=0,
            )
            key = jnp.concatenate([keys[:, lanes], blank_rows], axis=0).T
            left = []
            for head in range(heads):
                masked = jnp.where(lane // head_size == head, key, 0.0).reshape(8, 2, 8, 128)
                windows = [masked[:, window].reshape(64, 128).astype(jnp.bfloat16) for window in range(2)]
                left.append(jnp.concatenate(windows, axis=1))
            scores.append((jnp.concatenate(left, axis=0), right))
        held[plane]["s"] = scores

    def lateral_weights(plane):
        scores = held[plane].pop("s")
        held[plane]["w"] = []
        for pair in range(2):
            for head in range(heads):
                own_scores = scores[pair][64 * head : 64 * head + 64]
                weights = jnp.exp2(own_scores - jnp.max(own_scores, axis=0, keepdims=True))
                total = jnp.sum(weights, axis=0, keepdims=True)
                held[plane]["w"].append((weights.astype(jnp.bfloat16), 1.0 / total))

    def lateral_products(plane):
        held[plane]["s"] = [product(*held[plane]["s"][pair]) + bias_ref[pair] for pair in range(2)]

    def lateral_values(plane):
        weights, values = held[plane].pop("w"), held[plane].pop("v")
        attended = []
        for pair in range(2):
            mixed = []
            for head in range(heads):
                own_weights, inverse = weights[heads * pair + head]
                rows = slice(head_size * head, head_size * (head + 1))
                both = product(jnp.concatenate([values[pair][0][rows], values[pair][1][rows]], axis=0), own_weights)
                own_mixed = jnp.where(first, both[:head_size], both[head_size:])
                mixed.append((own_mixed * inverse).astype(jnp.bfloat16))
            attended.append(jnp.concatenate(mixed, axis=0))
        held[plane]["a"] = jnp.concatenate(attended, axis=1)

    def lateral_out(plane):
        held[plane]["x"] = held[plane]["x"] + product(out, held[plane].pop("a"))

    def raised(layer):
        def stage(plane):
            held[plane]["h"] = product(up[layer], held[plane].pop("n"))

        return stage

    def gelu(plane):
        held[plane]["g"] = gated(held[plane].pop("h"))

    def lowered(layer):
        def stage(plane):
            held[plane]["x"] = held[plane]["x"] + product(down[layer], held[plane].pop("g"))

        return stage

    def axial_qkv(plane):
        packed = product(qkv[1], held[plane].pop("n")).astype(jnp.bfloat16)
        planar_ref[rows_of(plane), :] = held[plane].pop("x")
        query_ref[rows_of(plane), :] = packed[:channels]
        key_ref[rows_of(plane), :] = packed[channels : 2 * channels]
        value_ref[rows_of(plane), :] = packed[2 * channels :]

    def axial_scores(other):
        key = key_ref[rows_of(other), :]
        half = head_size // 2
        pairs = []
        for plane in range(planes):
            pair = query_ref[rows_of(plane), :] * key
            for head in range(heads):
                top = head_size * head
                pairs.append(pair[top : top + half] + pair[top + half : top + head_size])
        held[other]["s"] = product(gather, jnp.concatenate(pairs, axis=0))

    def axial_top(plane):
        scores = held[plane]["s"]
        tops.append(scores if plane == 0 else jnp.maximum(tops[-1], scores))

    def axial_exponentials(plane):
        held[plane]["s"] = jnp.exp2(held[plane]["s"] - tops[-1])
        totals.append(held[plane]["s"] if plane == 0 else totals[-1] + held[plane]["s"])

    def axial_weights(plane):
        if plane == 0:
            totals.append(1.0 / totals[-1])
        held[plane]["w"] = held[plane].pop("s") * totals[-1]

    def axial_values(plane):
        spread = []
        for other in range(planes):
            weights = held[other]["w"]
            wide = jnp.concatenate(
                [
                    jnp.broadcast_to(weights[planes * head + plane][None], (head_size, 256)).astype(jnp.bfloat16)
                    for head in range(heads)
                ],
                axis=0,
            )
            spread.append(wide * value_ref[rows_of(other), :])
        while len(spread) > 4:
            spread = [one + two for one, two in zip(spread[::2], spread[1::2])]
        spread = jnp.concatenate(spread, axis=0)
        held[plane]["x"] = planar_ref[rows_of(plane), :] + product(mix, spread)

    def turn(plane):
        mixed = held[plane].pop("x").astype(jnp.bfloat16)
        one, two = mixed[:, :128], mixed[:, 128:]
        held[plane]["x"] = [jnp.where(own, one, two).T, jnp.where(own, two, one).T]

    def store(plane):
        for tile, tokens in enumerate(held[plane].pop("x")):
            rows = jnp.concatenate([tokens[16 * c : 16 * (c + 1)] for c in range(8)], axis=1)
            result_ref[2 * plane + tile] = rows

    lateral = [gather_columns, load, norm, lateral_qkv, lateral_scores, (lateral_products, lateral_weights, lateral_values, lateral_out)]
    lateral += [norm, (raised(0), gelu, lowered(0)), norm, axial_qkv]
    axial = [axial_scores, axial_top, axial_exponentials, axial_weights, axial_values, norm, (raised(1), gelu, lowered(1)), turn, store]
    in_lockstep(lateral + axial, planes)


def pack(rows, gains, windows):
    return pl.pallas_call(
        pack_kernel,
        out_shape=(
            jax.ShapeDtypeStruct((windows, rows.shape[0], rows.shape[1] // windows), jnp.bfloat16),
            jax.ShapeDtypeStruct(gains.shape, gains.dtype),
        ),
        in_specs=[pl.BlockSpec(memory_space=pltpu.HBM)] * 2,
        scratch_shapes=[pltpu.VMEM(rows.shape, rows.dtype), pltpu.SemaphoreType.DMA((2,))],
        compiler_params=pltpu.CompilerParams(vmem_limit_bytes=16 * 1024 * 1024),
        name="pack_windows",
    )(*(pltpu.with_memory_space_constraint(operand, pltpu.HBM) for operand in (rows, gains)))


def unpack(packed, rows, width):
    return pl.pallas_call(
        unpack_kernel,
        out_shape=jax.ShapeDtypeStruct((rows, width), jnp.bfloat16),
        out_specs=pl.BlockSpec(memory_space=pltpu.HBM),
        scratch_shapes=[pltpu.VMEM((rows, width), jnp.bfloat16), pltpu.SemaphoreType.DMA((2,))],
        compiler_params=pltpu.CompilerParams(vmem_limit_bytes=16 * 1024 * 1024),
        name="unpack_windows",
    )(packed)


def blocks(tokens, *operands):
    rows = tokens.shape[0] // 2 * operands[0].shape[1]
    heads = operands[5].shape[0] // 64
    return pl.pallas_call(
        blocks_kernel,
        out_shape=jax.ShapeDtypeStruct(tokens.shape, jnp.bfloat16),
        scratch_shapes=[
            pltpu.VMEM((2, heads * 64, 128), jnp.float32),
            pltpu.VMEM((rows, 256), jnp.float32),
            pltpu.VMEM((rows, 256), jnp.bfloat16),
            pltpu.VMEM((rows, 256), jnp.bfloat16),
            pltpu.VMEM((rows, 256), jnp.bfloat16),
        ],
        compiler_params=pltpu.CompilerParams(vmem_limit_bytes=40 * 1024 * 1024),
        name="both_blocks",
    )(tokens, *operands)


def token_order(heads):
    index = np.arange(64)
    order = np.zeros((64, heads * 64), np.float32)
    order[index, index % 8 * 8 + index // 8] = 1.0
    lane = np.arange(128)
    placed = np.zeros((heads, 128, heads, 64), np.float32)
    for head in range(heads):
        placed[head, lane, head, lane % 8 * 8 + lane // 16] = 1.0
    return np.concatenate([order, placed.reshape(heads * 128, heads * 64)]).astype(jnp.bfloat16)


def window_body(volume, norm_gains, qkv_weight, out_weight, up_weight, down_weight, window_bias):
    rows = volume.shape[1]
    width = volume.shape[2]
    channels = norm_gains.shape[1]
    heads = window_bias.shape[0]
    planes = lax.axis_size("gz")
    windows = width // channels // 8
    packed, held_gains = pack(volume.reshape(rows, width), norm_gains, windows)
    tokens = lax.all_to_all(packed, ("gz", "tile"), split_axis=0, concat_axis=0, tiled=True)
    mixed = blocks(
        tokens,
        held_gains,
        qkv_weight,
        out_weight,
        up_weight,
        jnp.transpose(down_weight, (0, 2, 1)),
        window_bias.reshape(heads * 64, 64),
        token_order(heads),
    )
    returned = lax.all_to_all(mixed, ("gz", "tile"), split_axis=0, concat_axis=0, tiled=True)
    return unpack(returned, rows, width).reshape(1, rows, width)


def fits_windows(mesh, volume, norm_gains, window_bias):
    planes, tiles = mesh.shape["gz"], mesh.shape["tile"]
    channels, heads = norm_gains.shape[1], window_bias.shape[0]
    return (
        tiles == 2
        and planes == 8
        and volume.shape[1] == 16 * tiles
        and volume.shape[2] == 8 * channels * planes * tiles
        and channels == 96
        and heads == 3
    )


def solution(mesh):
    placed = (P(("groups", "gz"), "tile", None), P(), P(), P(), P(), P(), P())

    def run(volume, norm_gains, *weights):
        chosen = window_body if fits_windows(mesh, volume, norm_gains, weights[-1]) else general_body
        return jax.shard_map(
            chosen,
            mesh=mesh,
            in_specs=placed,
            out_specs=P(("groups", "gz"), "tile", None),
            check_vma=False,
        )(volume, norm_gains, *weights)

    return run
```

```python
import jax
import jax.numpy as jnp
import numpy as np
from jax import lax
from jax.experimental import pallas as pl
from jax.experimental.pallas import tpu as pltpu
from jax.sharding import PartitionSpec as P

epsilon = 1e-05


def shifted(array, axis, by):
    peers = lax.axis_size(axis)
    return lax.ppermute(array, axis, [(i, (i + by) % peers) for i in range(peers)])


def layer_norm(tokens, gain):
    values = tokens.astype(jnp.float32)
    average = jnp.mean(values, -1, keepdims=True)
    centered = values - average
    variance = jnp.mean(centered * centered, -1, keepdims=True)
    return (centered * lax.rsqrt(variance + epsilon) * gain).astype(jnp.bfloat16)


def feed_forward(tokens, gain, up_matrix, down_matrix):
    normed = layer_norm(tokens, gain)
    hidden = jax.nn.gelu(jnp.dot(normed, up_matrix, preferred_element_type=jnp.float32)).astype(
        jnp.bfloat16
    )
    total = tokens.astype(jnp.float32) + jnp.dot(
        hidden, down_matrix, preferred_element_type=jnp.float32
    )
    return total.astype(jnp.bfloat16)


def edge_label(index, extent):
    return jnp.where(index < 4, 2, jnp.where(index >= extent - 4, 1, 0)).astype(jnp.int32)


def head_masks(heads, channels):
    owner = jnp.arange(channels, dtype=jnp.int32) // (channels // heads)
    return (owner[None, :] == jnp.arange(heads, dtype=jnp.int32)[:, None]).astype(jnp.bfloat16)


def window_attention(
    row_block, first_row, height, channels, norm_gains, qkv_weight, out_weight, window_bias
):
    count = row_block.shape[0]
    columns = row_block.shape[1] // channels
    heads = window_bias.shape[0]
    head_size = channels // heads
    masks = head_masks(heads, channels)
    rolled = jnp.roll(row_block, -4 * channels, axis=1)
    windowed = rolled.reshape(count // 8, 8, columns // 8, 8 * channels).transpose(0, 2, 1, 3)
    normed = layer_norm(windowed.reshape(-1, channels), norm_gains[0])
    packed = jnp.dot(normed, qkv_weight[0], preferred_element_type=jnp.float32).astype(jnp.bfloat16)
    packed = packed.reshape(-1, 64, 3 * channels)
    queries = packed[:, :, :channels]
    keys = packed[:, :, channels : 2 * channels]
    values = packed[:, :, 2 * channels :]
    initial_rows = jnp.mod(first_row + jnp.arange(count, dtype=jnp.int32), height)
    initial_columns = jnp.mod(jnp.arange(columns, dtype=jnp.int32) + 4, columns)
    labels = (
        edge_label(initial_rows, height)[:, None] * 3
        + edge_label(initial_columns, columns)[None, :]
    )
    window_labels = (
        labels.reshape(count // 8, 8, columns // 8, 8).transpose(0, 2, 1, 3).reshape(-1, 64)
    )
    allowed = window_labels[:, :, None] == window_labels[:, None, :]
    head_queries = queries[:, None] * masks[None, :, None, :]
    scores = jnp.einsum("nhqc,nkc->nhqk", head_queries, keys, preferred_element_type=jnp.float32)
    scores = scores * head_size ** (-0.5) + window_bias[None]
    scores = jnp.where(allowed[:, None], scores, -jnp.inf)
    weights = jax.nn.softmax(scores, axis=-1).astype(jnp.bfloat16)
    head_values = values[:, None] * masks[None, :, None, :]
    attended = jnp.einsum(
        "nhqk,nhkc->nqc", weights, head_values, preferred_element_type=jnp.float32
    ).astype(jnp.bfloat16)
    lateral = jnp.dot(
        attended.reshape(-1, channels), out_weight[0], preferred_element_type=jnp.float32
    ).astype(jnp.bfloat16)
    lateral = lateral.reshape(count // 8, columns // 8, 8, 8 * channels).transpose(0, 2, 1, 3)
    return jnp.roll(lateral.reshape(count, columns * channels), 4 * channels, axis=1)


def axial_block(pencils, norm_gains, qkv_weight, out_weight, up_weight, down_weight, heads):
    planes, count, channels = pencils.shape
    head_size = channels // heads
    masks = head_masks(heads, channels)
    flat = jnp.transpose(pencils, (1, 0, 2)).reshape(-1, channels)
    normed = layer_norm(flat, norm_gains[2])
    packed = jnp.dot(normed, qkv_weight[1], preferred_element_type=jnp.float32).astype(jnp.bfloat16)
    packed = packed.reshape(count, planes, 3 * channels)
    queries = packed[:, :, :channels]
    keys = packed[:, :, channels : 2 * channels]
    values = packed[:, :, 2 * channels :]
    head_queries = queries[:, None] * masks[None, :, None, :]
    scores = jnp.einsum("phzc,pyc->phzy", head_queries, keys, preferred_element_type=jnp.float32)
    weights = jax.nn.softmax(scores * head_size ** (-0.5), axis=-1).astype(jnp.bfloat16)
    head_values = values[:, None] * masks[None, :, None, :]
    attended = jnp.einsum(
        "phzy,phyc->pzc", weights, head_values, preferred_element_type=jnp.float32
    ).astype(jnp.bfloat16)
    projected = jnp.dot(
        attended.reshape(-1, channels), out_weight[1], preferred_element_type=jnp.float32
    ).astype(jnp.bfloat16)
    after = (flat.astype(jnp.float32) + projected.astype(jnp.float32)).astype(jnp.bfloat16)
    mixed = feed_forward(after, norm_gains[3], up_weight[1], down_weight[1]).reshape(
        count, planes, channels
    )
    return jnp.transpose(mixed, (1, 0, 2))


def general_body(volume, norm_gains, qkv_weight, out_weight, up_weight, down_weight, window_bias):
    rows_here = volume.shape[1]
    row_width = volume.shape[2]
    channels = norm_gains.shape[1]
    heads = window_bias.shape[0]
    height = rows_here * lax.axis_size("tile")
    tile_start = lax.axis_index("tile") * rows_here
    plane = volume.reshape(rows_here, row_width)
    next_rows = shifted(plane[:4], "tile", -1)
    extended = jnp.concatenate([plane[4:], next_rows], 0)
    attended = window_attention(
        extended, tile_start + 4, height, channels, norm_gains, qkv_weight, out_weight, window_bias
    )
    tail_rows = shifted(attended[-4:], "tile", 1)
    lateral = jnp.concatenate([tail_rows, attended[:-4]], 0)
    middle = (
        (plane.astype(jnp.float32) + lateral.astype(jnp.float32))
        .astype(jnp.bfloat16)
        .reshape(-1, channels)
    )
    planes = lax.axis_size("gz")
    middle = feed_forward(middle, norm_gains[1], up_weight[0], down_weight[0])
    grouped = middle.reshape(planes, -1, channels)
    pencils = lax.all_to_all(grouped, "gz", split_axis=0, concat_axis=0, tiled=True)
    returned = lax.all_to_all(
        axial_block(pencils, norm_gains, qkv_weight, out_weight, up_weight, down_weight, heads),
        "gz",
        split_axis=0,
        concat_axis=0,
        tiled=True,
    )
    return returned.reshape(1, rows_here, row_width)


LOG2E = 1.4426950408889634


def normalised(tokens):
    average = jnp.mean(tokens, 0, keepdims=True)
    centered = tokens - average
    variance = jnp.mean(centered * centered, 0, keepdims=True)
    return (centered * lax.rsqrt(variance + epsilon)).astype(jnp.bfloat16)


def product(left, right):
    return jnp.dot(left, right, preferred_element_type=jnp.float32)


GELU_IN = 0.035677408136300125 ** (1 / 3)
GELU_LINEAR = 0.7978845608028654 / GELU_IN
GELU_OUT = 0.5 / GELU_IN


def across(left, right):
    return lax.dot_general(left, right, (((1,), (1,)), ((), ())), preferred_element_type=jnp.float32)


def gated(scaled):
    scaled = scaled.astype(jnp.bfloat16)
    return scaled + scaled * jnp.tanh(scaled * (GELU_LINEAR + scaled * scaled))


def pack_kernel(volume_ref, gains_ref, packed_ref, held_gains_ref, rows_ref, sems):
    windows, _, width = packed_ref.shape
    half = width // 2
    copies = [
        pltpu.make_async_copy(volume_ref, rows_ref, sems.at[0]),
        pltpu.make_async_copy(gains_ref, held_gains_ref, sems.at[1]),
    ]
    for copy in copies:
        copy.start()
    for copy in copies:
        copy.wait()
    for window in range(windows):
        start = window * width + half
        if window < windows - 1:
            chunk = rows_ref[:, start : start + width]
        else:
            chunk = jnp.concatenate([rows_ref[:, start:], rows_ref[:, :half]], axis=1)
        packed_ref[window] = jnp.concatenate([chunk[4:], chunk[:4]], axis=0)


def unpack_kernel(packed_ref, volume_ref, rows_ref, sems):
    windows, _, width = packed_ref.shape
    half = width // 2
    cut = windows // 2 * width + half
    runs = (pl.ds(0, cut), pl.ds(cut, windows * width - cut))
    copies = [
        pltpu.make_async_copy(rows_ref.at[:, run], volume_ref.at[:, run], sems.at[index])
        for index, run in enumerate(runs)
    ]
    for window in [windows - 1, *range(windows - 1)]:
        chunk = packed_ref[window]
        rows = jnp.concatenate([chunk[12:], chunk[:12]], axis=0)
        start = window * width + half
        if window < windows - 1:
            rows_ref[:, start : start + width] = rows
        else:
            rows_ref[:, start:] = rows[:, :half]
            rows_ref[:, :half] = rows[:, half:]
        if window == windows // 2 - 1:
            copies[0].start()
    copies[1].start()
    for copy in copies:
        copy.wait()


LAG = 4


def in_lockstep(stages, planes):
    for group in stages:
        group = group if isinstance(group, tuple) else (group,)
        for step in range(planes + LAG * (len(group) - 1)):
            for index, stage in enumerate(group):
                if 0 <= step - LAG * index < planes:
                    stage(step - LAG * index)


def blocks_kernel(
    tokens_ref,
    gains_ref,
    qkv_weight_ref,
    out_weight_ref,
    up_weight_ref,
    down_weight_ref,
    window_bias_ref,
    order_ref,
    result_ref,
    bias_ref,
    planar_ref,
    query_ref,
    key_ref,
    value_ref,
):
    channels = gains_ref.shape[1]
    planes = tokens_ref.shape[0] // 2
    heads = window_bias_ref.shape[0] // 64
    head_size = channels // heads
    lane = lax.broadcasted_iota(jnp.int32, (1, 128), 1)
    own = lane % 16 < 12
    first = lane % 16 < 8
    place = lax.broadcasted_iota(jnp.int32, (channels, 128), 1)
    by_window = place % 64 // 8 * 16 + place // 64 * 8 + place % 8
    blank = jnp.zeros((128 - channels, 128), jnp.bfloat16)
    blank_rows = jnp.zeros((128 - channels, 128), jnp.float32)

    def turned(ref, layer):
        return ref[layer].astype(jnp.float32).T

    def gain(norm, scale):
        return gains_ref[norm : norm + 1, :] * scale

    def turned_qkv(layer):
        matrix = turned(qkv_weight_ref, layer)
        queries = matrix[:channels] * gain(2 * layer, LOG2E * head_size ** (-0.5))
        return jnp.concatenate([queries, matrix[channels:] * gain(2 * layer, 1.0)], axis=0).astype(jnp.bfloat16)

    qkv = [turned_qkv(layer) for layer in range(2)]
    up = [(turned(up_weight_ref, layer) * gain(2 * layer + 1, GELU_IN)).astype(jnp.bfloat16) for layer in range(2)]
    down = [(down_weight_ref[layer].astype(jnp.float32) * GELU_OUT).astype(jnp.bfloat16) for layer in range(2)]
    out = turned(out_weight_ref, 0).astype(jnp.bfloat16)
    mix = jnp.concatenate([turned(out_weight_ref, 1).astype(jnp.bfloat16)] * 8, axis=1)

    shape = (heads * planes, planes * channels // 2)
    row = lax.broadcasted_iota(jnp.int32, shape, 0)
    column = lax.broadcasted_iota(jnp.int32, shape, 1)
    mine = lax.div(column, head_size // 2) == lax.rem(row, planes) * heads + lax.div(row, planes)
    gather = jnp.where(mine, 1.0, 0.0).astype(jnp.bfloat16)

    high = window_bias_ref[...].astype(jnp.bfloat16)
    low = (window_bias_ref[...] - high.astype(jnp.float32)).astype(jnp.bfloat16)
    parts = [across(order_ref[:64, :64], part).astype(jnp.bfloat16) for part in (high, low)]
    position = lax.axis_index("gz") * lax.axis_size("tile") + lax.axis_index("tile")
    last = position == lax.axis_size("gz") * lax.axis_size("tile") - 1
    key_row = lax.broadcasted_iota(jnp.int32, (64, 128), 0)
    query_lane = lax.broadcasted_iota(jnp.int32, (64, 128), 1)
    column_cut = ((key_row < 32) != (query_lane < 64)) & last
    row_cut = ((key_row % 8 < 4) != (query_lane % 8 < 4)) & (query_lane % 16 >= 8)
    for head in range(heads):
        placed = order_ref[64 + 128 * head : 64 + 128 * (head + 1), :]
        plain = (across(parts[0], placed) + across(parts[1], placed)) * LOG2E
        plain = jnp.where(column_cut, -jnp.inf, plain)
        bias_ref[0, 64 * head : 64 * (head + 1), :] = plain
        bias_ref[1, 64 * head : 64 * (head + 1), :] = jnp.where(row_cut, -jnp.inf, plain)

    held = [{} for _ in range(planes)]
    tops, totals = [], []

    def rows_of(plane):
        return slice(plane * channels, (plane + 1) * channels)

    def gather_columns(plane):
        held[plane]["x"] = [
            jnp.concatenate([tokens_ref[source, :, channels * c : channels * (c + 1)] for c in range(8)], axis=0)
            for source in (2 * plane, 2 * plane + 1)
        ]

    def load(plane):
        one, two = (tokens.T for tokens in held[plane]["x"])
        tokens = jnp.concatenate([jnp.where(own, one, two), jnp.where(own, two, one)], axis=1)
        held[plane]["x"] = tokens.astype(jnp.float32)

    def norm(plane):
        held[plane]["n"] = normalised(held[plane]["x"])

    def lateral_qkv(plane):
        packed = product(qkv[0], held[plane].pop("n"))
        held[plane]["q"] = packed[:channels]
        held[plane]["k"] = packed[channels : 2 * channels]
        values = packed[2 * channels :]
        held[plane]["v"] = []
        for lanes in (slice(0, 128), slice(128, 256)):
            ordered = jnp.take_along_axis(values[:, lanes], by_window, axis=1, mode="promise_in_bounds")
            held[plane]["v"].append((ordered[:, :64].astype(jnp.bfloat16), ordered[:, 64:].astype(jnp.bfloat16)))

    def lateral_scores(plane):
        queries, keys = held[plane].pop("q"), held[plane].pop("k")
        scores = []
        for pair in range(2):
            lanes = slice(128 * pair, 128 * pair + 128)
            query = queries[:, lanes]
            right = jnp.concatenate(
                [
                    jnp.where(first, query, 0.0).astype(jnp.bfloat16),
                    blank,
                    jnp.where(first, 0.0, query).astype(jnp.bfloat16),
                    blank,
                ],
                axis=0,
            )
            key = jnp.concatenate([keys[:, lanes], blank_rows], axis=0).T
            left = []
            for head in range(heads):
                masked = jnp.where(lane // head_size == head, key, 0.0).reshape(8, 2, 8, 128)
                windows = [masked[:, window].reshape(64, 128).astype(jnp.bfloat16) for window in range(2)]
                left.append(jnp.concatenate(windows, axis=1))
            scores.append((jnp.concatenate(left, axis=0), right))
        held[plane]["s"] = scores

    def lateral_weights(plane):
        scores = held[plane].pop("s")
        held[plane]["w"] = []
        for pair in range(2):
            for head in range(heads):
                own_scores = scores[pair][64 * head : 64 * head + 64]
                weights = jnp.exp2(own_scores - jnp.max(own_scores, axis=0, keepdims=True))
                total = jnp.sum(weights, axis=0, keepdims=True)
                held[plane]["w"].append((weights.astype(jnp.bfloat16), 1.0 / total))

    def lateral_products(plane):
        held[plane]["s"] = [product(*held[plane]["s"][pair]) + bias_ref[pair] for pair in range(2)]

    def lateral_values(plane):
        weights, values = held[plane].pop("w"), held[plane].pop("v")
        attended = []
        for pair in range(2):
            mixed = []
            for head in range(heads):
                own_weights, inverse = weights[heads * pair + head]
                rows = slice(head_size * head, head_size * (head + 1))
                both = product(jnp.concatenate([values[pair][0][rows], values[pair][1][rows]], axis=0), own_weights)
                own_mixed = jnp.where(first, both[:head_size], both[head_size:])
                mixed.append((own_mixed * inverse).astype(jnp.bfloat16))
            attended.append(jnp.concatenate(mixed, axis=0))
        held[plane]["a"] = jnp.concatenate(attended, axis=1)

    def lateral_out(plane):
        held[plane]["x"] = held[plane]["x"] + product(out, held[plane].pop("a"))

    def raised(layer):
        def stage(plane):
            held[plane]["h"] = product(up[layer], held[plane].pop("n"))

        return stage

    def gelu(plane):
        held[plane]["g"] = gated(held[plane].pop("h"))

    def lowered(layer):
        def stage(plane):
            held[plane]["x"] = held[plane]["x"] + product(down[layer], held[plane].pop("g"))

        return stage

    def axial_qkv(plane):
        packed = product(qkv[1], held[plane].pop("n")).astype(jnp.bfloat16)
        planar_ref[rows_of(plane), :] = held[plane].pop("x")
        query_ref[rows_of(plane), :] = packed[:channels]
        key_ref[rows_of(plane), :] = packed[channels : 2 * channels]
        value_ref[rows_of(plane), :] = packed[2 * channels :]

    def axial_scores(other):
        key = key_ref[rows_of(other), :]
        half = head_size // 2
        pairs = []
        for plane in range(planes):
            pair = query_ref[rows_of(plane), :] * key
            for head in range(heads):
                top = head_size * head
                pairs.append(pair[top : top + half] + pair[top + half : top + head_size])
        held[other]["s"] = product(gather, jnp.concatenate(pairs, axis=0))

    def axial_top(plane):
        scores = held[plane]["s"]
        tops.append(scores if plane == 0 else jnp.maximum(tops[-1], scores))

    def axial_exponentials(plane):
        held[plane]["s"] = jnp.exp2(held[plane]["s"] - tops[-1])
        totals.append(held[plane]["s"] if plane == 0 else totals[-1] + held[plane]["s"])

    def axial_weights(plane):
        if plane == 0:
            totals.append(1.0 / totals[-1])
        held[plane]["w"] = held[plane].pop("s") * totals[-1]

    def axial_values(plane):
        spread = []
        for other in range(planes):
            weights = held[other]["w"]
            wide = jnp.concatenate(
                [
                    jnp.broadcast_to(weights[planes * head + plane][None], (head_size, 256)).astype(jnp.bfloat16)
                    for head in range(heads)
                ],
                axis=0,
            )
            spread.append(wide * value_ref[rows_of(other), :])
        while len(spread) > 8:
            spread = [one + two for one, two in zip(spread[::2], spread[1::2])]
        spread = jnp.concatenate(spread, axis=0)
        held[plane]["x"] = planar_ref[rows_of(plane), :] + product(mix, spread)

    def turn(plane):
        mixed = held[plane].pop("x").astype(jnp.bfloat16)
        one, two = mixed[:, :128], mixed[:, 128:]
        held[plane]["x"] = [jnp.where(own, one, two).T, jnp.where(own, two, one).T]

    def store(plane):
        for tile, tokens in enumerate(held[plane].pop("x")):
            rows = jnp.concatenate([tokens[16 * c : 16 * (c + 1)] for c in range(8)], axis=1)
            result_ref[2 * plane + tile] = rows

    lateral = [gather_columns, load, norm, lateral_qkv, lateral_scores, (lateral_products, lateral_weights, lateral_values, lateral_out)]
    lateral += [norm, (raised(0), gelu, lowered(0)), norm, axial_qkv]
    axial = [axial_scores, axial_top, axial_exponentials, axial_weights, axial_values, norm, (raised(1), gelu, lowered(1)), turn, store]
    in_lockstep(lateral + axial, planes)


def pack(rows, gains, windows):
    return pl.pallas_call(
        pack_kernel,
        out_shape=(
            jax.ShapeDtypeStruct((windows, rows.shape[0], rows.shape[1] // windows), jnp.bfloat16),
            jax.ShapeDtypeStruct(gains.shape, gains.dtype),
        ),
        in_specs=[pl.BlockSpec(memory_space=pltpu.HBM)] * 2,
        scratch_shapes=[pltpu.VMEM(rows.shape, rows.dtype), pltpu.SemaphoreType.DMA((2,))],
        compiler_params=pltpu.CompilerParams(vmem_limit_bytes=16 * 1024 * 1024),
        name="pack_windows",
    )(*(pltpu.with_memory_space_constraint(operand, pltpu.HBM) for operand in (rows, gains)))


def unpack(packed, rows, width):
    return pl.pallas_call(
        unpack_kernel,
        out_shape=jax.ShapeDtypeStruct((rows, width), jnp.bfloat16),
        out_specs=pl.BlockSpec(memory_space=pltpu.HBM),
        scratch_shapes=[pltpu.VMEM((rows, width), jnp.bfloat16), pltpu.SemaphoreType.DMA((2,))],
        compiler_params=pltpu.CompilerParams(vmem_limit_bytes=16 * 1024 * 1024),
        name="unpack_windows",
    )(packed)


def blocks(tokens, *operands):
    rows = tokens.shape[0] // 2 * operands[0].shape[1]
    heads = operands[5].shape[0] // 64
    return pl.pallas_call(
        blocks_kernel,
        out_shape=jax.ShapeDtypeStruct(tokens.shape, jnp.bfloat16),
        scratch_shapes=[
            pltpu.VMEM((2, heads * 64, 128), jnp.float32),
            pltpu.VMEM((rows, 256), jnp.float32),
            pltpu.VMEM((rows, 256), jnp.bfloat16),
            pltpu.VMEM((rows, 256), jnp.bfloat16),
            pltpu.VMEM((rows, 256), jnp.bfloat16),
        ],
        compiler_params=pltpu.CompilerParams(vmem_limit_bytes=40 * 1024 * 1024),
        name="both_blocks",
    )(tokens, *operands)


def token_order(heads):
    index = np.arange(64)
    order = np.zeros((64, heads * 64), np.float32)
    order[index, index % 8 * 8 + index // 8] = 1.0
    lane = np.arange(128)
    placed = np.zeros((heads, 128, heads, 64), np.float32)
    for head in range(heads):
        placed[head, lane, head, lane % 8 * 8 + lane // 16] = 1.0
    return np.concatenate([order, placed.reshape(heads * 128, heads * 64)]).astype(jnp.bfloat16)


def window_body(volume, norm_gains, qkv_weight, out_weight, up_weight, down_weight, window_bias):
    rows = volume.shape[1]
    width = volume.shape[2]
    channels = norm_gains.shape[1]
    heads = window_bias.shape[0]
    planes = lax.axis_size("gz")
    windows = width // channels // 8
    packed, held_gains = pack(volume.reshape(rows, width), norm_gains, windows)
    tokens = lax.all_to_all(packed, ("gz", "tile"), split_axis=0, concat_axis=0, tiled=True)
    mixed = blocks(
        tokens,
        held_gains,
        qkv_weight,
        out_weight,
        up_weight,
        jnp.transpose(down_weight, (0, 2, 1)),
        window_bias.reshape(heads * 64, 64),
        token_order(heads),
    )
    returned = lax.all_to_all(mixed, ("gz", "tile"), split_axis=0, concat_axis=0, tiled=True)
    return unpack(returned, rows, width).reshape(1, rows, width)


def fits_windows(mesh, volume, norm_gains, window_bias):
    planes, tiles = mesh.shape["gz"], mesh.shape["tile"]
    channels, heads = norm_gains.shape[1], window_bias.shape[0]
    return (
        tiles == 2
        and planes == 8
        and volume.shape[1] == 16 * tiles
        and volume.shape[2] == 8 * channels * planes * tiles
        and channels == 96
        and heads == 3
    )


def solution(mesh):
    placed = (P(("groups", "gz"), "tile", None), P(), P(), P(), P(), P(), P())

    def run(volume, norm_gains, *weights):
        chosen = window_body if fits_windows(mesh, volume, norm_gains, weights[-1]) else general_body
        return jax.shard_map(
            chosen,
            mesh=mesh,
            in_specs=placed,
            out_specs=P(("groups", "gz"), "tile", None),
            check_vma=False,
        )(volume, norm_gains, *weights)

    return run
```
